32 devices in a mesh: ctx: 8 (over y, x, core), sp: 4 (over z).
Axes of the slice: x: 2, y: 2, z: 4, core: 2. Of those that a mesh axis runs over, the one named last changes fastest.
Arguments:
- hidden_in: bfloat16 [2, 6144, 1024], P(None, ('ctx', 'sp')), may hold values from -6 to 6
- out_grad: bfloat16 [2, 6144, 1024], P(None, ('ctx', 'sp')), may hold values from -6 to 6
- lengths: int32 [2], replicated, may hold values from 1536 to 6144, as said below
- input_gain: bfloat16 [1024], P(('ctx', 'sp')), may hold values from 0.5 to 1.5
- attn_in_weight: bfloat16 [1024, 768], P(('ctx', 'sp')), may hold values from -0.1875 to 0.1875
- attn_out_weight: bfloat16 [512, 1024], P(('ctx', 'sp')), may hold values from -1 to 1
- zgate_weight: bfloat16 [1024, 1536], P(('ctx', 'sp')), may hold values from -0.1875 to 0.1875
- mixer_in_weight: bfloat16 [1024, 1792], P(('ctx', 'sp')), may hold values from -0.1875 to 0.1875
- step_weight: bfloat16 [1024, 24], P(('ctx', 'sp')), may hold values from -0.75 to 0.75
- conv_weight: bfloat16 [4, 1792], P(None, ('ctx', 'sp')), may hold values from -2.5 to 2.5
- conv_bias: bfloat16 [1792], P(('ctx', 'sp')), may hold values from -2.5 to 2.5
- step_bias: float32 [24], P('sp'), may hold values from -4 to -2
- decay_log: float32 [24], P('sp'), may hold values from -10 to -1
- skip_scale: float32 [24], P('sp'), may hold values from 0.5 to 1.5
- mixer_gain: bfloat16 [1536], P(('ctx', 'sp')), may hold values from 0.5 to 1.5
- mixer_out_weight: bfloat16 [1536, 1024], P(('ctx', 'sp')), may hold values from -0.15625 to 0.15625
- post_gain: bfloat16 [1024], P(('ctx', 'sp')), may hold values from 0.5 to 1.5
- gate_weight: bfloat16 [1024, 2048], P(('ctx', 'sp')), may hold values from -0.1875 to 0.1875
- up_weight: bfloat16 [1024, 2048], P(('ctx', 'sp')), may hold values from -0.1875 to 0.1875
- down_weight: bfloat16 [2048, 1024], P(('ctx', 'sp')), may hold values from -0.125 to 0.125
Outputs:
- layer_out: bfloat16 [2, 6144, 1024], P(None, ('ctx', 'sp'))
- input_grad: float32 [2, 6144, 1024], P(None, ('ctx', 'sp'))
- grad_input_gain: float32 [1024], P(('ctx', 'sp'))
- grad_attn_in: float32 [1024, 768], P(('ctx', 'sp'))
- grad_attn_out: float32 [512, 1024], P(('ctx', 'sp'))
- grad_zgate: float32 [1024, 1536], P(('ctx', 'sp'))
- grad_mixer_in: float32 [1024, 1792], P(('ctx', 'sp'))
- grad_step_weight: float32 [1024, 24], P(('ctx', 'sp'))
- grad_conv_weight: float32 [4, 1792], P(None, ('ctx', 'sp'))
- grad_conv_bias: float32 [1792], P(('ctx', 'sp'))
- grad_step_bias: float32 [24], P('sp')
- grad_decay_log: float32 [24], P('sp')
- grad_skip_scale: float32 [24], P('sp')
- grad_mixer_gain: float32 [1536], P(('ctx', 'sp'))
- grad_mixer_out: float32 [1536, 1024], P(('ctx', 'sp'))
- grad_post_gain: float32 [1024], P(('ctx', 'sp'))
- grad_gate: float32 [1024, 2048], P(('ctx', 'sp'))
- grad_up: float32 [1024, 2048], P(('ctx', 'sp'))
- grad_down: float32 [2048, 1024], P(('ctx', 'sp'))
The draws below stay inside these ranges and needn't reach their ends.
Inputs may be any that keep to these rules, and one draw needn't show every extreme that they name: Slot b's valid positions are its first lengths[b]; in every draw some slot is full, with 6144.
All inputs are finite; a program needn't handle non-finite values.
Results may differ from the reference program's by a relative error of at most 0.025.
Values may be sent and summed in bfloat16 or wider, within the bound.
No kernel may reach another device: no remote copies, remote signals or barrier semaphores. Data moves between devices by JAX's collectives and lax.ppermute only.
A program may use at most 256 MiB of HBM per device.

```python
import jax
import jax.numpy as jnp
from jax import lax

D = 1024
QH = 8
KVH = 2
HD = 64
SH = 24
SHD = 64
NS = 128
KC = 4
FF = 2048
CH = 768
SLOTS = 2
SEQ = 6144
DS = 1536
CW = 1792


def draw_lengths(key, part):
    first_key = jax.random.fold_in(key, 11)
    second_key = jax.random.fold_in(key, 23)
    longest = jax.random.randint(first_key, (), 0, SLOTS)
    drawn = jax.random.randint(second_key, (SLOTS,), SEQ // 4, SEQ + 1)
    return jnp.where(jnp.arange(SLOTS) == longest, SEQ, drawn).astype(jnp.int32)


def block_levels(own_key, extent, cuts, smallest, high):
    factor_of, own = 1.0, jax.random.fold_in(own_key, 6)
    for position, blocks in cuts:
        heights = jnp.exp(jax.random.uniform(jax.random.fold_in(own, position), (blocks,), jnp.float32, smallest / len(cuts), high / len(cuts)))
        factor_of = factor_of * jnp.repeat(heights, extent[position] // blocks).reshape([-1 if axis == position else 1 for axis in range(len(extent))])
    return factor_of


def normal_values(stream_key, shape, spread, bound, cuts=(), held_as=jnp.bfloat16):
    loudness = block_levels(stream_key, shape, cuts, -0.22, 0.18) if cuts else 1.0
    result = jax.random.normal(stream_key, shape, jnp.float32) * spread * loudness
    return jnp.minimum(jnp.maximum(result, -bound), bound).astype(held_as)


def setup_inputs(seed: int = 0) -> dict:
    seeds = jax.random.split(jax.random.key(seed), 21)
    hidden_in = normal_values(seeds[0], (SLOTS, SEQ, D), 1.0, 6.0, ((1, 32),))
    out_grad = normal_values(seeds[1], (SLOTS, SEQ, D), 1.0, 6.0, ((1, 32),))
    lengths = draw_lengths(jax.random.fold_in(seeds[20], 71), 0)
    input_gain = jnp.clip(1.0 + 0.1 * jax.random.normal(seeds[3], (D,), jnp.float32), 0.5, 1.5).astype(jnp.bfloat16)
    attn_in_weight = normal_values(seeds[4], (D, (QH + 2 * KVH) * HD), D ** -0.5, 0.1875, ((0, 32),))
    attn_out_weight = normal_values(seeds[5], (QH * HD, D), (QH * HD // 16) ** -0.5, 1.0, ((0, 32),))
    zgate_weight = normal_values(seeds[6], (D, DS), D ** -0.5, 0.1875, ((0, 32),))
    mixer_in_weight = normal_values(seeds[7], (D, CW), D ** -0.5, 0.1875, ((0, 32),))
    step_weight = normal_values(seeds[8], (D, SH), (D // 16) ** -0.5, 0.75, ((0, 32),))
    conv_weight = normal_values(seeds[9], (KC, CW), 0.5, 2.5, ((1, 32),))
    conv_bias = normal_values(seeds[10], (CW,), 0.5, 2.5, ((0, 32),))
    step_bias = jnp.clip(-4.0 + 2.0 * jax.random.uniform(seeds[11], (SH,), jnp.float32) ** block_levels(seeds[11], (SH,), ((0, 4),), -0.2, 0.2), -4.0, -2.0)
    decay_log = jnp.clip(-10.0 + 9.0 * jax.random.uniform(seeds[12], (SH,), jnp.float32) ** block_levels(seeds[12], (SH,), ((0, 4),), -0.2, 0.2), -10.0, -1.0)
    skip_scale = jnp.clip(0.5 + 1.0 * jax.random.uniform(seeds[13], (SH,), jnp.float32) ** block_levels(seeds[13], (SH,), ((0, 4),), -0.2, 0.2), 0.5, 1.5)
    mixer_gain = jnp.clip(1.0 + 0.1 * jax.random.normal(seeds[14], (DS,), jnp.float32), 0.5, 1.5).astype(jnp.bfloat16)
    mixer_out_weight = normal_values(seeds[15], (DS, D), DS ** -0.5, 0.15625, ((0, 32),))
    post_gain = jnp.clip(1.0 + 0.1 * jax.random.normal(seeds[16], (D,), jnp.float32), 0.5, 1.5).astype(jnp.bfloat16)
    gate_weight = normal_values(seeds[17], (D, FF), D ** -0.5, 0.1875, ((0, 32),))
    up_weight = normal_values(seeds[18], (D, FF), D ** -0.5, 0.1875, ((0, 32),))
    down_weight = normal_values(seeds[19], (FF, D), FF ** -0.5, 0.125, ((0, 32),))
    return dict(hidden_in=hidden_in, out_grad=out_grad, lengths=lengths, input_gain=input_gain, attn_in_weight=attn_in_weight, attn_out_weight=attn_out_weight, zgate_weight=zgate_weight, mixer_in_weight=mixer_in_weight, step_weight=step_weight, conv_weight=conv_weight, conv_bias=conv_bias, step_bias=step_bias, decay_log=decay_log, skip_scale=skip_scale, mixer_gain=mixer_gain, mixer_out_weight=mixer_out_weight, post_gain=post_gain, gate_weight=gate_weight, up_weight=up_weight, down_weight=down_weight)


@jax.custom_vjp
def low(v):
    return lax.optimization_barrier(v.astype(jnp.bfloat16)).astype(jnp.float32)

@jax.custom_vjp
def low_back(v):
    return v

def low_keep(v):
    return (low(v), None)

def low_pass(kept, grad):
    return (grad,)

def back_keep(v):
    return (v, None)

def back_low(kept, grad):
    return (low(grad),)
low.defvjp(low_keep, low_pass)
low_back.defvjp(back_keep, back_low)
MASKED = -1e+30

def product(form, left, right):
    return jnp.einsum(form, left, right, precision=lax.Precision.HIGHEST, preferred_element_type=jnp.float32)

def matmul(left, right):
    return jnp.dot(left, right, precision=lax.Precision.HIGHEST, preferred_element_type=jnp.float32)

def rms_scale(value, gain):
    return value * lax.rsqrt(lax.optimization_barrier(jnp.mean(value * value, axis=-1, keepdims=True)) + 1e-05) * gain

def gate_norm(ssd_values, gate_values, gain):
    return rms_scale(ssd_values * jax.nn.silu(gate_values), gain)

def rotary_tables(positions, width):
    half_width = width // 2
    inverse = 100000000000.0 ** (-jnp.arange(half_width, dtype=jnp.float32) * 2.0 / width)
    angles = positions.astype(jnp.float32)[:, None] * inverse[None, :]
    return (jnp.cos(angles), jnp.sin(angles))

def rotate(value, cos_table, sin_table):
    half_width = value.shape[-1] // 2
    first_half = value[..., :half_width]
    second_half = value[..., half_width:]
    cos_part = cos_table[:, None, :]
    sin_part = sin_table[:, None, :]
    return jnp.concatenate([first_half * cos_part - second_half * sin_part, second_half * cos_part + first_half * sin_part], axis=-1)

def conv_apply(padded, weight, bias):
    tap_count = weight.shape[0]
    out_rows = padded.shape[-2] - tap_count + 1
    running = bias
    for tap_index in range(tap_count):
        running = running + weight[tap_index] * lax.slice_in_dim(padded, tap_index, tap_index + out_rows, axis=padded.ndim - 2)
    return jax.nn.silu(running)

def block_local(features, inject, readout, step_sizes, decay_rates):
    log_decay = jnp.cumsum(step_sizes * decay_rates[None, :], axis=0)
    length = features.shape[0]
    causal = jnp.arange(length)[:, None] >= jnp.arange(length)[None, :]
    gap_logs = jnp.where(causal[:, :, None], log_decay[:, None, :] - log_decay[None, :, :], MASKED)
    kernel = product('tn,jn->tj', readout, inject)[:, :, None] * jnp.exp(gap_logs) * step_sizes[None, :, :]
    within = product('tjh,jhp->thp', kernel, features)
    tail_decay = jnp.exp(log_decay[-1][None, :] - log_decay) * step_sizes
    local_state = product('jhp,jn->hpn', features * tail_decay[:, :, None], inject)
    return (within, jnp.exp(log_decay[-1]), local_state, log_decay)

def block_carry(readout, log_decay, state):
    return jnp.exp(log_decay)[:, :, None] * product('tn,hpn->thp', readout, state)

def mixer_sequence(features, inject, readout, step_sizes, decay_rates):
    blocks = SEQ // CH

    def advance(state, pieces):
        within, decay, local_state, log_decay = block_local(pieces[0], pieces[1], pieces[2], pieces[3], decay_rates)
        output = within + block_carry(pieces[2], log_decay, state)
        return (decay[:, None, None] * state + local_state, output)
    initial = jnp.zeros((SH, SHD, NS), jnp.float32)
    pieces = (features.reshape(blocks, CH, SH, SHD), inject.reshape(blocks, CH, NS), readout.reshape(blocks, CH, NS), step_sizes.reshape(blocks, CH, SH))
    _, outputs = lax.scan(jax.checkpoint(advance), initial, pieces)
    return outputs.reshape(SEQ, SH, SHD)

def attention(queries, key_heads, value_heads):
    group = QH // KVH
    key_heads = jnp.repeat(key_heads, group, axis=1)
    value_heads = jnp.repeat(value_heads, group, axis=1)
    blocks = SEQ // CH
    key_pos = jnp.arange(SEQ)

    def attend(pieces):
        block_queries, first_row = pieces
        scores = low_back(product('qhd,khd->hqk', block_queries, key_heads) * HD ** (-0.5))
        query_pos = first_row + jnp.arange(CH)
        causal_keep = key_pos[None, :] <= query_pos[:, None]
        masked = jnp.where(causal_keep[None], scores, MASKED)
        row_max = lax.optimization_barrier(jnp.max(masked, axis=-1, keepdims=True))
        log_total = row_max + jnp.log(lax.optimization_barrier(jnp.sum(jnp.exp(masked - row_max), axis=-1, keepdims=True)))
        attn_probs = jnp.exp(masked - log_total)
        return product('hqk,khd->qhd', low(attn_probs), value_heads)
    outputs = lax.map(jax.checkpoint(attend), (queries.reshape(blocks, CH, QH, HD), jnp.arange(blocks) * CH))
    return outputs.reshape(SEQ, QH, HD)

def reference(hidden_in, out_grad, lengths, input_gain, attn_in_weight, attn_out_weight, zgate_weight, mixer_in_weight, step_weight, conv_weight, conv_bias, step_bias, decay_log, skip_scale, mixer_gain, mixer_out_weight, post_gain, gate_weight, up_weight, down_weight):
    params = tuple((item.astype(jnp.float32) for item in (hidden_in, input_gain, attn_in_weight, attn_out_weight, zgate_weight, mixer_in_weight, step_weight, conv_weight, conv_bias, step_bias, decay_log, skip_scale, mixer_gain, mixer_out_weight, post_gain, gate_weight, up_weight, down_weight)))
    valid_rows = (jnp.arange(SEQ)[None, :] < lengths[:, None]).astype(jnp.float32)
    cos_table, sin_table = rotary_tables(jnp.arange(SEQ), HD)

    def forward(tokens, gain_in, attn_in, attn_out, zgate_mat, mixer_in, step_mat, conv_taps, conv_shift, step_shift, log_rates, skip_terms, gain_mixer, mixer_out, gain_post, gate_mat, up_mat, down_mat):
        results = []
        for slot_index in range(SLOTS):
            row_tokens = tokens[slot_index]
            normed = low(rms_scale(row_tokens, gain_in))
            linear = low_back(matmul(normed, attn_in))
            queries = linear[:, :QH * HD].reshape(SEQ, QH, HD)
            key_heads = linear[:, QH * HD:(QH + KVH) * HD].reshape(SEQ, KVH, HD)
            value_heads = low(linear[:, (QH + KVH) * HD:].reshape(SEQ, KVH, HD))
            queries = low(rotate(queries, cos_table, sin_table))
            key_heads = low(rotate(key_heads, cos_table, sin_table))
            attended = low_back(low(attention(queries, key_heads, value_heads))).reshape(SEQ, QH * HD)
            attn_part = matmul(attended, attn_out)
            mixer_gate = low_back(low(matmul(normed, zgate_mat)))
            mixed_raw = low_back(low(matmul(normed, mixer_in)))
            step_raw = low_back(low(matmul(normed, step_mat)))
            padded = jnp.concatenate([jnp.zeros((KC - 1, CW), jnp.float32), mixed_raw], axis=0)
            conv = low(conv_apply(padded, conv_taps, conv_shift))
            features = conv[:, :DS].reshape(SEQ, SH, SHD)
            inject = conv[:, DS:DS + NS]
            readout = conv[:, DS + NS:]
            step_sizes = jax.nn.softplus(step_raw + step_shift[None, :])
            decay_rates = -jnp.exp(log_rates)
            ssd = mixer_sequence(features, inject, readout, step_sizes, decay_rates) + skip_terms[None, :, None] * features
            ssd = low_back(low(ssd)).reshape(SEQ, DS)
            gated = low(gate_norm(ssd, mixer_gate, gain_mixer))
            mixer_part = matmul(gated, mixer_out)
            residual = row_tokens + low_back(attn_part + mixer_part)
            post_norm = low(rms_scale(residual, gain_post))
            gate_lin = low_back(matmul(post_norm, gate_mat))
            up_lin = low_back(matmul(post_norm, up_mat))
            hidden = low(jax.nn.silu(gate_lin) * up_lin)
            results.append(valid_rows[slot_index][:, None] * (residual + matmul(hidden, down_mat)))
        return jnp.stack(results)
    layer_value, pullback = jax.vjp(forward, *params)
    gradients = pullback(out_grad.astype(jnp.float32))
    return (layer_value.astype(jnp.bfloat16), gradients[0], gradients[1], gradients[2], gradients[3], gradients[4], gradients[5], gradients[6], gradients[7], gradients[8], gradients[9], gradients[10], gradients[11], gradients[12], gradients[13], gradients[14], gradients[15], gradients[16], gradients[17])
```

```python
import functools
import math

import jax
import jax.numpy as jnp
from jax import lax
from jax.experimental import pallas as pl
from jax.experimental.pallas import tpu as pltpu
from jax.sharding import PartitionSpec as P

QH = 8
KVH = 2
HD = 64
SH = 24
SHD = 64
NS = 128
KC = 4
CORES = 2
MASKED = -1e30
AXES = ("ctx", "sp")
F32 = jnp.float32
BF16 = jnp.bfloat16
LANES = 128
HALO = 8
Q_SHARE = QH // CORES
M_SHARE = SH // CORES
VMEM = 56 * 2**20

NT = (((1,), (1,)), ((), ()))
TN = (((0,), (0,)), ((), ()))
NN = (((1,), (0,)), ((), ()))


def mm(left, right, dims=NN, precision=None):
    return lax.dot_general(
        left, right, dims, precision=precision, preferred_element_type=F32
    )


class Place:
    def __init__(self):
        ctx = lax.axis_size("ctx")
        groups = lax.axis_size("sp")
        chips = ctx // CORES
        nb = math.isqrt(chips)
        self.size = {"a": chips // nb, "b": nb, "z": groups, "c": CORES}
        self.devices = ctx * groups
        index = lax.axis_index("ctx")
        self.at = {
            "a": index // CORES // nb,
            "b": (index // CORES) % nb,
            "z": lax.axis_index("sp"),
            "c": index % CORES,
        }
        self.chip = index // CORES
        self.chips = chips
        self.flat = index * groups + self.at["z"]

    def flat_of(self, a, b, z, c):
        return ((a * self.size["b"] + b) * CORES + c) * self.size["z"] + z

    def pairs(self, dim, by):
        found = []
        for a in range(self.size["a"]):
            for b in range(self.size["b"]):
                for z in range(self.size["z"]):
                    for c in range(CORES):
                        spot = {"a": a, "b": b, "z": z, "c": c}
                        goal = dict(spot)
                        goal[dim] = (spot[dim] + by) % self.size[dim]
                        found.append((self.flat_of(**spot), self.flat_of(**goal)))
        return found

    def shift(self, x, dim, by):
        return lax.ppermute(x, AXES, self.pairs(dim, by))

    def swap(self, x):
        return self.shift(x, "c", 1)

    def by_core(self, zero, one):
        return jnp.where(self.at["c"] == 0, zero, one)

    def place(self, parts, dim, axis):
        n, v = self.size[dim], self.at[dim]
        if n == 2:
            return jnp.stack(
                [jnp.where(v == 0, parts[0], parts[1]), jnp.where(v == 0, parts[1], parts[0])],
                axis,
            )
        shape = parts[0].shape
        out = jnp.zeros(shape[:axis] + (n,) + shape[axis:], parts[0].dtype)
        for k, part in enumerate(parts):
            out = lax.dynamic_update_index_in_dim(out, part, (v - k) % n, axis)
        return out

    def gather(self, x, dim, axis):
        n = self.size[dim]
        return self.place([x] + [self.shift(x, dim, k) for k in range(1, n)], dim, axis)

    def exchange(self, x, dim, axis):
        n, v = self.size[dim], self.at[dim]
        parts = [lax.dynamic_index_in_dim(x, v, axis, False)]
        for k in range(1, n):
            parts.append(
                self.shift(lax.dynamic_index_in_dim(x, (v + k) % n, axis, False), dim, k)
            )
        return self.place(parts, dim, axis)

    def reduce(self, x, dim, axis):
        n, v = self.size[dim], self.at[dim]
        total = lax.dynamic_index_in_dim(x, v, axis, False).astype(F32)
        for k in range(1, n):
            piece = lax.dynamic_index_in_dim(x, (v + k) % n, axis, False).astype(BF16)
            total = total + self.shift(piece, dim, k).astype(F32)
        return total

    def gather_chips(self, x, z_axis, b_first):
        x = self.gather(x, "z", z_axis)
        if b_first:
            return self.gather(self.gather(x, "b", 0), "a", 0)
        return self.gather(self.gather(x, "a", 0), "b", 1)

    def reduce_chips(self, x, z_axis, b_first):
        if b_first:
            x = self.reduce(self.reduce(x, "a", 0), "b", 0)
        else:
            x = self.reduce(self.reduce(x, "b", 1), "a", 0)
        return self.reduce(x, "z", z_axis)


def rotary_tables(positions, width):
    half_width = width // 2
    inverse = 100000000000.0 ** (-jnp.arange(half_width, dtype=F32) * 2.0 / width)
    angles = positions.astype(F32)[..., None] * inverse
    return (jnp.cos(angles), jnp.sin(angles))


def rotate(value, cos_part, sin_part):
    half_width = value.shape[-1] // 2
    first = value[..., :half_width]
    second = value[..., half_width:]
    return jnp.concatenate(
        [first * cos_part - second * sin_part, second * cos_part + first * sin_part], axis=-1
    )


def inverse_rms(value):
    return lax.rsqrt(jnp.mean(value * value, axis=-1, keepdims=True) + 1e-05)


def rms_back(value, scale, gain, grad):
    scaled = grad * gain
    inner = jnp.mean(scaled * value, axis=-1, keepdims=True)
    return scale * scaled - value * (scale * scale * scale * inner)


def silu_and_slope(value):
    gate = jax.nn.sigmoid(value)
    out = value * gate
    return out, gate + out * (1.0 - gate)


def causal_keep(first_key, first_query, keys, piece, columns):
    key = first_key + lax.broadcasted_iota(jnp.int32, (keys, columns), 0)
    column = lax.broadcasted_iota(jnp.int32, (keys, columns), 1)
    head = sum((column >= piece * k).astype(jnp.int32) for k in range(1, columns // piece))
    return key <= first_query + column - head * piece


def attend_kernel(places, lengths, q_ref, kv_ref, out_ref, lse_ref, acc, top, total, *, piece):
    slot, which = pl.program_id(0), pl.program_id(1)
    first_query = places[which]
    columns = q_ref.shape[2]
    block = columns
    out_ref[...] = jnp.zeros_like(out_ref)
    lse_ref[...] = jnp.zeros_like(lse_ref)

    @pl.when(first_query < lengths[slot])
    def _():
        acc[...] = jnp.zeros_like(acc)
        top[...] = jnp.full_like(top, MASKED)
        total[...] = jnp.zeros_like(total)
        whole = first_query // block

        def visit(index, masked):
            start = pl.multiple_of(index * block, block)
            kv = kv_ref[0, pl.ds(start, block), :]
            scores = mm(kv, q_ref[0, 0], NT)
            if masked:
                keep = causal_keep(start, first_query, block, piece, columns)
                scores = jnp.where(keep, scores, MASKED)
            before = top[...]
            now = jnp.maximum(before, jnp.max(scores, axis=0, keepdims=True))
            weights = jnp.exp(scores - now)
            ratio = jnp.exp(before - now)
            total[...] = total[...] * ratio + jnp.sum(weights, axis=0, keepdims=True)
            acc[...] = acc[...] * ratio + mm(kv, weights.astype(BF16), TN)
            top[...] = now

        @pl.loop(0, whole)
        def _(index):
            visit(index, False)

        visit(whole, True)
        out_ref[0, 0] = (acc[...] / total[...]).T.astype(BF16)
        lse_ref[0, 0] = top[...] + jnp.log(total[...])


def attend(places, lengths, queries, kv, piece):
    slots, _, columns, width = queries.shape
    length = kv.shape[1]
    return pl.pallas_call(
        functools.partial(attend_kernel, piece=piece),
        grid_spec=pltpu.PrefetchScalarGridSpec(
            num_scalar_prefetch=2,
            grid=(slots, CORES),
            in_specs=[
                pl.BlockSpec((1, 1, columns, width), lambda s, e, *_: (s, e, 0, 0)),
                pl.BlockSpec((1, length, width), lambda s, e, *_: (s, 0, 0)),
            ],
            out_specs=[
                pl.BlockSpec((1, 1, columns, width), lambda s, e, *_: (s, e, 0, 0)),
                pl.BlockSpec((1, 1, 1, columns), lambda s, e, *_: (s, e, 0, 0)),
            ],
            scratch_shapes=[
                pltpu.VMEM((width, columns), F32),
                pltpu.VMEM((1, columns), F32),
                pltpu.VMEM((1, columns), F32),
            ],
        ),
        out_shape=[
            jax.ShapeDtypeStruct(queries.shape, BF16),
            jax.ShapeDtypeStruct((slots, CORES, 1, columns), F32),
        ],
        compiler_params=pltpu.CompilerParams(vmem_limit_bytes=VMEM),
        cost_estimate=pl.CostEstimate(
            flops=2 * 2 * slots * CORES * columns * length * width // 2,
            bytes_accessed=slots * length * width * 4,
            transcendentals=slots * CORES * columns * length // 2,
        ),
        name="attend",
    )(places, lengths, queries, kv)


def attend_back_kernel(
    places, lengths, q_ref, kv_ref, out_ref, dout_ref, lse_ref, dq_ref, dkv_ref, dkv, dq, *, piece
):
    slot, which = pl.program_id(0), pl.program_id(1)
    first_query = places[which]
    columns = q_ref.shape[2]
    block = columns
    dq_ref[...] = jnp.zeros_like(dq_ref)

    @pl.when(which == 0)
    def _():
        dkv[...] = jnp.zeros_like(dkv)

    @pl.when(first_query < lengths[slot])
    def _():
        dq[...] = jnp.zeros_like(dq)
        queries = q_ref[0, 0]
        dout = dout_ref[0, 0]
        both = dout.astype(F32) * out_ref[0, 0].astype(F32)
        delta = mm(jnp.ones((8, both.shape[1]), F32), both, NT, lax.Precision.HIGHEST)[:1]
        lse = lse_ref[0, 0]
        whole = first_query // block

        def visit(index, masked):
            start = pl.multiple_of(index * block, block)
            kv = kv_ref[0, pl.ds(start, block), :]
            scores = mm(kv, queries, NT)
            if masked:
                keep = causal_keep(start, first_query, block, piece, columns)
                scores = jnp.where(keep, scores, MASKED)
            probs = jnp.exp(scores - lse)
            dprobs = mm(kv, dout, NT)
            dscores = (probs * (dprobs - delta)).astype(BF16)
            probs = probs.astype(BF16)
            dkv[pl.ds(start, block), :] += mm(dscores, queries) + mm(probs, dout)
            dq[...] += mm(kv, dscores, TN)

        @pl.loop(0, whole)
        def _(index):
            visit(index, False)

        visit(whole, True)
        dq_ref[0, 0] = dq[...].T.astype(dq_ref.dtype)

    @pl.when(which == CORES - 1)
    def _():
        dkv_ref[0] = dkv[...].astype(dkv_ref.dtype)


def attend_back(places, lengths, queries, kv, out, dout, lse, piece):
    slots, _, columns, width = queries.shape
    length = kv.shape[1]
    rows = pl.BlockSpec((1, 1, columns, width), lambda s, e, *_: (s, e, 0, 0))
    keys = pl.BlockSpec((1, length, width), lambda s, e, *_: (s, 0, 0))
    return pl.pallas_call(
        functools.partial(attend_back_kernel, piece=piece),
        grid_spec=pltpu.PrefetchScalarGridSpec(
            num_scalar_prefetch=2,
            grid=(slots, CORES),
            in_specs=[
                rows,
                keys,
                rows,
                rows,
                pl.BlockSpec((1, 1, 1, columns), lambda s, e, *_: (s, e, 0, 0)),
            ],
            out_specs=[rows, keys],
            scratch_shapes=[pltpu.VMEM((length, width), F32), pltpu.VMEM((width, columns), F32)],
        ),
        out_shape=[
            jax.ShapeDtypeStruct(queries.shape, F32),
            jax.ShapeDtypeStruct(kv.shape, BF16),
        ],
        compiler_params=pltpu.CompilerParams(vmem_limit_bytes=VMEM),
        cost_estimate=pl.CostEstimate(
            flops=5 * 2 * slots * CORES * columns * length * width // 2,
            bytes_accessed=slots * length * width * 6,
            transcendentals=slots * CORES * columns * length // 2,
        ),
        name="attend_back",
    )(places, lengths, queries, kv, out, dout, lse)


def lower(rows, transposed=False):
    row = lax.broadcasted_iota(jnp.int32, (rows, rows), 0)
    column = lax.broadcasted_iota(jnp.int32, (rows, rows), 1)
    return row <= column if transposed else row >= column


def paired(first, second, shape):
    lane = lax.broadcasted_iota(jnp.int32, shape, 1)
    return jnp.where(lane < SHD, first, second)


def chunk_terms(raw_ref, raw_t_ref, bias_ref, bias_t_ref, rate_ref, rate_t_ref):
    rows = raw_ref.shape[1]
    steps = jax.nn.softplus(raw_ref[0] + bias_ref[...])
    steps_t = jax.nn.softplus(raw_t_ref[0] + bias_t_ref[...])
    high = lax.Precision.HIGHEST
    logs = mm(lower(rows).astype(F32), steps * rate_ref[...], NN, high)
    logs_t = mm(steps_t * rate_t_ref[...], lower(rows, True).astype(F32), NN, high)
    return steps, steps_t, logs, logs_t


def chunk_kernel(
    f_ref, b_ref, c_ref, raw_ref, raw_t_ref, bias_ref, bias_t_ref, rate_ref, rate_t_ref, skip_ref,
    out_ref, state_ref, logs_ref,
):
    steps, steps_t, logs, logs_t = chunk_terms(
        raw_ref, raw_t_ref, bias_ref, bias_t_ref, rate_ref, rate_t_ref
    )
    logs_ref[0] = logs
    rows = logs.shape[0]
    inject = b_ref[0]
    mix = jnp.where(lower(rows), mm(c_ref[0], inject, NT), 0.0)
    tail = jnp.exp(logs[rows - 1 :] - logs) * steps
    for pair in range(M_SHARE // 2):
        lanes = slice(pair * LANES, (pair + 1) * LANES)
        feats = f_ref[0, :, lanes]
        outs = []
        for head in (2 * pair, 2 * pair + 1):
            gap = jnp.minimum(logs[:, head : head + 1] - logs_t[head : head + 1, :], 0.0)
            kernel = mix * jnp.exp(gap) * steps_t[head : head + 1, :]
            outs.append(mm(kernel.astype(BF16), feats))
        wide = feats.astype(F32)
        out_ref[0, :, lanes] = paired(outs[0], outs[1], wide.shape) + skip_ref[:, lanes] * wide
        weight = paired(
            tail[:, 2 * pair : 2 * pair + 1], tail[:, 2 * pair + 1 : 2 * pair + 2], wide.shape
        )
        state_ref[0, lanes, :] = mm((wide * weight).astype(BF16), inject, TN).astype(BF16)


def carry_kernel(out_ref, c_ref, state_ref, logs_ref, ssd_ref):
    decay = jnp.exp(logs_ref[0])
    for pair in range(M_SHARE // 2):
        lanes = slice(pair * LANES, (pair + 1) * LANES)
        read = mm(c_ref[0], state_ref[0, lanes, :], NT)
        weight = paired(
            decay[:, 2 * pair : 2 * pair + 1], decay[:, 2 * pair + 1 : 2 * pair + 2], read.shape
        )
        ssd_ref[0, :, lanes] = (out_ref[0, :, lanes] + read * weight).astype(BF16)


def direct_kernel(d_ref, c_ref, logs_ref, direct_ref):
    decay = jnp.exp(logs_ref[0])
    for pair in range(M_SHARE // 2):
        lanes = slice(pair * LANES, (pair + 1) * LANES)
        grad = d_ref[0, :, lanes].astype(F32)
        weight = paired(
            decay[:, 2 * pair : 2 * pair + 1], decay[:, 2 * pair + 1 : 2 * pair + 2], grad.shape
        )
        direct_ref[0, lanes, :] = mm((grad * weight).astype(BF16), c_ref[0], TN).astype(BF16)


def chunk_back_kernel(
    f_ref, b_ref, c_ref, raw_ref, raw_t_ref, bias_ref, bias_t_ref, rate_ref, rate_t_ref, skip_ref,
    d_ref, state_ref, later_ref, agree_ref, df_ref, db_ref, dc_ref, draw_ref, sums_ref,
    columns, row_sums,
):
    steps, steps_t, logs, logs_t = chunk_terms(
        raw_ref, raw_t_ref, bias_ref, bias_t_ref, rate_ref, rate_t_ref
    )
    rows = logs.shape[0]
    inject, readout = b_ref[0], c_ref[0]
    keep = lower(rows)
    mix = jnp.where(keep, mm(readout, inject, NT), 0.0)
    columns[...] = jnp.zeros_like(columns)
    row_sums[...] = jnp.zeros_like(row_sums)
    decay = jnp.exp(logs)
    end_decay = jnp.exp(logs[rows - 1 :] - logs)
    tail = end_decay * steps
    dmix = jnp.zeros((rows, rows), F32)
    db = jnp.zeros((rows, NS), F32)
    dc = jnp.zeros((rows, NS), F32)
    to_state = jnp.zeros((rows, LANES), F32)
    from_state = jnp.zeros((rows, LANES), F32)
    skips = jnp.zeros((1, LANES), F32)
    head_lane = lax.broadcasted_iota(jnp.int32, (rows, LANES), 1)
    for pair in range(M_SHARE // 2):
        lanes = slice(pair * LANES, (pair + 1) * LANES)
        feats, grad = f_ref[0, :, lanes], d_ref[0, :, lanes]
        wide, wide_grad = feats.astype(F32), grad.astype(F32)
        later = later_ref[0, lanes, :]
        state = state_ref[0, lanes, :]
        pushed = mm(inject, later, NT)
        read = mm(readout, state, NT)
        push_part = wide * pushed
        read_part = wide_grad * read
        skip_part = wide * wide_grad
        grads = []
        for half, head in enumerate((2 * pair, 2 * pair + 1)):
            column = slice(head, head + 1)
            lane = lax.broadcasted_iota(jnp.int32, wide.shape, 1)
            mine = (lane < SHD) if half == 0 else (lane >= SHD)
            step_row = steps_t[column, :]
            gap = jnp.minimum(logs[:, column] - logs_t[column, :], 0.0)
            fade = jnp.exp(gap)
            dkernel = mm(jnp.where(mine, wide_grad, 0.0).astype(BF16), feats, NT)
            faded = dkernel * fade
            stepped = faded * step_row
            dmix = dmix + stepped
            kernel = mix * fade * step_row
            columns[column, 0:rows] = jnp.sum(faded * mix, axis=0, keepdims=True)
            here = head_lane == head
            row_sums[...] += jnp.where(here, jnp.sum(stepped * mix, axis=1, keepdims=True), 0.0)
            grads.append(mm(kernel.astype(BF16), grad, TN))
            to_state = to_state + jnp.where(
                here, jnp.sum(jnp.where(mine, push_part, 0.0), axis=1, keepdims=True), 0.0
            )
            from_state = from_state + jnp.where(
                here, jnp.sum(jnp.where(mine, read_part, 0.0), axis=1, keepdims=True), 0.0
            )
            skips = skips + jnp.where(
                here[:1],
                jnp.sum(
                    jnp.sum(jnp.where(mine, skip_part, 0.0), axis=1, keepdims=True),
                    axis=0,
                    keepdims=True,
                ),
                0.0,
            )
        first, second = slice(2 * pair, 2 * pair + 1), slice(2 * pair + 1, 2 * pair + 2)
        weight = paired(tail[:, first], tail[:, second], wide.shape)
        df_ref[0, :, lanes] = (
            paired(grads[0], grads[1], wide.shape) + skip_ref[:, lanes] * wide_grad + weight * pushed
        )
        db = db + mm((wide * weight).astype(BF16), later)
        seen = paired(decay[:, first], decay[:, second], wide.shape)
        dc = dc + mm((wide_grad * seen).astype(BF16), state)
    low = dmix * jnp.where(keep, 1.0, 0.0)
    low = low.astype(BF16)
    db_ref[0] = db + mm(low, readout, TN)
    dc_ref[0] = dc + mm(low, inject)
    direct = columns[...].T[:rows]
    push = end_decay * to_state
    dlogs = row_sums[...] - steps * direct + decay * from_state - steps * push
    end = jnp.sum(steps * push, axis=0, keepdims=True) + decay[rows - 1 :] * agree_ref[0]
    last = lax.broadcasted_iota(jnp.int32, (rows, LANES), 0) == rows - 1
    dlogs = dlogs + jnp.where(last, end, 0.0)
    summed = mm(lower(rows, True).astype(F32), dlogs, NN, lax.Precision.HIGHEST)
    dsteps = direct + push + summed * rate_ref[...]
    draw = dsteps * jax.nn.sigmoid(raw_ref[0] + bias_ref[...])
    draw_ref[0] = draw
    line = lax.broadcasted_iota(jnp.int32, (8, LANES), 0)
    dbias = jnp.sum(draw, axis=0, keepdims=True)
    dlog = jnp.sum(summed * steps, axis=0, keepdims=True) * rate_ref[...]
    sums_ref[0] = jnp.where(
        line == 0, dbias, jnp.where(line == 1, dlog, jnp.where(line == 2, skips, 0.0))
    )


def over_pieces(kernel, name, args, whole, outs, flops, scratch=()):
    pieces = args[0].shape[0]

    def spec(shape, split):
        if split:
            return pl.BlockSpec((1,) + shape[1:], lambda i: (i,) + (0,) * (len(shape) - 1))
        return pl.BlockSpec(shape, lambda i: (0,) * len(shape))

    shapes = [(arg.shape, index not in whole) for index, arg in enumerate(args)]
    nbytes = sum(arg.size * arg.dtype.itemsize for arg in args)
    nbytes += sum(math.prod(shape) * dtype.dtype.itemsize for shape, dtype in outs)
    return pl.pallas_call(
        kernel,
        grid=(pieces,),
        in_specs=[spec(shape, split) for shape, split in shapes],
        out_specs=[spec(shape, True) for shape, _ in outs],
        out_shape=[jax.ShapeDtypeStruct(shape, dtype) for shape, dtype in outs],
        scratch_shapes=list(scratch),
        compiler_params=pltpu.CompilerParams(vmem_limit_bytes=VMEM),
        cost_estimate=pl.CostEstimate(flops=flops, bytes_accessed=nbytes, transcendentals=0),
        name=name,
    )(*args)


def carried(place, states, decays, reverse):
    groups = place.size["z"]
    z, chips = place.at["z"], place.chips
    e, slots = states.shape[:2]
    share = M_SHARE // groups
    parts = states.reshape(e, slots, groups, share * SHD, NS)
    parts = place.exchange(parts, "z", 2)
    by_h = place.by_core(parts, parts[::-1]).astype(F32).reshape(e, slots, groups, share, SHD, NS)
    mine = lax.dynamic_slice_in_dim(decays, z * share, share, 4)
    here = lax.dynamic_index_in_dim(mine, place.chip, 0, False)
    order = [(h, k) for h in range(CORES) for k in range(groups)]
    if reverse:
        order = order[::-1]
    run = jnp.zeros((slots, share, SHD, NS), F32)
    fade = jnp.ones((slots, share), F32)
    entered, faded = {}, {}
    for h, k in order:
        entered[h, k], faded[h, k] = run, fade
        factor = here[k, h]
        run = factor[..., None, None] * run + by_h[h, :, k]
        fade = factor * fade
    totals = place.gather(place.gather(run.astype(BF16), "b", 0), "a", 0)
    totals = totals.reshape(chips, slots, share, SHD, NS)
    fades = jnp.prod(mine, axis=(1, 2))
    carry = jnp.zeros_like(run)
    for chip in range(chips)[::-1] if reverse else range(chips):
        reached = chip > place.chip if reverse else chip < place.chip
        new = fades[chip][..., None, None] * carry + totals[chip].astype(F32)
        carry = jnp.where(reached, new, carry)
    whole = [
        jnp.stack(
            [entered[h, k] + faded[h, k][..., None, None] * carry for k in range(groups)], 1
        ).astype(BF16)
        for h in range(CORES)
    ]
    back = jnp.stack([place.by_core(whole[0], whole[1]), place.by_core(whole[1], whole[0])])
    back = place.exchange(back.reshape(e, slots, groups, share * SHD, NS), "z", 2)
    return back.reshape(e, slots, M_SHARE * SHD, NS)


def shards(
    hidden_in,
    out_grad,
    lengths,
    input_gain,
    attn_in_weight,
    attn_out_weight,
    zgate_weight,
    mixer_in_weight,
    step_weight,
    conv_weight,
    conv_bias,
    step_bias,
    decay_log,
    skip_scale,
    mixer_gain,
    mixer_out_weight,
    post_gain,
    gate_weight,
    up_weight,
    down_weight,
):
    place = Place()
    core = place.at["c"]
    groups, chips, devices = place.size["z"], place.chips, place.devices
    na, nb = place.size["a"], place.size["b"]
    slots, piece, width = hidden_in.shape
    span = piece * groups
    rows_all = CORES * slots * piece
    rows_halo = CORES * slots * (piece + HALO)
    q_cols, m_cols = Q_SHARE * HD, M_SHARE * SHD
    az_cols = q_cols + 2 * HD + m_cols
    c_cols = m_cols + NS
    shard_rows = attn_in_weight.shape[0]
    out_rows, mix_rows, ff_rows = (
        attn_out_weight.shape[0],
        mixer_out_weight.shape[0],
        down_weight.shape[0],
    )
    ff_half = ff_rows * groups * chips

    rim = lax.ppermute(
        hidden_in[:, piece - KC + 1 :], AXES, [(i, i + 1) for i in range(devices - 1)]
    )
    block = jnp.concatenate(
        [jnp.zeros((slots, HALO - KC + 1, width), BF16), rim, hidden_in], axis=1
    )
    other_index = place.flat + jnp.where(core == 0, groups, -groups)
    pieces_at = jnp.stack([place.flat, other_index]) * piece
    positions = pieces_at[:, None] + jnp.arange(piece, dtype=jnp.int32)
    valid = (positions[:, None, :] < lengths[None, :, None]).astype(F32)
    tokens = jnp.stack([block, place.swap(block)]).astype(F32)
    dy_own = out_grad.astype(F32) * valid[0][..., None]
    dy_low = dy_own.astype(BF16)
    dy = jnp.stack([dy_low, place.swap(dy_low)]).reshape(rows_all, width)

    small = jnp.concatenate([input_gain, mixer_gain, post_gain, conv_bias, conv_weight.reshape(-1)])
    small_cols = -(-small.shape[0] // shard_rows)
    small = jnp.pad(small, (0, small_cols * shard_rows - small.shape[0]))
    small = small.reshape(shard_rows, small_cols)
    step_at = c_cols
    small_at = step_at + M_SHARE
    ms_cols = -(-(small_at + small_cols) // LANES) * LANES

    def ff_columns(weight, half):
        return weight.reshape(shard_rows, chips, CORES, -1)[:, :, half].reshape(shard_rows, -1)

    def half_columns(half):
        return jnp.concatenate(
            [
                attn_in_weight[:, half * q_cols : (half + 1) * q_cols],
                attn_in_weight[:, QH * HD + half * HD : QH * HD + (half + 1) * HD],
                attn_in_weight[:, (QH + KVH + half) * HD : (QH + KVH + half + 1) * HD],
                zgate_weight[:, half * m_cols : (half + 1) * m_cols],
                mixer_in_weight[:, half * m_cols : (half + 1) * m_cols],
                mixer_in_weight[:, SH * SHD + half * NS : SH * SHD + (half + 1) * NS],
                step_weight[:, half * M_SHARE : (half + 1) * M_SHARE],
                small,
                jnp.zeros((shard_rows, ms_cols - small_at - small_cols), BF16),
                ff_columns(gate_weight, half),
                ff_columns(up_weight, half),
            ],
            axis=1,
        )

    halves = (half_columns(0), half_columns(1))
    kept = place.by_core(*halves)
    got = place.swap(place.by_core(halves[1], halves[0]))
    both = jnp.stack([place.by_core(kept, got), place.by_core(got, kept)])
    cut = (0, az_cols, az_cols + ms_cols, az_cols + ms_cols + ff_half, both.shape[2])
    w_az, w_ms, w_gate, w_up = (
        place.gather_chips(both[:, :, cut[i] : cut[i + 1]], 1, i % 2 == 0).reshape(width, -1)
        for i in range(4)
    )
    w_out = place.gather_chips(
        jnp.concatenate([attn_out_weight, mixer_out_weight], axis=0), 0, True
    )
    w_out = w_out.reshape(2, chips // 2, groups, out_rows + mix_rows, width)
    kept = lax.dynamic_index_in_dim(w_out, core, 0, False)
    got = place.swap(lax.dynamic_index_in_dim(w_out, 1 - core, 0, False))
    w_out = jnp.stack([place.by_core(kept, got), place.by_core(got, kept)], 1)
    w_attn_out = w_out[..., :out_rows, :].reshape(q_cols, width)
    w_mixer_out = w_out[..., out_rows:, :].reshape(m_cols, width)
    w_down = place.gather_chips(down_weight, 0, False).reshape(ff_half, width)

    vectors = w_ms[:, small_at : small_at + small_cols].reshape(devices, -1).astype(F32)
    sizes = [input_gain.shape[0], mixer_gain.shape[0], post_gain.shape[0], conv_bias.shape[0]]
    ends = [sum(sizes[: k + 1]) for k in range(4)]
    gain_in = vectors[:, : ends[0]].reshape(-1)
    gain_mixer = vectors[:, ends[0] : ends[1]].reshape(-1)
    gain_mixer = place.by_core(gain_mixer[:m_cols], gain_mixer[m_cols:])
    gain_post = vectors[:, ends[1] : ends[2]].reshape(-1)
    shift_all = vectors[:, ends[2] : ends[3]].reshape(-1)
    taps_all = vectors[:, ends[3] : ends[3] + KC * sizes[3]].reshape(devices, KC, sizes[3])
    taps_all = jnp.transpose(taps_all, (1, 0, 2)).reshape(KC, -1)

    def conv_half(value):
        first = jnp.concatenate(
            [value[..., :m_cols], value[..., 2 * m_cols : 2 * m_cols + NS]], axis=-1
        )
        second = jnp.concatenate(
            [value[..., m_cols : 2 * m_cols], value[..., 2 * m_cols + NS :]], axis=-1
        )
        return place.by_core(first, second)

    taps, shift = conv_half(taps_all), conv_half(shift_all)
    head_terms = lax.all_gather(jnp.stack([step_bias, decay_log, skip_scale]), "sp", axis=1, tiled=True)
    head_terms = lax.dynamic_slice_in_dim(head_terms, core * M_SHARE, M_SHARE, 1)
    bias, log_rates, skip = head_terms[0], head_terms[1], head_terms[2]
    rates = -jnp.exp(log_rates)

    scale_in = inverse_rms(tokens)
    normed = (tokens * scale_in * gain_in).astype(BF16).reshape(rows_halo, width)

    def body_rows(value):
        return value.reshape(CORES, slots, piece + HALO, -1)[:, :, HALO:]

    linear = body_rows(mm(normed, w_az[:, : q_cols + 2 * HD]))
    zgate = body_rows(mm(normed, w_az[:, q_cols + 2 * HD :]).astype(BF16))
    mixed_step = mm(normed, w_ms).astype(BF16).reshape(CORES, slots, piece + HALO, ms_cols)
    mixed = mixed_step[..., :c_cols]
    step_raw = mixed_step[:, :, HALO:, step_at:small_at].astype(F32)

    cos_part, sin_part = rotary_tables(positions, HD)
    cos_part, sin_part = cos_part[:, None, :, None], sin_part[:, None, :, None]
    queries = rotate(
        linear[..., :q_cols].reshape(CORES, slots, piece, Q_SHARE, HD), cos_part, sin_part
    ).astype(BF16)
    keys = rotate(
        linear[..., q_cols : q_cols + HD][..., None, :], cos_part, sin_part
    ).astype(BF16)[..., 0, :]
    kv_own = jnp.concatenate([keys, linear[..., q_cols + HD :].astype(BF16)], axis=-1)
    kv_own = place.by_core(kv_own, kv_own[::-1])
    kv = jnp.stack(
        [
            place.gather_chips(kv_own[:, s], 1, s % 2 == 0).reshape(-1, 2 * HD)
            for s in range(slots)
        ]
    )

    def by_heads(value, before, after):
        value = jnp.transpose(value, (1, 0, 3, 2, 4)).reshape(slots, CORES, Q_SHARE * piece, HD)
        return jnp.pad(value, ((0, 0), (0, 0), (0, 0), (before, after)))

    def from_heads(value):
        value = value.reshape(slots, CORES, Q_SHARE, piece, HD)
        return jnp.transpose(value, (1, 0, 3, 2, 4))

    scale = HD ** (-0.5)
    queries = by_heads(queries * jnp.asarray(scale, BF16), 0, HD)
    heads_out, lse = attend(pieces_at, lengths, queries, kv, piece)
    attended = from_heads(heads_out[..., HD:]).reshape(rows_all, q_cols)

    pre = shift
    for tap in range(KC):
        first = HALO - KC + 1 + tap
        pre = pre + taps[tap] * mixed[:, :, first : first + piece].astype(F32)
    conv_out, conv_slope = silu_and_slope(pre)
    conv_out = conv_out.astype(BF16)
    features = conv_out[..., :m_cols].reshape(CORES * slots, piece, m_cols)
    shared = conv_out[..., m_cols:]
    shared_other = place.swap(shared)[::-1]
    inject = place.by_core(shared, shared_other).reshape(CORES * slots, piece, NS)
    readout = place.by_core(shared_other, shared).reshape(CORES * slots, piece, NS)
    raw = jnp.pad(step_raw.reshape(CORES * slots, piece, M_SHARE), ((0, 0), (0, 0), (0, LANES - M_SHARE)))
    raw_t = jnp.transpose(raw[..., :16], (0, 2, 1))
    bias_row = jnp.pad(bias, (0, LANES - M_SHARE))[None]
    rate_row = jnp.pad(rates, (0, LANES - M_SHARE))[None]
    bias_col, rate_col = bias_row[0, :16, None], rate_row[0, :16, None]
    skip_row = jnp.repeat(skip, SHD)[None]
    pieces = CORES * slots
    state_flops = 2 * pieces * piece * m_cols * (piece + 2 * NS)
    chunk_args = [
        features, inject, readout, raw, raw_t, bias_row, bias_col, rate_row, rate_col, skip_row,
    ]
    within, local_state, logs = over_pieces(
        chunk_kernel,
        "chunk",
        chunk_args,
        range(5, 10),
        [
            ((pieces, piece, m_cols), F32),
            ((pieces, m_cols, NS), BF16),
            ((pieces, piece, LANES), F32),
        ],
        state_flops,
    )
    decays = jnp.exp(logs[:, piece - 1, :M_SHARE]).reshape(CORES, slots, M_SHARE)
    decays_h = place.by_core(decays, decays[::-1])
    all_decays = lax.all_gather(decays_h, AXES, axis=0, tiled=False)
    all_decays = all_decays.reshape(chips, CORES, groups, CORES, slots, M_SHARE)
    all_decays = lax.dynamic_index_in_dim(all_decays, core, 1, False)
    state_in = carried(
        place, local_state.reshape(CORES, slots, m_cols, NS), all_decays, False
    ).reshape(pieces, m_cols, NS)
    (ssd,) = over_pieces(
        carry_kernel,
        "carry",
        [within, readout, state_in, logs],
        (),
        [((pieces, piece, m_cols), BF16)],
        2 * pieces * piece * m_cols * NS,
    )
    ssd = ssd.reshape(CORES, slots, piece, m_cols).astype(F32)
    gate_value, gate_slope = silu_and_slope(zgate.astype(F32))
    gated_raw = ssd * gate_value
    squares = jnp.sum(gated_raw * gated_raw, axis=-1)
    squares = squares + place.swap(squares)[::-1]
    scale_mixer = lax.rsqrt(squares / (SH * SHD) + 1e-05)[..., None]
    gated = (gated_raw * scale_mixer * gain_mixer).astype(BF16).reshape(rows_all, m_cols)

    def own_sum(partial):
        partial = partial.reshape(CORES, -1, partial.shape[-1])
        return partial[0] + place.swap(partial[1].astype(BF16)).astype(F32)

    def with_other(value):
        return jnp.stack([value, place.swap(value)]).reshape(-1, value.shape[-1])

    mixers = own_sum(mm(attended, w_attn_out) + mm(gated, w_mixer_out))
    residual = tokens[0][:, HALO:].reshape(-1, width) + mixers
    scale_post = inverse_rms(residual)
    post = with_other((residual * scale_post * gain_post).astype(BF16))
    gate_lin = mm(post, w_gate)
    up_lin = mm(post, w_up)
    gate_act, gate_act_slope = silu_and_slope(gate_lin)
    hidden = (gate_act * up_lin).astype(BF16)
    valid_own = valid[0].reshape(-1, 1)
    layer_out = (valid_own * (residual + own_sum(mm(hidden, w_down)))).astype(BF16)

    dhidden = mm(dy, w_down, NT)
    dgate = (dhidden * up_lin * gate_act_slope).astype(BF16)
    dup = (dhidden * gate_act).astype(BF16)

    def scatter_parity(grad, rows, b_first):
        return place.reduce_chips(grad.reshape(na, nb, groups, rows, width), 0, b_first)

    def scatter_columns(grad, b_first):
        return place.reduce_chips(
            grad.reshape(na, nb, CORES, groups, shard_rows, -1), 1, b_first
        )

    grad_down = scatter_parity(mm(hidden, dy, TN), ff_rows, True)
    grad_gate = scatter_columns(mm(post, dgate, TN), False)
    grad_up = scatter_columns(mm(post, dup, TN), True)
    dpost = own_sum(mm(dgate, w_gate, NT) + mm(dup, w_up, NT))
    dresidual = dy_own.reshape(-1, width) + rms_back(residual, scale_post, gain_post, dpost)
    grad_post_gain = jnp.sum(dpost * residual * scale_post, axis=0)
    dmix = with_other(dresidual.astype(BF16))

    dattended = mm(dmix, w_attn_out, NT).astype(BF16)
    dgated = mm(dmix, w_mixer_out, NT).reshape(CORES, slots, piece, m_cols)
    grad_outs = jnp.concatenate(
        [
            mm(attended, dmix, TN).reshape(chips // 2, CORES, groups, out_rows, width),
            mm(gated, dmix, TN).reshape(chips // 2, CORES, groups, mix_rows, width),
        ],
        axis=3,
    )
    kept = lax.dynamic_index_in_dim(grad_outs, core, 1, False)
    got = place.swap(lax.dynamic_index_in_dim(grad_outs, 1 - core, 1, False).astype(BF16))
    got = got.astype(F32)
    grad_outs = jnp.concatenate([place.by_core(kept, got), place.by_core(got, kept)], axis=0)
    grad_outs = scatter_parity(grad_outs, out_rows + mix_rows, False)
    scaled = dgated * gain_mixer
    inner = jnp.sum(scaled * gated_raw, axis=-1)
    inner = (inner + place.swap(inner)[::-1])[..., None] / (SH * SHD)
    dgated_raw = scale_mixer * scaled - gated_raw * (scale_mixer**3 * inner)
    grad_mixer_gain = jnp.sum(dgated * gated_raw * scale_mixer, axis=(0, 1, 2))
    dssd = (dgated_raw * gate_value).astype(BF16).reshape(pieces, piece, m_cols)
    dzgate = (dgated_raw * ssd * gate_slope).astype(BF16)

    (direct,) = over_pieces(
        direct_kernel,
        "direct",
        [dssd, readout, logs],
        (),
        [((pieces, m_cols, NS), BF16)],
        2 * pieces * piece * m_cols * NS,
    )
    later = carried(
        place, direct.reshape(CORES, slots, m_cols, NS), all_decays, True
    ).reshape(pieces, m_cols, NS)

    dout = by_heads(
        dattended.reshape(CORES, slots, piece, Q_SHARE, HD), HD, 0
    )
    dqueries, dkv = attend_back(pieces_at, lengths, queries, kv, heads_out, dout, lse, piece)
    dkv_own = jnp.stack(
        [
            place.reduce_chips(
                dkv[s].reshape(na, nb, CORES, groups, piece, 2 * HD), 1, s % 2 == 0
            )
            for s in range(slots)
        ],
        axis=1,
    )
    dkv_own = place.by_core(dkv_own, dkv_own[::-1])

    agree = jnp.sum(
        later.astype(F32) * state_in.astype(F32), axis=-1
    ).reshape(pieces, M_SHARE, SHD)
    agree = jnp.pad(jnp.sum(agree, axis=-1), ((0, 0), (0, LANES - M_SHARE)))[:, None]
    dfeatures, dinject, dreadout, draw, sums = over_pieces(
        chunk_back_kernel,
        "chunk_back",
        chunk_args + [dssd, state_in, later, agree],
        range(5, 10),
        [
            ((pieces, piece, m_cols), F32),
            ((pieces, piece, NS), F32),
            ((pieces, piece, NS), F32),
            ((pieces, piece, LANES), F32),
            ((pieces, 8, LANES), F32),
        ],
        4 * state_flops,
        [pltpu.VMEM((LANES, 2 * LANES), F32), pltpu.VMEM((piece, LANES), F32)],
    )
    head_sums = jnp.sum(sums, axis=0)[:3, :M_SHARE]
    nothing = jnp.zeros_like(head_sums)
    head_sums = jnp.concatenate(
        [place.by_core(head_sums, nothing), place.by_core(nothing, head_sums)], axis=1
    )
    head_sums = lax.psum(head_sums, AXES)
    head_sums = lax.dynamic_slice_in_dim(head_sums, place.at["z"] * (SH // groups), SH // groups, 1)

    dinject = dinject.reshape(CORES, slots, piece, NS)
    dreadout = dreadout.reshape(CORES, slots, piece, NS)
    dshared = place.by_core(dinject, dreadout) + place.swap(
        place.by_core(dreadout, dinject).astype(BF16)
    )[::-1].astype(F32)
    dconv = jnp.concatenate([dfeatures.reshape(CORES, slots, piece, m_cols), dshared], axis=-1)
    dpre = dconv * conv_slope
    grad_taps = []
    dmixed = jnp.zeros((CORES, slots, piece + HALO, c_cols), F32)
    for tap in range(KC):
        first = HALO - KC + 1 + tap
        seen = mixed[:, :, first : first + piece].astype(F32)
        grad_taps.append(jnp.sum(dpre * seen, axis=(0, 1, 2)))
        dmixed = dmixed + jnp.pad(
            dpre * taps[tap], ((0, 0), (0, 0), (first, KC - 1 - tap), (0, 0))
        )
    grad_shift = jnp.sum(dpre, axis=(0, 1, 2))
    dmixed = dmixed.astype(BF16)

    def halo_rows(value):
        value = value.reshape(CORES, slots, piece, -1)
        return jnp.pad(value, ((0, 0), (0, 0), (HALO, 0), (0, 0)))

    dstep = draw[..., :M_SHARE].astype(BF16)
    dms = jnp.concatenate(
        [
            dmixed,
            halo_rows(dstep),
            jnp.zeros((CORES, slots, piece + HALO, ms_cols - small_at), BF16),
        ],
        axis=-1,
    ).reshape(rows_halo, ms_cols)
    dq_rows = from_heads(dqueries[..., :HD] * scale)
    dq_rows = rotate(dq_rows, cos_part, -sin_part).reshape(CORES, slots, piece, q_cols)
    dk_rows = rotate(dkv_own[..., None, :HD], cos_part, -sin_part)[..., 0, :]
    dlin = jnp.concatenate([dq_rows, dk_rows, dkv_own[..., HD:]], axis=-1).astype(BF16)
    daz = halo_rows(jnp.concatenate([dlin, dzgate], axis=-1)).reshape(rows_halo, az_cols)
    dnormed = mm(daz, w_az, NT) + mm(dms, w_ms, NT)
    dnormed = own_sum(dnormed).reshape(slots, piece + HALO, width)
    rim_back = lax.ppermute(
        dnormed[:, HALO - KC + 1 : HALO].astype(BF16),
        AXES,
        [(i + 1, i) for i in range(devices - 1)],
    ).astype(F32)
    dnormed = dnormed[:, HALO:] + jnp.pad(rim_back, ((0, 0), (piece - KC + 1, 0), (0, 0)))
    own, own_scale = tokens[0][:, HALO:], scale_in[0][:, HALO:]
    input_grad = dresidual.reshape(slots, piece, width) + rms_back(
        own, own_scale, gain_in, dnormed
    )
    grad_input_gain = jnp.sum(dnormed * own * own_scale, axis=(0, 1))

    zero_half = jnp.zeros((m_cols,), F32)

    def conv_whole(value):
        none = jnp.zeros_like(value)
        first, second = place.by_core(value, none), place.by_core(none, value)
        return jnp.concatenate(
            [first[..., :m_cols], second[..., :m_cols], first[..., m_cols:], second[..., m_cols:]],
            axis=-1,
        )

    grad_mixer_gain = jnp.concatenate(
        [place.by_core(grad_mixer_gain, zero_half), place.by_core(zero_half, grad_mixer_gain)]
    )
    grad_taps = conv_whole(jnp.stack(grad_taps)).reshape(KC, devices, -1)
    vector_grads = jnp.concatenate(
        [
            grad_input_gain.reshape(devices, -1),
            grad_mixer_gain.reshape(devices, -1),
            grad_post_gain.reshape(devices, -1),
            conv_whole(grad_shift).reshape(devices, -1),
            jnp.transpose(grad_taps, (1, 0, 2)).reshape(devices, -1),
        ],
        axis=1,
    )
    vector_size = vector_grads.shape[1]
    vector_grads = jnp.pad(
        vector_grads, ((0, 0), (0, small_cols * shard_rows - vector_size))
    ).reshape(width, small_cols)
    grad_az = scatter_columns(mm(normed, daz, TN), False)
    grad_ms = mm(normed, dms, TN)
    grad_ms = lax.dynamic_update_slice(grad_ms, vector_grads, (0, small_at))
    grad_ms = scatter_columns(grad_ms, True)

    columns = jnp.concatenate([grad_az, grad_ms, grad_gate, grad_up], axis=-1)
    kept = lax.dynamic_index_in_dim(columns, core, 0, False)
    got = place.swap(lax.dynamic_index_in_dim(columns, 1 - core, 0, False))
    first, second = place.by_core(kept, got), place.by_core(got, kept)

    def both_halves(start, size):
        return jnp.concatenate([first[:, start : start + size], second[:, start : start + size]], 1)

    def ff_whole(start):
        parts = [
            half[:, start : start + ff_half].reshape(shard_rows, chips, 1, -1)
            for half in (first, second)
        ]
        return jnp.concatenate(parts, axis=2).reshape(shard_rows, -1)

    grad_attn_in = jnp.concatenate(
        [both_halves(0, q_cols), both_halves(q_cols, HD), both_halves(q_cols + HD, HD)], axis=1
    )
    grad_zgate = both_halves(q_cols + 2 * HD, m_cols)
    grad_mixer_in = jnp.concatenate(
        [both_halves(az_cols, m_cols), both_halves(az_cols + m_cols, NS)], axis=1
    )
    grad_step = both_halves(az_cols + step_at, M_SHARE)
    small_sum = first + second
    small_sum = small_sum[:, az_cols + small_at : az_cols + small_at + small_cols].reshape(-1)

    return (
        layer_out.reshape(slots, piece, width),
        input_grad,
        small_sum[: ends[0]],
        grad_attn_in,
        grad_outs[:out_rows],
        grad_zgate,
        grad_mixer_in,
        grad_step,
        small_sum[ends[3] : vector_size].reshape(KC, -1),
        small_sum[ends[2] : ends[3]],
        head_sums[0],
        head_sums[1],
        head_sums[2],
        small_sum[ends[0] : ends[1]],
        grad_outs[out_rows:],
        small_sum[ends[1] : ends[2]],
        ff_whole(az_cols + ms_cols),
        ff_whole(az_cols + ms_cols + ff_half),
        grad_down,
    )


def solution(mesh):
    rows, columns, vector = P(AXES, None), P(None, AXES), P(AXES)
    tokens, heads = P(None, AXES, None), P("sp")
    in_specs = (
        tokens,
        tokens,
        P(),
        vector,
        rows,
        rows,
        rows,
        rows,
        rows,
        columns,
        vector,
        heads,
        heads,
        heads,
        vector,
        rows,
        vector,
        rows,
        rows,
        rows,
    )
    out_specs = (
        tokens,
        tokens,
        vector,
        rows,
        rows,
        rows,
        rows,
        rows,
        columns,
        vector,
        heads,
        heads,
        heads,
        vector,
        rows,
        vector,
        rows,
        rows,
        rows,
    )
    return jax.shard_map(shards, mesh=mesh, in_specs=in_specs, out_specs=out_specs, check_vma=False)
```

```python
import functools
import math

import jax
import jax.numpy as jnp
from jax import lax
from jax.experimental import pallas as pl
from jax.experimental.pallas import tpu as pltpu
from jax.sharding import PartitionSpec as P

QH = 8
KVH = 2
HD = 64
SH = 24
SHD = 64
NS = 128
KC = 4
CORES = 2
MASKED = -1e30
AXES = ("ctx", "sp")
F32 = jnp.float32
BF16 = jnp.bfloat16
LANES = 128
HALO = 8
EXTRA = 16
Q_SHARE = QH // CORES
M_SHARE = SH // CORES
VMEM = 56 * 2**20

NT = (((1,), (1,)), ((), ()))
TN = (((0,), (0,)), ((), ()))
NN = (((1,), (0,)), ((), ()))


def mm(left, right, dims=NN, precision=None):
    return lax.dot_general(
        left, right, dims, precision=precision, preferred_element_type=F32
    )


class Place:
    def __init__(self):
        ctx = lax.axis_size("ctx")
        groups = lax.axis_size("sp")
        chips = ctx // CORES
        nb = math.isqrt(chips)
        self.size = {"a": chips // nb, "b": nb, "z": groups, "c": CORES}
        self.devices = ctx * groups
        index = lax.axis_index("ctx")
        self.at = {
            "a": index // CORES // nb,
            "b": (index // CORES) % nb,
            "z": lax.axis_index("sp"),
            "c": index % CORES,
        }
        self.chip = index // CORES
        self.chips = chips
        self.scalars = jnp.stack(
            [self.at["a"], self.at["b"], self.at["z"], self.at["c"], self.chip]
        ).astype(jnp.int32)
        self.flat = index * groups + self.at["z"]

    def flat_of(self, a, b, z, c):
        return ((a * self.size["b"] + b) * CORES + c) * self.size["z"] + z

    def pairs(self, dim, by):
        found = []
        for a in range(self.size["a"]):
            for b in range(self.size["b"]):
                for z in range(self.size["z"]):
                    for c in range(CORES):
                        spot = {"a": a, "b": b, "z": z, "c": c}
                        goal = dict(spot)
                        goal[dim] = (spot[dim] + by) % self.size[dim]
                        found.append((self.flat_of(**spot), self.flat_of(**goal)))
        return found

    def shift(self, x, dim, by):
        return lax.ppermute(x, AXES, self.pairs(dim, by))

    def swap(self, x):
        return self.shift(x, "c", 1)

    def by_core(self, zero, one):
        return jnp.where(self.at["c"] == 0, zero, one)

    def chip_pairs(self, by):
        groups = self.size["z"]
        return [
            ((chip * CORES + c) * groups + z, (((chip + by) % self.chips) * CORES + c) * groups + z)
            for chip in range(self.chips)
            for c in range(CORES)
            for z in range(groups)
        ]

    def spread_z(self, x):
        return [x] + [self.shift(x, "z", k) for k in range(1, self.size["z"])]

    def spread_plane(self, x, b_first):
        found = {(0, 0): x}
        for dim in ("b", "a") if b_first else ("a", "b"):
            for key, value in list(found.items()):
                for k in range(1, self.size[dim]):
                    to = (key[0], k) if dim == "b" else (k, key[1])
                    found[to] = self.shift(value, dim, k)
        return found

    def place_z(self, parts, halves):
        groups = self.size["z"]
        rows = parts[0].shape[0]
        outs = [
            jax.ShapeDtypeStruct((groups * rows, sum(size for _, size, _ in half)), parts[0].dtype)
            for half in halves
        ]
        plan = []
        for index, half in enumerate(halves):
            to = 0
            for start, size, count in half:
                block = rows // count
                for r in range(groups):
                    for m in range(count):

                        def source(at, m=m, start=start, size=size, block=block):
                            return pl.ds(m * block, block), pl.ds(start, size)

                        def goal(at, m=m, r=r, to=to, size=size, block=block):
                            z = lax.rem(at[2] + groups - r, groups)
                            return pl.ds((m * groups + z) * block, block), pl.ds(to, size)

                        plan.append((r, source, index, goal))
                to += size
        return moved(self, parts, outs, plan)

    def gather_plane(self, halves, wanted):
        rows = halves[0].shape[0]
        near = [self.spread_plane(half, index % 2 == 0) for index, half in enumerate(halves)]
        keys = sorted(near[0])
        na, nb = self.size["a"], self.size["b"]
        widths = {}
        for _, _, size, array, column in wanted:
            widths[array] = max(widths.get(array, 0), column + size)
        outs = [
            jax.ShapeDtypeStruct((self.chips * rows, widths[k]), halves[0].dtype)
            for k in range(len(widths))
        ]
        plan = []
        for half, start, size, array, column in wanted:
            for index, (da, db) in enumerate(keys):

                def source(at, start=start, size=size):
                    return pl.ds(0, rows), pl.ds(start, size)

                def goal(at, da=da, db=db, column=column, size=size):
                    chip = lax.rem(at[0] + na - da, na) * nb + lax.rem(at[1] + nb - db, nb)
                    return pl.ds(chip * rows, rows), pl.ds(column, size)

                plan.append((half * len(keys) + index, source, array, goal))
        return moved(self, [n[key] for n in near for key in keys], outs, plan)

    def reduce_far(self, grads):
        cores = [[chip * CORES + c for chip in range(self.chips)] for c in range(CORES)]
        groups, chips = self.size["z"], self.chips
        rows = grads[0][0].shape[0] // chips
        widths = [grad.shape[1] for grad, _ in grads]
        stacked = len(set(widths)) == 1
        high = len(grads) * rows if stacked else rows
        wide = widths[0] if stacked else sum(widths)
        corner = [
            (k * rows, 0) if stacked else (0, sum(widths[:k])) for k in range(len(grads))
        ]
        outs = [jax.ShapeDtypeStruct((chips * high, wide), BF16)]
        plan = []
        for k, (row, column) in enumerate(corner):
            for chip in range(chips):

                def source(at, chip=chip, size=widths[k]):
                    return pl.ds(chip * rows, rows), pl.ds(0, size)

                def goal(at, chip=chip, row=row, column=column, size=widths[k]):
                    return pl.ds(chip * high + row, rows), pl.ds(column, size)

                plan.append((k, source, 0, goal))
        (flat,) = moved(self, [grad for grad, _ in grads], outs, plan)
        flat = lax.psum_scatter(
            flat, "ctx", scatter_dimension=0, tiled=True, axis_index_groups=cores
        )
        share, deep = rows // groups, high // groups

        def finish(flat):
            plan = []
            for k, (row, column) in enumerate(corner):
                count = grads[k][1]
                block = share // count
                for z in range(groups):
                    for m in range(count):

                        def source(at, z=z, m=m, row=row, column=column, size=widths[k], block=block):
                            return (
                                pl.ds(row + (m * groups + z) * block, block),
                                pl.ds(column, size),
                            )

                        def goal(
                            at, z=z, m=m, row=row, column=column, size=widths[k], block=block
                        ):
                            return (
                                pl.ds(z * deep + row // groups + m * block, block),
                                pl.ds(column, size),
                            )

                        plan.append((0, source, 0, goal))
            outs = [jax.ShapeDtypeStruct((high, wide), BF16)]
            (flat,) = moved(self, [flat], outs, plan)
            return lax.psum_scatter(flat, "sp", scatter_dimension=0, tiled=True)

        return flat, finish

    def reduce(self, x, dim, axis):
        n, v = self.size[dim], self.at[dim]
        total = lax.dynamic_index_in_dim(x, v, axis, False).astype(F32)
        for k in range(1, n):
            piece = lax.dynamic_index_in_dim(x, (v + k) % n, axis, False).astype(BF16)
            total = total + self.shift(piece, dim, k).astype(F32)
        return total

    def reduce_chips(self, grads, firsts):
        left = []
        for grad, b_first in zip(grads, firsts):
            if b_first:
                left.append(self.reduce(self.reduce(grad, "a", 0), "b", 0))
            else:
                left.append(self.reduce(self.reduce(grad, "b", 1), "a", 0))
        n, v = self.size["z"], self.at["z"]

        def cut(x, index):
            piece = lax.dynamic_index_in_dim(x, index, 1, False)
            return piece.reshape(-1, piece.shape[-1])

        totals = [cut(x, v) for x in left]
        for k in range(1, n):
            sent = jnp.concatenate([cut(x, (v + k) % n).astype(BF16) for x in left], axis=-1)
            got = self.shift(sent, "z", k).astype(F32)
            start = 0
            for index, total in enumerate(totals):
                stop = start + total.shape[-1]
                totals[index] = total + got[:, start:stop]
                start = stop
        return totals

    def sum_all(self, x):
        for dim in ("z", "b", "a"):
            step = 1
            while step < self.size[dim]:
                found = []
                for a in range(self.size["a"]):
                    for b in range(self.size["b"]):
                        for z in range(self.size["z"]):
                            for c in range(CORES):
                                spot = {"a": a, "b": b, "z": z, "c": c}
                                goal = dict(spot)
                                goal[dim] = spot[dim] ^ step
                                found.append((self.flat_of(**spot), self.flat_of(**goal)))
                x = x + lax.ppermute(x, AXES, found)
                step *= 2
        return x


def moved_kernel(at_ref, *refs, plan, count):
    sems = refs[-1]
    copies = [
        pltpu.make_async_copy(
            refs[source].at[where(at_ref)], refs[count + goal].at[to(at_ref)], sems.at[index]
        )
        for index, (source, where, goal, to) in enumerate(plan)
    ]
    for copy in copies:
        copy.start()
    for copy in copies:
        copy.wait()


def moved(place, sources, outs, plan):
    size = sum(math.prod(out.shape) * out.dtype.itemsize for out in outs)
    return pl.pallas_call(
        functools.partial(moved_kernel, plan=plan, count=len(sources)),
        in_specs=[pl.BlockSpec(memory_space=pltpu.SMEM)]
        + [pl.BlockSpec(memory_space=pl.ANY)] * len(sources),
        out_specs=[pl.BlockSpec(memory_space=pltpu.VMEM)] * len(outs),
        out_shape=outs,
        scratch_shapes=[pltpu.SemaphoreType.DMA((len(plan),))],
        compiler_params=pltpu.CompilerParams(vmem_limit_bytes=VMEM),
        cost_estimate=pl.CostEstimate(flops=0, bytes_accessed=2 * size, transcendentals=0),
        name="moved",
    )(place.scalars, *sources)


def rotary_tables(positions, width):
    half_width = width // 2
    inverse = 100000000000.0 ** (-jnp.arange(half_width, dtype=F32) * 2.0 / width)
    angles = positions.astype(F32)[..., None] * inverse
    return (jnp.cos(angles), jnp.sin(angles))


def rotate(value, cos_part, sin_part):
    half_width = value.shape[-1] // 2
    first = value[..., :half_width]
    second = value[..., half_width:]
    return jnp.concatenate(
        [first * cos_part - second * sin_part, second * cos_part + first * sin_part], axis=-1
    )


def inverse_rms(value):
    return lax.rsqrt(jnp.mean(value * value, axis=-1, keepdims=True) + 1e-05)


def rms_back(value, scale, gain, grad):
    scaled = grad * gain
    inner = jnp.mean(scaled * value, axis=-1, keepdims=True)
    return scale * scaled - value * (scale * scale * scale * inner)


def silu_and_slope(value):
    gate = jax.nn.sigmoid(value)
    out = value * gate
    return out, gate + out * (1.0 - gate)


def causal_keep(first_key, first_query, keys, piece, columns):
    key = first_key + lax.broadcasted_iota(jnp.int32, (keys, columns), 0)
    column = lax.broadcasted_iota(jnp.int32, (keys, columns), 1)
    head = sum((column >= piece * k).astype(jnp.int32) for k in range(1, columns // piece))
    return key <= first_query + column - head * piece


def attend_kernel(places, lengths, q_ref, kv_ref, out_ref, lse_ref, acc, top, total, *, piece):
    slot, which = pl.program_id(0), pl.program_id(1)
    first_query = places[which]
    columns = q_ref.shape[2]
    block = columns
    out_ref[...] = jnp.zeros_like(out_ref)
    lse_ref[...] = jnp.zeros_like(lse_ref)

    @pl.when(first_query < lengths[slot])
    def _():
        acc[...] = jnp.zeros_like(acc)
        top[...] = jnp.full_like(top, MASKED)
        total[...] = jnp.zeros_like(total)
        whole = first_query // block

        def visit(index, masked):
            start = pl.multiple_of(index * block, block)
            kv = kv_ref[0, pl.ds(start, block), :]
            scores = mm(kv, q_ref[0, 0], NT)
            if masked:
                keep = causal_keep(start, first_query, block, piece, columns)
                scores = jnp.where(keep, scores, MASKED)
            before = top[...]
            now = jnp.maximum(before, jnp.max(scores, axis=0, keepdims=True))
            weights = jnp.exp(scores - now)
            ratio = jnp.exp(before - now)
            total[...] = total[...] * ratio + jnp.sum(weights, axis=0, keepdims=True)
            acc[...] = acc[...] * ratio + mm(kv, weights.astype(BF16), TN)
            top[...] = now

        @pl.loop(0, whole)
        def _(index):
            visit(index, False)

        visit(whole, True)
        out_ref[0, 0] = (acc[...] / total[...]).T.astype(BF16)
        lse_ref[0, 0] = top[...] + jnp.log(total[...])


def attend(places, lengths, queries, kv, piece):
    slots, _, columns, width = queries.shape
    length = kv.shape[1]
    return pl.pallas_call(
        functools.partial(attend_kernel, piece=piece),
        grid_spec=pltpu.PrefetchScalarGridSpec(
            num_scalar_prefetch=2,
            grid=(slots, CORES),
            in_specs=[
                pl.BlockSpec((1, 1, columns, width), lambda s, e, *_: (s, e, 0, 0)),
                pl.BlockSpec((1, length, width), lambda s, e, *_: (s, 0, 0)),
            ],
            out_specs=[
                pl.BlockSpec((1, 1, columns, width), lambda s, e, *_: (s, e, 0, 0)),
                pl.BlockSpec((1, 1, 1, columns), lambda s, e, *_: (s, e, 0, 0)),
            ],
            scratch_shapes=[
                pltpu.VMEM((width, columns), F32),
                pltpu.VMEM((1, columns), F32),
                pltpu.VMEM((1, columns), F32),
            ],
        ),
        out_shape=[
            jax.ShapeDtypeStruct(queries.shape, BF16),
            jax.ShapeDtypeStruct((slots, CORES, 1, columns), F32),
        ],
        compiler_params=pltpu.CompilerParams(vmem_limit_bytes=VMEM),
        cost_estimate=pl.CostEstimate(
            flops=2 * 2 * slots * CORES * columns * length * width // 2,
            bytes_accessed=slots * length * width * 4,
            transcendentals=slots * CORES * columns * length // 2,
        ),
        name="attend",
    )(places, lengths, queries, kv)


def attend_back_kernel(
    places, lengths, q_ref, kv_ref, out_ref, dout_ref, lse_ref, dq_ref, dkv_ref, dkv, dq, *, piece
):
    slot, which = pl.program_id(0), pl.program_id(1)
    first_query = places[which]
    columns = q_ref.shape[2]
    block = columns
    dq_ref[...] = jnp.zeros_like(dq_ref)

    @pl.when(which == 0)
    def _():
        dkv[...] = jnp.zeros_like(dkv)

    @pl.when(first_query < lengths[slot])
    def _():
        dq[...] = jnp.zeros_like(dq)
        queries = q_ref[0, 0]
        dout = dout_ref[0, 0]
        both = dout.astype(F32) * out_ref[0, 0].astype(F32)
        delta = mm(jnp.ones((8, both.shape[1]), F32), both, NT, lax.Precision.HIGHEST)[:1]
        lse = lse_ref[0, 0]
        whole = first_query // block

        def visit(index, masked):
            start = pl.multiple_of(index * block, block)
            kv = kv_ref[0, pl.ds(start, block), :]
            scores = mm(kv, queries, NT)
            if masked:
                keep = causal_keep(start, first_query, block, piece, columns)
                scores = jnp.where(keep, scores, MASKED)
            probs = jnp.exp(scores - lse)
            dprobs = mm(kv, dout, NT)
            dscores = (probs * (dprobs - delta)).astype(BF16)
            probs = probs.astype(BF16)
            dkv[pl.ds(start, block), :] += mm(dscores, queries) + mm(probs, dout)
            dq[...] += mm(kv, dscores, TN)

        @pl.loop(0, whole)
        def _(index):
            visit(index, False)

        visit(whole, True)
        dq_ref[0, 0] = dq[...].T.astype(dq_ref.dtype)

    @pl.when(which == CORES - 1)
    def _():
        dkv_ref[0] = dkv[...].astype(dkv_ref.dtype)


def attend_back(places, lengths, queries, kv, out, dout, lse, piece):
    slots, _, columns, width = queries.shape
    length = kv.shape[1]
    rows = pl.BlockSpec((1, 1, columns, width), lambda s, e, *_: (s, e, 0, 0))
    keys = pl.BlockSpec((1, length, width), lambda s, e, *_: (s, 0, 0))
    return pl.pallas_call(
        functools.partial(attend_back_kernel, piece=piece),
        grid_spec=pltpu.PrefetchScalarGridSpec(
            num_scalar_prefetch=2,
            grid=(slots, CORES),
            in_specs=[
                rows,
                keys,
                rows,
                rows,
                pl.BlockSpec((1, 1, 1, columns), lambda s, e, *_: (s, e, 0, 0)),
            ],
            out_specs=[rows, keys],
            scratch_shapes=[pltpu.VMEM((length, width), F32), pltpu.VMEM((width, columns), F32)],
        ),
        out_shape=[
            jax.ShapeDtypeStruct(queries.shape, F32),
            jax.ShapeDtypeStruct(kv.shape, BF16),
        ],
        compiler_params=pltpu.CompilerParams(vmem_limit_bytes=VMEM),
        cost_estimate=pl.CostEstimate(
            flops=5 * 2 * slots * CORES * columns * length * width // 2,
            bytes_accessed=slots * length * width * 6,
            transcendentals=slots * CORES * columns * length // 2,
        ),
        name="attend_back",
    )(places, lengths, queries, kv, out, dout, lse)


def lower(rows, transposed=False):
    row = lax.broadcasted_iota(jnp.int32, (rows, rows), 0)
    column = lax.broadcasted_iota(jnp.int32, (rows, rows), 1)
    return row <= column if transposed else row >= column


def paired(first, second, shape):
    lane = lax.broadcasted_iota(jnp.int32, shape, 1)
    return jnp.where(lane < SHD, first, second)


def chunk_terms(raw_ref, raw_t_ref, bias_ref, bias_t_ref, rate_ref, rate_t_ref):
    rows = raw_ref.shape[1]
    steps = jax.nn.softplus(raw_ref[0] + bias_ref[...])
    steps_t = jax.nn.softplus(raw_t_ref[0] + bias_t_ref[...])
    high = lax.Precision.HIGHEST
    logs = mm(lower(rows).astype(F32), steps * rate_ref[...], NN, high)
    logs_t = mm(steps_t * rate_t_ref[...], lower(rows, True).astype(F32), NN, high)
    return steps, steps_t, logs, logs_t


def chunk_kernel(
    f_ref, b_ref, c_ref, raw_ref, raw_t_ref, bias_ref, bias_t_ref, rate_ref, rate_t_ref, skip_ref,
    at_ref, out_ref, logs_ref, *rest,
):
    state_refs, held = rest[:-1], rest[-1]
    steps, steps_t, logs, logs_t = chunk_terms(
        raw_ref, raw_t_ref, bias_ref, bias_t_ref, rate_ref, rate_t_ref
    )
    logs_ref[0] = logs
    rows = logs.shape[0]
    inject = b_ref[0]
    mix = jnp.where(lower(rows), mm(c_ref[0], inject, NT), 0.0)
    tail = jnp.exp(logs[rows - 1 :] - logs) * steps
    for pair in range(M_SHARE // 2):
        lanes = slice(pair * LANES, (pair + 1) * LANES)
        feats = f_ref[0, :, lanes]
        outs = []
        for head in (2 * pair, 2 * pair + 1):
            gap = jnp.minimum(logs[:, head : head + 1] - logs_t[head : head + 1, :], 0.0)
            kernel = mix * jnp.exp(gap) * steps_t[head : head + 1, :]
            outs.append(mm(kernel.astype(BF16), feats))
        wide = feats.astype(F32)
        out_ref[0, :, lanes] = paired(outs[0], outs[1], wide.shape) + skip_ref[:, lanes] * wide
        weight = paired(
            tail[:, 2 * pair : 2 * pair + 1], tail[:, 2 * pair + 1 : 2 * pair + 2], wide.shape
        )
        state = mm((wide * weight).astype(BF16), inject, TN).astype(BF16)
        keep_heads(held, state, pair)
    decay = jnp.exp(logs[rows - 1 :])
    line = lax.broadcasted_iota(jnp.int32, (EXTRA, LANES), 0)
    high = decay.astype(BF16).astype(F32)
    extra = jnp.where(line == 0, high, jnp.where(line == 1, decay - high, 0.0)).astype(BF16)
    for group in range(len(state_refs)):
        held[group, held.shape[1] - EXTRA :, :] = extra
    send_groups(held, state_refs, at_ref)


def carry_kernel(out_ref, c_ref, logs_ref, *rest):
    groups = len(rest) - 3
    at_ref, ssd_ref, held = rest[groups], rest[groups + 1], rest[groups + 2]
    take_groups(held, rest[:groups], at_ref)
    decay = jnp.exp(logs_ref[0])
    for pair in range(M_SHARE // 2):
        lanes = slice(pair * LANES, (pair + 1) * LANES)
        read = mm(c_ref[0], pair_rows(held, pair), NT)
        weight = paired(
            decay[:, 2 * pair : 2 * pair + 1], decay[:, 2 * pair + 1 : 2 * pair + 2], read.shape
        )
        ssd_ref[0, :, lanes] = (out_ref[0, :, lanes] + read * weight).astype(BF16)


def direct_kernel(d_ref, c_ref, logs_ref, at_ref, *rest):
    held = rest[-1]
    decay = jnp.exp(logs_ref[0])
    for pair in range(M_SHARE // 2):
        lanes = slice(pair * LANES, (pair + 1) * LANES)
        grad = d_ref[0, :, lanes].astype(F32)
        weight = paired(
            decay[:, 2 * pair : 2 * pair + 1], decay[:, 2 * pair + 1 : 2 * pair + 2], grad.shape
        )
        state = mm((grad * weight).astype(BF16), c_ref[0], TN).astype(BF16)
        keep_heads(held, state, pair)
    send_groups(held, rest[:-1], at_ref)


def chunk_back_kernel(
    f_ref, b_ref, c_ref, raw_ref, raw_t_ref, bias_ref, bias_t_ref, rate_ref, rate_t_ref, skip_ref,
    d_ref, *rest,
):
    groups = (len(rest) - 10) // 2
    at_ref = rest[2 * groups]
    df_ref, db_ref, dc_ref, draw_ref, sums_ref = rest[2 * groups + 1 : 2 * groups + 6]
    columns, row_sums, states, laters = rest[2 * groups + 6 :]
    take_groups(states, rest[:groups], at_ref)
    take_groups(laters, rest[groups : 2 * groups], at_ref)
    steps, steps_t, logs, logs_t = chunk_terms(
        raw_ref, raw_t_ref, bias_ref, bias_t_ref, rate_ref, rate_t_ref
    )
    rows = logs.shape[0]
    inject, readout = b_ref[0], c_ref[0]
    keep = lower(rows)
    mix = jnp.where(keep, mm(readout, inject, NT), 0.0)
    columns[...] = jnp.zeros_like(columns)
    row_sums[...] = jnp.zeros_like(row_sums)
    decay = jnp.exp(logs)
    end_decay = jnp.exp(logs[rows - 1 :] - logs)
    tail = end_decay * steps
    dmix = jnp.zeros((rows, rows), F32)
    db = jnp.zeros((rows, NS), F32)
    dc = jnp.zeros((rows, NS), F32)
    to_state = jnp.zeros((rows, LANES), F32)
    from_state = jnp.zeros((rows, LANES), F32)
    skips = jnp.zeros((1, LANES), F32)
    agree = jnp.zeros((1, LANES), F32)
    head_lane = lax.broadcasted_iota(jnp.int32, (rows, LANES), 1)
    for pair in range(M_SHARE // 2):
        lanes = slice(pair * LANES, (pair + 1) * LANES)
        feats, grad = f_ref[0, :, lanes], d_ref[0, :, lanes]
        wide, wide_grad = feats.astype(F32), grad.astype(F32)
        later = pair_rows(laters, pair)
        state = pair_rows(states, pair)
        agreed = later.astype(F32) * state.astype(F32)
        pushed = mm(inject, later, NT)
        read = mm(readout, state, NT)
        push_part = wide * pushed
        read_part = wide_grad * read
        skip_part = wide * wide_grad
        grads = []
        for half, head in enumerate((2 * pair, 2 * pair + 1)):
            column = slice(head, head + 1)
            lane = lax.broadcasted_iota(jnp.int32, wide.shape, 1)
            mine = (lane < SHD) if half == 0 else (lane >= SHD)
            step_row = steps_t[column, :]
            gap = jnp.minimum(logs[:, column] - logs_t[column, :], 0.0)
            fade = jnp.exp(gap)
            dkernel = mm(jnp.where(mine, wide_grad, 0.0).astype(BF16), feats, NT)
            faded = dkernel * fade
            stepped = faded * step_row
            dmix = dmix + stepped
            kernel = mix * fade * step_row
            columns[column, 0:rows] = jnp.sum(faded * mix, axis=0, keepdims=True)
            here = head_lane == head
            row_sums[...] += jnp.where(here, jnp.sum(stepped * mix, axis=1, keepdims=True), 0.0)
            grads.append(mm(kernel.astype(BF16), grad, TN))
            to_state = to_state + jnp.where(
                here, jnp.sum(jnp.where(mine, push_part, 0.0), axis=1, keepdims=True), 0.0
            )
            from_state = from_state + jnp.where(
                here, jnp.sum(jnp.where(mine, read_part, 0.0), axis=1, keepdims=True), 0.0
            )
            same = agreed[half * SHD : (half + 1) * SHD]
            same = jnp.sum(jnp.sum(same, axis=0, keepdims=True), axis=1, keepdims=True)
            agree = agree + jnp.where(here[:1], same, 0.0)
            skips = skips + jnp.where(
                here[:1],
                jnp.sum(
                    jnp.sum(jnp.where(mine, skip_part, 0.0), axis=1, keepdims=True),
                    axis=0,
                    keepdims=True,
                ),
                0.0,
            )
        first, second = slice(2 * pair, 2 * pair + 1), slice(2 * pair + 1, 2 * pair + 2)
        weight = paired(tail[:, first], tail[:, second], wide.shape)
        df_ref[0, :, lanes] = (
            paired(grads[0], grads[1], wide.shape) + skip_ref[:, lanes] * wide_grad + weight * pushed
        )
        db = db + mm((wide * weight).astype(BF16), later)
        seen = paired(decay[:, first], decay[:, second], wide.shape)
        dc = dc + mm((wide_grad * seen).astype(BF16), state)
    low = dmix * jnp.where(keep, 1.0, 0.0)
    low = low.astype(BF16)
    db_ref[0] = db + mm(low, readout, TN)
    dc_ref[0] = dc + mm(low, inject)
    direct = columns[...].T[:rows]
    push = end_decay * to_state
    dlogs = row_sums[...] - steps * direct + decay * from_state - steps * push
    end = jnp.sum(steps * push, axis=0, keepdims=True) + decay[rows - 1 :] * agree
    last = lax.broadcasted_iota(jnp.int32, (rows, LANES), 0) == rows - 1
    dlogs = dlogs + jnp.where(last, end, 0.0)
    summed = mm(lower(rows, True).astype(F32), dlogs, NN, lax.Precision.HIGHEST)
    dsteps = direct + push + summed * rate_ref[...]
    draw = dsteps * jax.nn.sigmoid(raw_ref[0] + bias_ref[...])
    draw_ref[0] = draw
    line = lax.broadcasted_iota(jnp.int32, (8, LANES), 0)
    dbias = jnp.sum(draw, axis=0, keepdims=True)
    dlog = jnp.sum(summed * steps, axis=0, keepdims=True) * rate_ref[...]
    sums_ref[0] = jnp.where(
        line == 0, dbias, jnp.where(line == 1, dlog, jnp.where(line == 2, skips, 0.0))
    )


def over_pieces(kernel, name, args, whole, outs, flops, at, scratch=()):
    pieces = args[0].shape[0]

    def spec(shape, split):
        if split:
            return pl.BlockSpec((1,) + shape[1:], lambda i: (i,) + (0,) * (len(shape) - 1))
        return pl.BlockSpec(shape, lambda i: (0,) * len(shape))

    shapes = [(arg.shape, index not in whole) for index, arg in enumerate(args)]
    nbytes = sum(arg.size * arg.dtype.itemsize for arg in args)
    nbytes += sum(math.prod(shape) * dtype.dtype.itemsize for shape, dtype in outs)
    return pl.pallas_call(
        kernel,
        grid=(pieces,),
        in_specs=[spec(shape, split) for shape, split in shapes]
        + [pl.BlockSpec(memory_space=pltpu.SMEM)],
        out_specs=[spec(shape, True) for shape, _ in outs],
        out_shape=[jax.ShapeDtypeStruct(shape, dtype) for shape, dtype in outs],
        scratch_shapes=list(scratch),
        compiler_params=pltpu.CompilerParams(vmem_limit_bytes=VMEM),
        cost_estimate=pl.CostEstimate(flops=flops, bytes_accessed=nbytes, transcendentals=0),
        name=name,
    )(*args, at)


def keep_heads(held, state, pair):
    share = M_SHARE // held.shape[0]
    for half in range(2):
        group, spot = divmod(2 * pair + half, share)
        held[group, spot * SHD : (spot + 1) * SHD, :] = state[half * SHD : (half + 1) * SHD]


def pair_rows(held, pair):
    share = M_SHARE // held.shape[0]
    found = []
    for half in range(2):
        group, spot = divmod(2 * pair + half, share)
        found.append(held[group, spot * SHD : (spot + 1) * SHD, :])
    return jnp.concatenate(found, axis=0)


def send_groups(held, refs, at_ref):
    for r, ref in enumerate(refs):
        ref[0] = held[lax.rem(at_ref[2] + r, len(refs))]


def take_groups(held, refs, at_ref):
    for r, ref in enumerate(refs):
        held[lax.rem(at_ref[2] + len(refs) - r, len(refs))] = ref[0]


def scan_kernel(at_ref, *refs, groups, chips, share, reverse, last):
    rows = share * SHD
    states, marks = refs[:groups], refs[groups : 2 * groups]
    refs = refs[2 * groups :]
    chip, z, core = at_ref[4], at_ref[2], at_ref[3]
    lane = lax.broadcasted_iota(jnp.int32, (1, LANES), 1)

    def pick(pair, offset):
        both = pair[0:1].astype(F32) + pair[1:2].astype(F32)
        return [
            jnp.sum(jnp.where(lane == offset + i, both, 0.0), axis=1, keepdims=True)
            for i in range(share)
        ]

    def step(run, factors, new):
        return jnp.concatenate(
            [
                factors[i] * run[i * SHD : (i + 1) * SHD] + new[i * SHD : (i + 1) * SHD]
                for i in range(share)
            ],
            axis=0,
        )

    if last:
        totals, fades = refs[: chips - 1], refs[chips - 1 : 2 * chips - 2]
        outs, held, decay, entered = (
            refs[2 * chips - 2 : 2 * chips - 2 + groups],
            refs[-3],
            refs[-2],
            refs[-1],
        )
    else:
        total_ref, held, decay = refs
    for r in range(groups):
        to = lax.rem(z + groups - r, groups)
        held[to] = states[r][:, 0, :rows]
        decay[to] = marks[r][:, 0]
    run = jnp.zeros((rows, NS), F32)
    if last:
        for k in range(chips - 1, 0, -1):
            part = chips - k if reverse else k
            reached = chip + k < chips if reverse else chip >= k
            new = step(run, pick(fades[part - 1][0], 0), totals[part - 1][0, :rows].astype(F32))
            run = jnp.where(reached, new, run)
    fade = [jnp.ones((1, 1), F32)] * share
    order = [(h, k) for h in range(CORES) for k in range(groups)]
    for h, k in order[::-1] if reverse else order:
        e = lax.rem(h + core, CORES)
        if last:
            entered[k, e] = run.astype(BF16)
        factors = pick(decay[k, e], z * share)
        run = step(run, factors, held[k, e].astype(F32))
        fade = [one * two for one, two in zip(fade, factors)]
    if last:
        for r in range(groups):
            outs[r][:, 0] = entered[lax.rem(z + r, groups)]
        return
    line = lax.broadcasted_iota(jnp.int32, (EXTRA, LANES), 0)
    place = lax.broadcasted_iota(jnp.int32, (EXTRA, LANES), 1)
    extra = jnp.zeros((EXTRA, LANES), F32)
    for i in range(share):
        high = fade[i].astype(BF16).astype(F32)
        extra = extra + jnp.where((line == 0) & (place == i), high, 0.0)
        extra = extra + jnp.where((line == 1) & (place == i), fade[i] - high, 0.0)
    total_ref[0, :rows] = run.astype(BF16)
    total_ref[0, rows:] = extra.astype(BF16)


def carried(place, at, states, marks, fades, reverse):
    groups, chips = place.size["z"], place.chips
    share = M_SHARE // groups
    rows = share * SHD
    slots = states[0].shape[1]
    parts = [part if r == 0 else place.shift(part, "z", r) for r, part in enumerate(states)]
    marks = parts if marks is None else marks
    block = [pl.BlockSpec((CORES, 1, part.shape[2], NS), lambda s, *_: (0, s, 0, 0)) for part in parts]
    mark = pl.BlockSpec((CORES, 1, EXTRA, NS), lambda s, *_: (0, s, rows // EXTRA, 0))
    total = pl.BlockSpec((1, rows + EXTRA, NS), lambda s, *_: (s, 0, 0))
    fade = pl.BlockSpec((1, EXTRA, NS), lambda s, *_: (s, rows // EXTRA, 0))
    result = pl.BlockSpec((CORES, 1, rows, NS), lambda s, *_: (0, s, 0, 0))
    scratch = [
        pltpu.VMEM((groups, CORES, rows, NS), BF16),
        pltpu.VMEM((groups, CORES, EXTRA, NS), BF16),
    ]

    def call(last, args, specs, outs, out_specs, more):
        return pl.pallas_call(
            functools.partial(
                scan_kernel, groups=groups, chips=chips, share=share, reverse=reverse, last=last
            ),
            grid_spec=pltpu.PrefetchScalarGridSpec(
                num_scalar_prefetch=1,
                grid=(slots,),
                in_specs=block + [mark] * groups + specs,
                out_specs=out_specs,
                scratch_shapes=scratch + more,
            ),
            out_shape=outs,
            compiler_params=pltpu.CompilerParams(vmem_limit_bytes=VMEM),
            cost_estimate=pl.CostEstimate(
                flops=4 * slots * CORES * groups * rows * NS,
                bytes_accessed=4 * slots * CORES * groups * rows * NS,
                transcendentals=0,
            ),
            name="scan",
        )(at, *parts, *marks, *args)

    leaving = call(
        False, [], [], jax.ShapeDtypeStruct((slots, rows + EXTRA, NS), BF16), total, []
    )
    totals = [lax.ppermute(leaving, AXES, place.chip_pairs(k)) for k in range(1, chips)]
    fades = totals if fades is None else fades
    entering = call(
        True,
        [*totals, *fades],
        [total] * (chips - 1) + [fade] * (chips - 1),
        [jax.ShapeDtypeStruct((CORES, slots, rows, NS), BF16)] * groups,
        [result] * groups,
        [pltpu.VMEM((groups, CORES, rows, NS), BF16)],
    )
    found = [part if r == 0 else place.shift(part, "z", r) for r, part in enumerate(entering)]
    return [part.reshape(CORES * slots, rows, NS) for part in found], marks, fades


def shards(
    hidden_in,
    out_grad,
    lengths,
    input_gain,
    attn_in_weight,
    attn_out_weight,
    zgate_weight,
    mixer_in_weight,
    step_weight,
    conv_weight,
    conv_bias,
    step_bias,
    decay_log,
    skip_scale,
    mixer_gain,
    mixer_out_weight,
    post_gain,
    gate_weight,
    up_weight,
    down_weight,
):
    place = Place()
    core = place.at["c"]
    groups, chips, devices = place.size["z"], place.chips, place.devices
    na, nb = place.size["a"], place.size["b"]
    slots, piece, width = hidden_in.shape
    span = piece * groups
    rows_all = CORES * slots * piece
    rows_halo = CORES * slots * (piece + HALO)
    q_cols, m_cols = Q_SHARE * HD, M_SHARE * SHD
    lin_cols = q_cols + 2 * HD
    c_cols = m_cols + NS
    f_cols = m_cols // 2
    at = place.scalars
    shard_rows = attn_in_weight.shape[0]
    out_rows, mix_rows, ff_rows = (
        attn_out_weight.shape[0],
        mixer_out_weight.shape[0],
        down_weight.shape[0],
    )
    ff_half = ff_rows * groups * chips

    rim = lax.ppermute(
        hidden_in[:, piece - KC + 1 :], AXES, [(i, i + 1) for i in range(devices - 1)]
    )
    block = jnp.concatenate(
        [jnp.zeros((slots, HALO - KC + 1, width), BF16), rim, hidden_in], axis=1
    )
    other_index = place.flat + jnp.where(core == 0, groups, -groups)
    pieces_at = jnp.stack([place.flat, other_index]) * piece
    positions = pieces_at[:, None] + jnp.arange(piece, dtype=jnp.int32)
    valid = (positions[:, None, :] < lengths[None, :, None]).astype(F32)
    tokens = jnp.stack([block, place.swap(block)]).astype(F32)
    dy_own = out_grad.astype(F32) * valid[0][..., None]
    dy_low = dy_own.astype(BF16)
    dy = jnp.stack([dy_low, place.swap(dy_low)]).reshape(rows_all, width)

    small = jnp.concatenate([input_gain, mixer_gain, post_gain, conv_bias, conv_weight.reshape(-1)])
    vector_size = small.shape[0]
    terms = jnp.stack([step_bias, decay_log, skip_scale])
    term_size = terms.size
    split_terms = []
    for _ in range(3):
        part = lax.reduce_precision(terms, 8, 7)
        split_terms.append(part.reshape(-1).astype(BF16))
        terms = terms - part
    small = jnp.concatenate([small, *split_terms])
    small_cols = -(-small.shape[0] // shard_rows)
    small = jnp.pad(small, (0, small_cols * shard_rows - small.shape[0]))
    small = small.reshape(shard_rows, small_cols)
    small_at = M_SHARE
    ms_cols = -(-(small_at + small_cols) // LANES) * LANES
    a_cols, b_cols = lin_cols + f_cols, c_cols - f_cols + ms_cols

    def ff_columns(weight, half):
        return weight.reshape(shard_rows, chips, CORES, -1)[:, :, half].reshape(shard_rows, -1)

    def early_columns(half):
        return jnp.concatenate(
            [
                attn_in_weight[:, half * q_cols : (half + 1) * q_cols],
                attn_in_weight[:, QH * HD + half * HD : QH * HD + (half + 1) * HD],
                attn_in_weight[:, (QH + KVH + half) * HD : (QH + KVH + half + 1) * HD],
                mixer_in_weight[:, half * m_cols : (half + 1) * m_cols],
                mixer_in_weight[:, SH * SHD + half * NS : SH * SHD + (half + 1) * NS],
                step_weight[:, half * M_SHARE : (half + 1) * M_SHARE],
                small,
                jnp.zeros((shard_rows, ms_cols - small_at - small_cols), BF16),
            ],
            axis=1,
        )

    def zgate_columns(half):
        return zgate_weight[:, half * m_cols : (half + 1) * m_cols]

    def late_columns(half):
        return jnp.concatenate([ff_columns(gate_weight, half), ff_columns(up_weight, half)], axis=1)

    def sorted_halves(columns):
        halves = (columns(0), columns(1))
        kept = place.by_core(*halves)
        got = place.swap(place.by_core(halves[1], halves[0]))
        return jnp.concatenate([place.by_core(kept, got), place.by_core(got, kept)], axis=0)

    early = place.spread_z(sorted_halves(early_columns))
    late_one = jnp.concatenate(
        [
            sorted_halves(zgate_columns),
            jnp.concatenate([attn_out_weight, mixer_out_weight], axis=0),
        ],
        axis=1,
    )
    early, late_one = lax.optimization_barrier((early, late_one))
    w_a, w_b = place.gather_plane(
        place.place_z(early, [[(0, a_cols, 2)], [(a_cols, b_cols, 2)]]),
        [(0, 0, a_cols, 0, 0), (1, 0, b_cols, 1, 0)],
    )
    late_one = place.spread_z(late_one)

    tail_at = c_cols - f_cols
    vectors = w_b[:, tail_at + small_at : tail_at + small_at + small_cols]
    vectors = vectors.reshape(devices, -1).astype(F32)
    sizes = [input_gain.shape[0], mixer_gain.shape[0], post_gain.shape[0], conv_bias.shape[0]]
    ends = [sum(sizes[: k + 1]) for k in range(4)]
    gain_in = vectors[:, : ends[0]].reshape(-1)
    gain_mixer = vectors[:, ends[0] : ends[1]].reshape(-1)
    gain_mixer = place.by_core(gain_mixer[:m_cols], gain_mixer[m_cols:])
    gain_post = vectors[:, ends[1] : ends[2]].reshape(-1)
    shift_all = vectors[:, ends[2] : ends[3]].reshape(-1)
    taps_all = vectors[:, ends[3] : vector_size].reshape(devices, KC, sizes[3])
    taps_all = jnp.transpose(taps_all, (1, 0, 2)).reshape(KC, -1)

    def conv_half(value):
        first = jnp.concatenate(
            [value[..., :m_cols], value[..., 2 * m_cols : 2 * m_cols + NS]], axis=-1
        )
        second = jnp.concatenate(
            [value[..., m_cols : 2 * m_cols], value[..., 2 * m_cols + NS :]], axis=-1
        )
        return place.by_core(first, second)

    taps, shift = conv_half(taps_all), conv_half(shift_all)
    terms = vectors[:groups, vector_size : vector_size + 3 * term_size]
    terms = terms.reshape(groups, 3, 3, SH // groups)
    terms = terms[:, 0] + terms[:, 1] + terms[:, 2]
    terms = jnp.transpose(terms, (1, 0, 2)).reshape(3, SH)
    terms = place.by_core(terms[:, :M_SHARE], terms[:, M_SHARE:])
    bias, log_rates, skip = terms[0], terms[1], terms[2]
    rates = -jnp.exp(log_rates)

    scale_in = inverse_rms(tokens)
    normed = (tokens * scale_in * gain_in).astype(BF16).reshape(rows_halo, width)

    def body_rows(value):
        return value.reshape(CORES, slots, piece + HALO, -1)[:, :, HALO:]

    linear = body_rows(mm(normed, w_a[:, :lin_cols]))
    mixed_step = mm(normed, w_b).astype(BF16)
    mixed = jnp.concatenate(
        [mm(normed, w_a[:, lin_cols:]).astype(BF16), mixed_step[:, :tail_at]], axis=-1
    ).reshape(CORES, slots, piece + HALO, c_cols)
    step_raw = body_rows(mixed_step[:, tail_at : tail_at + M_SHARE]).astype(F32)

    late_one, mixed = lax.optimization_barrier((late_one, mixed))
    w_z, w_out = place.gather_plane(
        place.place_z(late_one, [[(0, m_cols, 2)], [(m_cols, width, 1)]]),
        [(0, 0, m_cols, 0, 0), (1, 0, width, 1, 0)],
    )
    late_two = jnp.concatenate([sorted_halves(late_columns), down_weight], axis=1)
    late_two, late_one = lax.optimization_barrier((late_two, late_one))
    late_two = place.spread_z(late_two)
    w_out = w_out.reshape(2, chips // 2, groups, out_rows + mix_rows, width)
    kept = lax.dynamic_index_in_dim(w_out, core, 0, False)
    got = place.swap(lax.dynamic_index_in_dim(w_out, 1 - core, 0, False))
    w_out = jnp.stack([place.by_core(kept, got), place.by_core(got, kept)], 1)
    w_attn_out = w_out[..., :out_rows, :].reshape(q_cols, width)
    w_mixer_out = w_out[..., out_rows:, :].reshape(m_cols, width)
    half = width // 2
    w_gate, w_up, w_down = place.gather_plane(
        place.place_z(
            late_two,
            [
                [(0, ff_half, 2), (2 * ff_half, half, 1)],
                [(ff_half, ff_half, 2), (2 * ff_half + half, half, 1)],
            ],
        ),
        [
            (0, 0, ff_half, 0, 0),
            (1, 0, ff_half, 1, 0),
            (0, ff_half, half, 2, 0),
            (1, ff_half, half, 2, half),
        ],
    )

    cos_part, sin_part = rotary_tables(positions, HD)
    cos_part, sin_part = cos_part[:, None, :, None], sin_part[:, None, :, None]
    queries = rotate(
        linear[..., :q_cols].reshape(CORES, slots, piece, Q_SHARE, HD), cos_part, sin_part
    ).astype(BF16)
    keys = rotate(
        linear[..., q_cols : q_cols + HD][..., None, :], cos_part, sin_part
    ).astype(BF16)[..., 0, :]
    kv_own = jnp.concatenate([keys, linear[..., q_cols + HD :].astype(BF16)], axis=-1)
    kv_parts = [part.reshape(-1, 2 * HD) for part in place.spread_z(kv_own)]
    plan = []
    for r in range(groups):
        for e in range(CORES):
            for s in range(slots):

                def source(at, e=e, s=s):
                    return pl.ds((e * slots + s) * piece, piece), pl.ds(0, 2 * HD)

                def goal(at, r=r, e=e):
                    z = lax.rem(at[2] + groups - r, groups)
                    h = lax.rem(at[3] + e, CORES)
                    return pl.ds((h * groups + z) * piece, piece), pl.ds(0, 2 * HD)

                plan.append((r, source, s, goal))
    kv_size = jax.ShapeDtypeStruct((CORES * groups * piece, 2 * HD), BF16)
    kv = moved(place, kv_parts, [kv_size] * slots, plan)
    kv = place.gather_plane(kv, [(s, 0, 2 * HD, s, 0) for s in range(slots)])

    def by_heads(value, before, after):
        value = jnp.transpose(value, (1, 0, 3, 2, 4)).reshape(slots, CORES, Q_SHARE * piece, HD)
        return jnp.pad(value, ((0, 0), (0, 0), (0, 0), (before, after)))

    def from_heads(value):
        value = value.reshape(slots, CORES, Q_SHARE, piece, HD)
        return jnp.transpose(value, (1, 0, 3, 2, 4))

    scale = HD ** (-0.5)
    queries = by_heads(queries * jnp.asarray(scale, BF16), 0, HD)
    heads_out, lse = zip(
        *[
            attend(pieces_at, lengths[s : s + 1], queries[s : s + 1], kv[s][None], piece)
            for s in range(slots)
        ]
    )
    attended = from_heads(jnp.concatenate(heads_out)[..., HD:]).reshape(rows_all, q_cols)

    pre = shift
    for tap in range(KC):
        first = HALO - KC + 1 + tap
        pre = pre + taps[tap] * mixed[:, :, first : first + piece].astype(F32)
    conv_out, conv_slope = silu_and_slope(pre)
    conv_out = conv_out.astype(BF16)
    features = conv_out[..., :m_cols].reshape(CORES * slots, piece, m_cols)
    shared = conv_out[..., m_cols:]
    shared_other = place.swap(shared)[::-1]
    inject = place.by_core(shared, shared_other).reshape(CORES * slots, piece, NS)
    readout = place.by_core(shared_other, shared).reshape(CORES * slots, piece, NS)
    raw = jnp.pad(step_raw.reshape(CORES * slots, piece, M_SHARE), ((0, 0), (0, 0), (0, LANES - M_SHARE)))
    raw_t = jnp.transpose(raw[..., :16], (0, 2, 1))
    bias_row = jnp.pad(bias, (0, LANES - M_SHARE))[None]
    rate_row = jnp.pad(rates, (0, LANES - M_SHARE))[None]
    bias_col, rate_col = bias_row[0, :16, None], rate_row[0, :16, None]
    skip_row = jnp.repeat(skip, SHD)[None]
    pieces = CORES * slots
    state_flops = 2 * pieces * piece * m_cols * (piece + 2 * NS)
    chunk_args = [
        features, inject, readout, raw, raw_t, bias_row, bias_col, rate_row, rate_col, skip_row,
    ]
    share_rows = m_cols // groups
    held = pltpu.VMEM((groups, share_rows, NS), BF16)
    held_more = pltpu.VMEM((groups, share_rows + EXTRA, NS), BF16)
    within, logs, *local = over_pieces(
        chunk_kernel,
        "chunk",
        chunk_args,
        range(5, 10),
        [
            ((pieces, piece, m_cols), F32),
            ((pieces, piece, LANES), F32),
            *[((pieces, share_rows + EXTRA, NS), BF16)] * groups,
        ],
        state_flops,
        at,
        [held_more],
    )
    local = [part.reshape(CORES, slots, share_rows + EXTRA, NS) for part in local]
    state_in, marks, fades = carried(place, at, local, None, None, False)
    (ssd,) = over_pieces(
        carry_kernel,
        "carry",
        [within, readout, logs, *state_in],
        (),
        [((pieces, piece, m_cols), BF16)],
        2 * pieces * piece * m_cols * NS,
        at,
        [held],
    )
    ssd = ssd.reshape(CORES, slots, piece, m_cols).astype(F32)
    zgate = body_rows(mm(normed, w_z).astype(BF16))
    gate_value, gate_slope = silu_and_slope(zgate.astype(F32))
    gated_raw = ssd * gate_value
    squares = jnp.sum(gated_raw * gated_raw, axis=-1)
    squares = squares + place.swap(squares)[::-1]
    scale_mixer = lax.rsqrt(squares / (SH * SHD) + 1e-05)[..., None]
    gated = (gated_raw * scale_mixer * gain_mixer).astype(BF16).reshape(rows_all, m_cols)

    def own_sum(partial):
        partial = partial.reshape(CORES, -1, partial.shape[-1])
        return partial[0] + place.swap(partial[1].astype(BF16)).astype(F32)

    def with_other(value):
        return jnp.stack([value, place.swap(value)]).reshape(-1, value.shape[-1])

    mixers = own_sum(mm(attended, w_attn_out) + mm(gated, w_mixer_out))
    residual = tokens[0][:, HALO:].reshape(-1, width) + mixers
    scale_post = inverse_rms(residual)
    post = with_other((residual * scale_post * gain_post).astype(BF16))
    gate_lin = mm(post, w_gate)
    up_lin = mm(post, w_up)
    gate_act, gate_act_slope = silu_and_slope(gate_lin)
    hidden = (gate_act * up_lin).astype(BF16)
    valid_own = valid[0].reshape(-1, 1)
    layer_out = (valid_own * (residual + own_sum(mm(hidden, w_down)))).astype(BF16)

    dhidden = mm(dy, w_down, NT)
    dgate = (dhidden * up_lin * gate_act_slope).astype(BF16)
    dup = (dhidden * gate_act).astype(BF16)

    def by_parity(grad):
        return grad.reshape(na, nb, 1, groups, -1, grad.shape[-1])

    def by_columns(grad):
        return grad.reshape(na, nb, CORES, groups, shard_rows, grad.shape[-1])

    ff_grads, ff_finish = place.reduce_far(
        [
            (mm(post, dgate, TN).astype(BF16), 2),
            (mm(post, dup, TN).astype(BF16), 2),
            (mm(hidden, dy, TN).astype(BF16), 1),
        ]
    )
    dpost = own_sum(mm(dgate, w_gate, NT) + mm(dup, w_up, NT))
    dresidual = dy_own.reshape(-1, width) + rms_back(residual, scale_post, gain_post, dpost)
    grad_post_gain = jnp.sum(dpost * residual * scale_post, axis=0)
    dmix = with_other(dresidual.astype(BF16))

    dattended = mm(dmix, w_attn_out, NT).astype(BF16)
    dgated = mm(dmix, w_mixer_out, NT).reshape(CORES, slots, piece, m_cols)
    grad_outs = jnp.concatenate(
        [
            mm(attended, dmix, TN).reshape(chips // 2, CORES, groups, out_rows, width),
            mm(gated, dmix, TN).reshape(chips // 2, CORES, groups, mix_rows, width),
        ],
        axis=3,
    )
    grad_outs = grad_outs.astype(BF16)
    kept = lax.dynamic_index_in_dim(grad_outs, core, 1, False)
    got = place.swap(lax.dynamic_index_in_dim(grad_outs, 1 - core, 1, False))
    grad_outs = jnp.concatenate([place.by_core(kept, got), place.by_core(got, kept)], axis=0)
    scaled = dgated * gain_mixer
    inner = jnp.sum(scaled * gated_raw, axis=-1)
    inner = (inner + place.swap(inner)[::-1])[..., None] / (SH * SHD)
    dgated_raw = scale_mixer * scaled - gated_raw * (scale_mixer**3 * inner)
    grad_mixer_gain = jnp.sum(dgated * gated_raw * scale_mixer, axis=(0, 1, 2))
    dssd = (dgated_raw * gate_value).astype(BF16).reshape(pieces, piece, m_cols)
    dzgate = (dgated_raw * ssd * gate_slope).astype(BF16)

    def halo_rows(value):
        value = value.reshape(CORES, slots, piece, -1)
        return jnp.pad(value, ((0, 0), (0, 0), (HALO, 0), (0, 0)))

    dzgate = halo_rows(dzgate).reshape(rows_halo, m_cols)
    mid_grads, mid_finish = place.reduce_far(
        [
            (grad_outs.reshape(-1, width), 1),
            (mm(normed, dzgate, TN).astype(BF16), 2),
        ]
    )
    dnormed = mm(dzgate, w_z, NT)

    direct = over_pieces(
        direct_kernel,
        "direct",
        [dssd, readout, logs],
        (),
        [((pieces, share_rows, NS), BF16)] * groups,
        2 * pieces * piece * m_cols * NS,
        at,
        [held],
    )
    direct = [part.reshape(CORES, slots, share_rows, NS) for part in direct]
    dattended, direct = lax.optimization_barrier((dattended, direct))
    later, _, _ = carried(place, at, direct, marks, fades, True)

    dout = by_heads(
        dattended.reshape(CORES, slots, piece, Q_SHARE, HD), HD, 0
    )
    dqueries, dkv = zip(
        *[
            attend_back(
                pieces_at,
                lengths[s : s + 1],
                queries[s : s + 1],
                kv[s][None],
                heads_out[s],
                dout[s : s + 1],
                lse[s],
                piece,
            )
            for s in range(slots)
        ]
    )
    dqueries = jnp.concatenate(dqueries)
    dkv_own = place.reduce_chips(
        [dkv[s].reshape(na, nb, CORES, groups, piece, 2 * HD) for s in range(slots)],
        [s % 2 == 0 for s in range(slots)],
    )
    dkv_own = jnp.stack([part.reshape(CORES, piece, 2 * HD) for part in dkv_own], axis=1)
    dkv_own = place.by_core(dkv_own, dkv_own[::-1])

    dfeatures, dinject, dreadout, draw, sums = over_pieces(
        chunk_back_kernel,
        "chunk_back",
        chunk_args + [dssd, *state_in, *later],
        range(5, 10),
        [
            ((pieces, piece, m_cols), F32),
            ((pieces, piece, NS), F32),
            ((pieces, piece, NS), F32),
            ((pieces, piece, LANES), F32),
            ((pieces, 8, LANES), F32),
        ],
        4 * state_flops,
        at,
        [pltpu.VMEM((LANES, 2 * LANES), F32), pltpu.VMEM((piece, LANES), F32), held, held],
    )
    ff_grads, mid_grads, dfeatures = lax.optimization_barrier((ff_grads, mid_grads, dfeatures))
    ff_grads, mid_grads = ff_finish(ff_grads), mid_finish(mid_grads)
    dinject = dinject.reshape(CORES, slots, piece, NS)
    dreadout = dreadout.reshape(CORES, slots, piece, NS)
    dshared = place.by_core(dinject, dreadout) + place.swap(
        place.by_core(dreadout, dinject).astype(BF16)
    )[::-1].astype(F32)
    dconv = jnp.concatenate([dfeatures.reshape(CORES, slots, piece, m_cols), dshared], axis=-1)
    dpre = dconv * conv_slope
    grad_taps = []
    dmixed = jnp.zeros((CORES, slots, piece + HALO, c_cols), F32)
    for tap in range(KC):
        first = HALO - KC + 1 + tap
        seen = mixed[:, :, first : first + piece].astype(F32)
        grad_taps.append(jnp.sum(dpre * seen, axis=(0, 1, 2)))
        dmixed = dmixed + jnp.pad(
            dpre * taps[tap], ((0, 0), (0, 0), (first, KC - 1 - tap), (0, 0))
        )
    grad_shift = jnp.sum(dpre, axis=(0, 1, 2))
    dmixed = dmixed.astype(BF16)

    dstep = draw[..., :M_SHARE].astype(BF16)
    db_low = jnp.concatenate(
        [
            dmixed[..., f_cols:],
            halo_rows(dstep),
            jnp.zeros((CORES, slots, piece + HALO, ms_cols - small_at), BF16),
        ],
        axis=-1,
    ).reshape(rows_halo, b_cols)
    dq_rows = from_heads(dqueries[..., :HD] * scale)
    dq_rows = rotate(dq_rows, cos_part, -sin_part).reshape(CORES, slots, piece, q_cols)
    dk_rows = rotate(dkv_own[..., None, :HD], cos_part, -sin_part)[..., 0, :]
    dlin = jnp.concatenate([dq_rows, dk_rows, dkv_own[..., HD:]], axis=-1).astype(BF16)
    da_low = jnp.concatenate([halo_rows(dlin), dmixed[..., :f_cols]], axis=-1)
    da_low = da_low.reshape(rows_halo, a_cols)
    dnormed = dnormed + mm(da_low, w_a, NT) + mm(db_low, w_b, NT)
    dnormed = own_sum(dnormed).reshape(slots, piece + HALO, width)
    rim_back = lax.ppermute(
        dnormed[:, HALO - KC + 1 : HALO].astype(BF16),
        AXES,
        [(i + 1, i) for i in range(devices - 1)],
    ).astype(F32)
    dnormed = dnormed[:, HALO:] + jnp.pad(rim_back, ((0, 0), (piece - KC + 1, 0), (0, 0)))
    own, own_scale = tokens[0][:, HALO:], scale_in[0][:, HALO:]
    input_grad = dresidual.reshape(slots, piece, width) + rms_back(
        own, own_scale, gain_in, dnormed
    )
    grad_input_gain = jnp.sum(dnormed * own * own_scale, axis=(0, 1))

    zero_half = jnp.zeros((m_cols,), F32)

    def conv_whole(value):
        none = jnp.zeros_like(value)
        first, second = place.by_core(value, none), place.by_core(none, value)
        return jnp.concatenate(
            [first[..., :m_cols], second[..., :m_cols], first[..., m_cols:], second[..., m_cols:]],
            axis=-1,
        )

    grad_mixer_gain = jnp.concatenate(
        [place.by_core(grad_mixer_gain, zero_half), place.by_core(zero_half, grad_mixer_gain)]
    )
    grad_taps = conv_whole(jnp.stack(grad_taps)).reshape(KC, devices, -1)
    vector_grads = jnp.concatenate(
        [
            grad_input_gain.reshape(devices, -1),
            grad_mixer_gain.reshape(devices, -1),
            grad_post_gain.reshape(devices, -1),
            conv_whole(grad_shift).reshape(devices, -1),
            jnp.transpose(grad_taps, (1, 0, 2)).reshape(devices, -1),
        ],
        axis=1,
    )
    vector_grads = jnp.pad(
        vector_grads, ((0, 0), (0, small_cols * shard_rows - vector_size))
    ).reshape(width, small_cols)
    grad_b = mm(normed, db_low, TN)
    grad_b = lax.dynamic_update_slice(grad_b, vector_grads, (0, tail_at + small_at))
    grad_a = mm(normed, da_low, TN)
    head_sums = jnp.sum(sums, axis=0)[:3, :M_SHARE]
    head_sums, grad_a = lax.optimization_barrier((head_sums, grad_a))
    head_sums = place.sum_all(head_sums)
    other_sums = place.swap(head_sums)
    head_sums = jnp.concatenate(
        [place.by_core(head_sums, other_sums), place.by_core(other_sums, head_sums)], axis=1
    )
    head_sums = lax.dynamic_slice_in_dim(head_sums, place.at["z"] * (SH // groups), SH // groups, 1)

    grad_a, grad_b = place.reduce_chips(
        [by_columns(grad_a), by_columns(grad_b)], [True, False]
    )

    def between_cores(columns):
        columns = columns.reshape(CORES, shard_rows, -1)
        kept = lax.dynamic_index_in_dim(columns, core, 0, False)
        got = place.swap(lax.dynamic_index_in_dim(columns, 1 - core, 0, False))
        return place.by_core(kept, got), place.by_core(got, kept)

    def ff_whole(pair):
        parts = [half.reshape(shard_rows, chips, 1, -1) for half in pair]
        return jnp.concatenate(parts, axis=2).reshape(shard_rows, -1)

    ff_rows_each = ff_grads.shape[0] // 3
    both = between_cores(
        jnp.concatenate([ff_grads[:ff_rows_each], ff_grads[ff_rows_each : 2 * ff_rows_each]], axis=1)
    )
    grad_gate = ff_whole([half[:, :ff_half] for half in both]).astype(F32)
    grad_up = ff_whole([half[:, ff_half:] for half in both]).astype(F32)
    grad_down = ff_grads[2 * ff_rows_each :].astype(F32)
    grad_outs = mid_grads[:, :width].astype(F32)
    grad_zgate = jnp.concatenate(between_cores(mid_grads[:, width:]), axis=1).astype(F32)
    first, second = between_cores(jnp.concatenate([grad_a, grad_b], axis=1))

    def both_halves(start, size):
        return jnp.concatenate([first[:, start : start + size], second[:, start : start + size]], 1)

    grad_attn_in = jnp.concatenate(
        [both_halves(0, q_cols), both_halves(q_cols, HD), both_halves(q_cols + HD, HD)], axis=1
    )
    grad_mixer_in = jnp.concatenate(
        [both_halves(lin_cols, m_cols), both_halves(lin_cols + m_cols, NS)], axis=1
    )
    grad_step = both_halves(lin_cols + c_cols, M_SHARE)
    small_at = lin_cols + c_cols + small_at
    small_sum = (first + second)[:, small_at : small_at + small_cols].reshape(-1)

    return (
        layer_out.reshape(slots, piece, width),
        input_grad,
        small_sum[: ends[0]],
        grad_attn_in,
        grad_outs[:out_rows],
        grad_zgate,
        grad_mixer_in,
        grad_step,
        small_sum[ends[3] : vector_size].reshape(KC, -1),
        small_sum[ends[2] : ends[3]],
        head_sums[0],
        head_sums[1],
        head_sums[2],
        small_sum[ends[0] : ends[1]],
        grad_outs[out_rows:],
        small_sum[ends[1] : ends[2]],
        grad_gate,
        grad_up,
        grad_down,
    )


def solution(mesh):
    rows, columns, vector = P(AXES, None), P(None, AXES), P(AXES)
    tokens, heads = P(None, AXES, None), P("sp")
    in_specs = (
        tokens,
        tokens,
        P(),
        vector,
        rows,
        rows,
        rows,
        rows,
        rows,
        columns,
        vector,
        heads,
        heads,
        heads,
        vector,
        rows,
        vector,
        rows,
        rows,
        rows,
    )
    out_specs = (
        tokens,
        tokens,
        vector,
        rows,
        rows,
        rows,
        rows,
        rows,
        columns,
        vector,
        heads,
        heads,
        heads,
        vector,
        rows,
        vector,
        rows,
        rows,
        rows,
    )
    return jax.shard_map(shards, mesh=mesh, in_specs=in_specs, out_specs=out_specs, check_vma=False)
```

```python
import functools
import math

import jax
import jax.numpy as jnp
from jax import lax
from jax.experimental import pallas as pl
from jax.experimental.pallas import tpu as pltpu
from jax.sharding import PartitionSpec as P

QH = 8
KVH = 2
HD = 64
SH = 24
SHD = 64
NS = 128
KC = 4
CORES = 2
MASKED = -1e30
AXES = ("ctx", "sp")
F32 = jnp.float32
BF16 = jnp.bfloat16
LANES = 128
HALO = 8
EXTRA = 16
Q_SHARE = QH // CORES
M_SHARE = SH // CORES
VMEM = 56 * 2**20

NT = (((1,), (1,)), ((), ()))
TN = (((0,), (0,)), ((), ()))
NN = (((1,), (0,)), ((), ()))


def mm(left, right, dims=NN, precision=None):
    return lax.dot_general(
        left, right, dims, precision=precision, preferred_element_type=F32
    )


def tie(*values):
    return lax.optimization_barrier(values)


def cost(micros):
    return pl.CostEstimate(flops=int(micros * 1.15e9), bytes_accessed=0, transcendentals=0)


class Place:
    def __init__(self):
        ctx = lax.axis_size("ctx")
        groups = lax.axis_size("sp")
        chips = ctx // CORES
        nb = math.isqrt(chips)
        self.size = {"a": chips // nb, "b": nb, "z": groups, "c": CORES}
        self.devices = ctx * groups
        index = lax.axis_index("ctx")
        self.at = {
            "a": index // CORES // nb,
            "b": (index // CORES) % nb,
            "z": lax.axis_index("sp"),
            "c": index % CORES,
        }
        self.chip = index // CORES
        self.chips = chips
        self.scalars = jnp.stack(
            [self.at["a"], self.at["b"], self.at["z"], self.at["c"], self.chip]
        ).astype(jnp.int32)
        self.flat = index * groups + self.at["z"]

    def flat_of(self, a, b, z, c):
        return ((a * self.size["b"] + b) * CORES + c) * self.size["z"] + z

    def pairs(self, dim, by):
        found = []
        for a in range(self.size["a"]):
            for b in range(self.size["b"]):
                for z in range(self.size["z"]):
                    for c in range(CORES):
                        spot = {"a": a, "b": b, "z": z, "c": c}
                        goal = dict(spot)
                        goal[dim] = (spot[dim] + by) % self.size[dim]
                        found.append((self.flat_of(**spot), self.flat_of(**goal)))
        return found

    def shift(self, x, dim, by):
        return lax.ppermute(x, AXES, self.pairs(dim, by))

    def swap(self, x):
        return self.shift(x, "c", 1)

    def by_core(self, zero, one):
        return jnp.where(self.at["c"] == 0, zero, one)

    def chip_pairs(self, by):
        groups = self.size["z"]
        return [
            ((chip * CORES + c) * groups + z, (((chip + by) % self.chips) * CORES + c) * groups + z)
            for chip in range(self.chips)
            for c in range(CORES)
            for z in range(groups)
        ]

    def spread_z(self, x):
        return [x] + [self.shift(x, "z", k) for k in range(1, self.size["z"])]

    def plane_first(self, halves):
        found = []
        for index, half in enumerate(halves):
            dim = "ab"[index % 2 == 0]
            found.append([half] + [self.shift(half, dim, k) for k in range(1, self.size[dim])])
        return found

    def plane_second(self, halves):
        found = []
        for index, parts in enumerate(halves):
            dim = "ba"[index % 2 == 0]
            moves = range(1, self.size[dim])
            found.append([parts] + [[self.shift(part, dim, k) for part in parts] for k in moves])
        return found

    def place_z(self, parts, halves):
        groups = self.size["z"]
        rows = parts[0].shape[0]
        outs = [
            jax.ShapeDtypeStruct((groups * rows, sum(size for _, size, _ in half)), parts[0].dtype)
            for half in halves
        ]
        plan = []
        for index, half in enumerate(halves):
            to = 0
            for start, size, count in half:
                block = rows // count
                for r in range(groups):
                    for m in range(count):

                        def source(at, m=m, start=start, size=size, block=block):
                            return pl.ds(m * block, block), pl.ds(start, size)

                        def goal(at, m=m, r=r, to=to, size=size, block=block):
                            z = lax.rem(at[2] + groups - r, groups)
                            return pl.ds((m * groups + z) * block, block), pl.ds(to, size)

                        plan.append((r, source, index, goal))
                to += size
        return moved(self, parts, outs, plan)

    def plane_third(self, halves, wanted):
        rows, dtype = halves[0][0][0].shape[0], halves[0][0][0].dtype
        na, nb = self.size["a"], self.size["b"]
        keys = [(da, db) for da in range(na) for db in range(nb)]
        widths = {}
        for _, _, size, array, column in wanted:
            widths[array] = max(widths.get(array, 0), column + size)
        outs = [
            jax.ShapeDtypeStruct((self.chips * rows, widths[k]), dtype) for k in range(len(widths))
        ]
        sources = []
        for index, half in enumerate(halves):
            sources += [half[da][db] if index % 2 == 0 else half[db][da] for da, db in keys]
        plan = []
        for half, start, size, array, column in wanted:
            for index, (da, db) in enumerate(keys):

                def source(at, start=start, size=size):
                    return pl.ds(0, rows), pl.ds(start, size)

                def goal(at, da=da, db=db, column=column, size=size):
                    chip = lax.rem(at[0] + na - da, na) * nb + lax.rem(at[1] + nb - db, nb)
                    return pl.ds(chip * rows, rows), pl.ds(column, size)

                plan.append((half * len(keys) + index, source, array, goal))
        return moved(self, sources, outs, plan)

    def reduce_far(self, grads):
        cores = [[chip * CORES + c for chip in range(self.chips)] for c in range(CORES)]
        groups, chips = self.size["z"], self.chips
        rows = grads[0][0].shape[0] // chips
        widths = [grad.shape[1] for grad, _ in grads]
        stacked = len(set(widths)) == 1
        high = len(grads) * rows if stacked else rows
        wide = widths[0] if stacked else sum(widths)
        corner = [
            (k * rows, 0) if stacked else (0, sum(widths[:k])) for k in range(len(grads))
        ]
        outs = [jax.ShapeDtypeStruct((chips * high, wide), BF16)]
        plan = []
        for k, (row, column) in enumerate(corner):
            for chip in range(chips):

                def source(at, chip=chip, size=widths[k]):
                    return pl.ds(chip * rows, rows), pl.ds(0, size)

                def goal(at, chip=chip, row=row, column=column, size=widths[k]):
                    return pl.ds(chip * high + row, rows), pl.ds(column, size)

                plan.append((k, source, 0, goal))
        (flat,) = moved(self, [grad for grad, _ in grads], outs, plan)

        def start(flat):
            return lax.psum_scatter(
                flat, "ctx", scatter_dimension=0, tiled=True, axis_index_groups=cores
            )

        share, deep = rows // groups, high // groups

        def finish(flat):
            plan = []
            for k, (row, column) in enumerate(corner):
                count = grads[k][1]
                block = share // count
                for z in range(groups):
                    for m in range(count):

                        def source(at, z=z, m=m, row=row, column=column, size=widths[k], block=block):
                            return (
                                pl.ds(row + (m * groups + z) * block, block),
                                pl.ds(column, size),
                            )

                        def goal(
                            at, z=z, m=m, row=row, column=column, size=widths[k], block=block
                        ):
                            return (
                                pl.ds(z * deep + row // groups + m * block, block),
                                pl.ds(column, size),
                            )

                        plan.append((0, source, 0, goal))
            outs = [jax.ShapeDtypeStruct((high, wide), BF16)]
            (flat,) = moved(self, [flat], outs, plan)
            return lax.psum_scatter(flat, "sp", scatter_dimension=0, tiled=True)

        return flat, start, finish

    def reduce(self, x, dim, axis):
        n, v = self.size[dim], self.at[dim]
        total = lax.dynamic_index_in_dim(x, v, axis, False).astype(F32)
        for k in range(1, n):
            piece = lax.dynamic_index_in_dim(x, (v + k) % n, axis, False).astype(BF16)
            total = total + self.shift(piece, dim, k).astype(F32)
        return total

    def reduce_first(self, grad, b_first):
        return self.reduce(grad, "a", 0) if b_first else self.reduce(grad, "b", 1)

    def reduce_second(self, grad, b_first):
        return self.reduce(grad, "b" if b_first else "a", 0)

    def reduce_z(self, left):
        n, v = self.size["z"], self.at["z"]

        def cut(x, index):
            piece = lax.dynamic_index_in_dim(x, index, 1, False)
            return piece.reshape(-1, piece.shape[-1])

        totals = [cut(x, v) for x in left]
        for k in range(1, n):
            sent = jnp.concatenate([cut(x, (v + k) % n).astype(BF16) for x in left], axis=-1)
            got = self.shift(sent, "z", k).astype(F32)
            start = 0
            for index, total in enumerate(totals):
                stop = start + total.shape[-1]
                totals[index] = total + got[:, start:stop]
                start = stop
        return totals

    def sum_step(self, x, dim, step):
        found = []
        for a in range(self.size["a"]):
            for b in range(self.size["b"]):
                for z in range(self.size["z"]):
                    for c in range(CORES):
                        spot = {"a": a, "b": b, "z": z, "c": c}
                        goal = dict(spot)
                        goal[dim] = spot[dim] ^ step
                        found.append((self.flat_of(**spot), self.flat_of(**goal)))
        return x + lax.ppermute(x, AXES, found)

    def sum_along(self, x, dims):
        for dim in dims:
            step = 1
            while step < self.size[dim]:
                x = self.sum_step(x, dim, step)
                step *= 2
        return x


def moved_kernel(at_ref, *refs, plan, count):
    sems = refs[-1]
    copies = [
        pltpu.make_async_copy(
            refs[source].at[where(at_ref)], refs[count + goal].at[to(at_ref)], sems.at[index]
        )
        for index, (source, where, goal, to) in enumerate(plan)
    ]
    for copy in copies:
        copy.start()
    for copy in copies:
        copy.wait()


def moved(place, sources, outs, plan):
    size = sum(math.prod(out.shape) * out.dtype.itemsize for out in outs)
    return pl.pallas_call(
        functools.partial(moved_kernel, plan=plan, count=len(sources)),
        in_specs=[pl.BlockSpec(memory_space=pltpu.SMEM)]
        + [pl.BlockSpec(memory_space=pl.ANY)] * len(sources),
        out_specs=[pl.BlockSpec(memory_space=pltpu.VMEM)] * len(outs),
        out_shape=outs,
        scratch_shapes=[pltpu.SemaphoreType.DMA((len(plan),))],
        compiler_params=pltpu.CompilerParams(vmem_limit_bytes=VMEM),
        cost_estimate=pl.CostEstimate(flops=0, bytes_accessed=2 * size, transcendentals=0),
        name="moved",
    )(place.scalars, *sources)


def rotary_tables(positions, width):
    half_width = width // 2
    inverse = 100000000000.0 ** (-jnp.arange(half_width, dtype=F32) * 2.0 / width)
    angles = positions.astype(F32)[..., None] * inverse
    return (jnp.cos(angles), jnp.sin(angles))


def rotate(value, cos_part, sin_part):
    half_width = value.shape[-1] // 2
    first = value[..., :half_width]
    second = value[..., half_width:]
    return jnp.concatenate(
        [first * cos_part - second * sin_part, second * cos_part + first * sin_part], axis=-1
    )


def inverse_rms(value):
    return lax.rsqrt(jnp.mean(value * value, axis=-1, keepdims=True) + 1e-05)


def rms_back(value, scale, gain, grad):
    scaled = grad * gain
    inner = jnp.mean(scaled * value, axis=-1, keepdims=True)
    return scale * scaled - value * (scale * scale * scale * inner)


def silu_and_slope(value):
    gate = jax.nn.sigmoid(value)
    out = value * gate
    return out, gate + out * (1.0 - gate)


def causal_keep(first_key, first_query, keys, piece, columns):
    key = first_key + lax.broadcasted_iota(jnp.int32, (keys, columns), 0)
    column = lax.broadcasted_iota(jnp.int32, (keys, columns), 1)
    head = sum((column >= piece * k).astype(jnp.int32) for k in range(1, columns // piece))
    return key <= first_query + column - head * piece


def attend_kernel(places, lengths, q_ref, kv_ref, out_ref, lse_ref, acc, top, total, *, piece):
    slot, which = pl.program_id(0), pl.program_id(1)
    first_query = places[which]
    columns = q_ref.shape[2]
    block = columns
    out_ref[...] = jnp.zeros_like(out_ref)
    lse_ref[...] = jnp.zeros_like(lse_ref)

    @pl.when(first_query < lengths[slot])
    def _():
        acc[...] = jnp.zeros_like(acc)
        top[...] = jnp.full_like(top, MASKED)
        total[...] = jnp.zeros_like(total)
        whole = first_query // block

        def visit(index, masked):
            start = pl.multiple_of(index * block, block)
            kv = kv_ref[0, pl.ds(start, block), :]
            scores = mm(kv, q_ref[0, 0], NT)
            if masked:
                keep = causal_keep(start, first_query, block, piece, columns)
                scores = jnp.where(keep, scores, MASKED)
            before = top[...]
            now = jnp.maximum(before, jnp.max(scores, axis=0, keepdims=True))
            weights = jnp.exp(scores - now)
            ratio = jnp.exp(before - now)
            total[...] = total[...] * ratio + jnp.sum(weights, axis=0, keepdims=True)
            acc[...] = acc[...] * ratio + mm(kv, weights.astype(BF16), TN)
            top[...] = now

        @pl.loop(0, whole)
        def _(index):
            visit(index, False)

        visit(whole, True)
        out_ref[0, 0] = (acc[...] / total[...]).T.astype(BF16)
        lse_ref[0, 0] = top[...] + jnp.log(total[...])


def attend(places, lengths, queries, kv, piece):
    slots, _, columns, width = queries.shape
    length = kv.shape[1]
    return pl.pallas_call(
        functools.partial(attend_kernel, piece=piece),
        grid_spec=pltpu.PrefetchScalarGridSpec(
            num_scalar_prefetch=2,
            grid=(slots, CORES),
            in_specs=[
                pl.BlockSpec((1, 1, columns, width), lambda s, e, *_: (s, e, 0, 0)),
                pl.BlockSpec((1, length, width), lambda s, e, *_: (s, 0, 0)),
            ],
            out_specs=[
                pl.BlockSpec((1, 1, columns, width), lambda s, e, *_: (s, e, 0, 0)),
                pl.BlockSpec((1, 1, 1, columns), lambda s, e, *_: (s, e, 0, 0)),
            ],
            scratch_shapes=[
                pltpu.VMEM((width, columns), F32),
                pltpu.VMEM((1, columns), F32),
                pltpu.VMEM((1, columns), F32),
            ],
        ),
        out_shape=[
            jax.ShapeDtypeStruct(queries.shape, BF16),
            jax.ShapeDtypeStruct((slots, CORES, 1, columns), F32),
        ],
        compiler_params=pltpu.CompilerParams(vmem_limit_bytes=VMEM),
        cost_estimate=cost(20),
        name="attend",
    )(places, lengths, queries, kv)


def attend_back_kernel(
    places, lengths, q_ref, kv_ref, out_ref, dout_ref, lse_ref, dq_ref, dkv_ref, dkv, dq, *, piece
):
    slot, which = pl.program_id(0), pl.program_id(1)
    first_query = places[which]
    columns = q_ref.shape[2]
    block = columns
    dq_ref[...] = jnp.zeros_like(dq_ref)

    @pl.when(which == 0)
    def _():
        dkv[...] = jnp.zeros_like(dkv)

    @pl.when(first_query < lengths[slot])
    def _():
        dq[...] = jnp.zeros_like(dq)
        queries = q_ref[0, 0]
        dout = dout_ref[0, 0]
        both = dout.astype(F32) * out_ref[0, 0].astype(F32)
        delta = mm(jnp.ones((8, both.shape[1]), F32), both, NT, lax.Precision.HIGHEST)[:1]
        lse = lse_ref[0, 0]
        whole = first_query // block

        def visit(index, masked):
            start = pl.multiple_of(index * block, block)
            kv = kv_ref[0, pl.ds(start, block), :]
            scores = mm(kv, queries, NT)
            if masked:
                keep = causal_keep(start, first_query, block, piece, columns)
                scores = jnp.where(keep, scores, MASKED)
            probs = jnp.exp(scores - lse)
            dprobs = mm(kv, dout, NT)
            dscores = (probs * (dprobs - delta)).astype(BF16)
            probs = probs.astype(BF16)
            dkv[pl.ds(start, block), :] += mm(dscores, queries) + mm(probs, dout)
            dq[...] += mm(kv, dscores, TN)

        @pl.loop(0, whole)
        def _(index):
            visit(index, False)

        visit(whole, True)
        dq_ref[0, 0] = dq[...].T.astype(dq_ref.dtype)

    @pl.when(which == CORES - 1)
    def _():
        dkv_ref[0] = dkv[...].astype(dkv_ref.dtype)


def attend_back(places, lengths, queries, kv, out, dout, lse, piece):
    slots, _, columns, width = queries.shape
    length = kv.shape[1]
    rows = pl.BlockSpec((1, 1, columns, width), lambda s, e, *_: (s, e, 0, 0))
    keys = pl.BlockSpec((1, length, width), lambda s, e, *_: (s, 0, 0))
    return pl.pallas_call(
        functools.partial(attend_back_kernel, piece=piece),
        grid_spec=pltpu.PrefetchScalarGridSpec(
            num_scalar_prefetch=2,
            grid=(slots, CORES),
            in_specs=[
                rows,
                keys,
                rows,
                rows,
                pl.BlockSpec((1, 1, 1, columns), lambda s, e, *_: (s, e, 0, 0)),
            ],
            out_specs=[rows, keys],
            scratch_shapes=[pltpu.VMEM((length, width), F32), pltpu.VMEM((width, columns), F32)],
        ),
        out_shape=[
            jax.ShapeDtypeStruct(queries.shape, F32),
            jax.ShapeDtypeStruct(kv.shape, BF16),
        ],
        compiler_params=pltpu.CompilerParams(vmem_limit_bytes=VMEM),
        cost_estimate=cost(25),
        name="attend_back",
    )(places, lengths, queries, kv, out, dout, lse)


def lower(rows, transposed=False):
    row = lax.broadcasted_iota(jnp.int32, (rows, rows), 0)
    column = lax.broadcasted_iota(jnp.int32, (rows, rows), 1)
    return row <= column if transposed else row >= column


def paired(first, second, shape):
    lane = lax.broadcasted_iota(jnp.int32, shape, 1)
    return jnp.where(lane < SHD, first, second)


def chunk_terms(raw_ref, raw_t_ref, bias_ref, bias_t_ref, rate_ref, rate_t_ref):
    rows = raw_ref.shape[1]
    steps = jax.nn.softplus(raw_ref[0] + bias_ref[...])
    steps_t = jax.nn.softplus(raw_t_ref[0] + bias_t_ref[...])
    high = lax.Precision.HIGHEST
    logs = mm(lower(rows).astype(F32), steps * rate_ref[...], NN, high)
    logs_t = mm(steps_t * rate_t_ref[...], lower(rows, True).astype(F32), NN, high)
    return steps, steps_t, logs, logs_t


def chunk_kernel(
    f_ref, b_ref, c_ref, raw_ref, raw_t_ref, bias_ref, bias_t_ref, rate_ref, rate_t_ref, skip_ref,
    at_ref, out_ref, logs_ref, *rest,
):
    state_refs, held = rest[:-1], rest[-1]
    steps, steps_t, logs, logs_t = chunk_terms(
        raw_ref, raw_t_ref, bias_ref, bias_t_ref, rate_ref, rate_t_ref
    )
    logs_ref[0] = logs
    rows = logs.shape[0]
    inject = b_ref[0]
    mix = jnp.where(lower(rows), mm(c_ref[0], inject, NT), 0.0)
    tail = jnp.exp(logs[rows - 1 :] - logs) * steps
    for pair in range(M_SHARE // 2):
        lanes = slice(pair * LANES, (pair + 1) * LANES)
        feats = f_ref[0, :, lanes]
        outs = []
        for head in (2 * pair, 2 * pair + 1):
            gap = jnp.minimum(logs[:, head : head + 1] - logs_t[head : head + 1, :], 0.0)
            kernel = mix * jnp.exp(gap) * steps_t[head : head + 1, :]
            outs.append(mm(kernel.astype(BF16), feats))
        wide = feats.astype(F32)
        out_ref[0, :, lanes] = paired(outs[0], outs[1], wide.shape) + skip_ref[:, lanes] * wide
        weight = paired(
            tail[:, 2 * pair : 2 * pair + 1], tail[:, 2 * pair + 1 : 2 * pair + 2], wide.shape
        )
        state = mm((wide * weight).astype(BF16), inject, TN).astype(BF16)
        keep_heads(held, state, pair)
    decay = jnp.exp(logs[rows - 1 :])
    line = lax.broadcasted_iota(jnp.int32, (EXTRA, LANES), 0)
    high = decay.astype(BF16).astype(F32)
    extra = jnp.where(line == 0, high, jnp.where(line == 1, decay - high, 0.0)).astype(BF16)
    for group in range(len(state_refs)):
        held[group, held.shape[1] - EXTRA :, :] = extra
    send_groups(held, state_refs, at_ref)


def carry_kernel(out_ref, c_ref, logs_ref, *rest):
    groups = len(rest) - 3
    at_ref, ssd_ref, held = rest[groups], rest[groups + 1], rest[groups + 2]
    take_groups(held, rest[:groups], at_ref)
    decay = jnp.exp(logs_ref[0])
    for pair in range(M_SHARE // 2):
        lanes = slice(pair * LANES, (pair + 1) * LANES)
        read = mm(c_ref[0], pair_rows(held, pair), NT)
        weight = paired(
            decay[:, 2 * pair : 2 * pair + 1], decay[:, 2 * pair + 1 : 2 * pair + 2], read.shape
        )
        ssd_ref[0, :, lanes] = (out_ref[0, :, lanes] + read * weight).astype(BF16)


def direct_kernel(d_ref, c_ref, logs_ref, at_ref, *rest):
    held = rest[-1]
    decay = jnp.exp(logs_ref[0])
    for pair in range(M_SHARE // 2):
        lanes = slice(pair * LANES, (pair + 1) * LANES)
        grad = d_ref[0, :, lanes].astype(F32)
        weight = paired(
            decay[:, 2 * pair : 2 * pair + 1], decay[:, 2 * pair + 1 : 2 * pair + 2], grad.shape
        )
        state = mm((grad * weight).astype(BF16), c_ref[0], TN).astype(BF16)
        keep_heads(held, state, pair)
    send_groups(held, rest[:-1], at_ref)


def chunk_back_kernel(
    f_ref, b_ref, c_ref, raw_ref, raw_t_ref, bias_ref, bias_t_ref, rate_ref, rate_t_ref, skip_ref,
    d_ref, *rest,
):
    groups = (len(rest) - 10) // 2
    at_ref = rest[2 * groups]
    df_ref, db_ref, dc_ref, draw_ref, sums_ref = rest[2 * groups + 1 : 2 * groups + 6]
    columns, row_sums, states, laters = rest[2 * groups + 6 :]
    take_groups(states, rest[:groups], at_ref)
    take_groups(laters, rest[groups : 2 * groups], at_ref)
    steps, steps_t, logs, logs_t = chunk_terms(
        raw_ref, raw_t_ref, bias_ref, bias_t_ref, rate_ref, rate_t_ref
    )
    rows = logs.shape[0]
    inject, readout = b_ref[0], c_ref[0]
    keep = lower(rows)
    mix = jnp.where(keep, mm(readout, inject, NT), 0.0)
    columns[...] = jnp.zeros_like(columns)
    row_sums[...] = jnp.zeros_like(row_sums)
    decay = jnp.exp(logs)
    end_decay = jnp.exp(logs[rows - 1 :] - logs)
    tail = end_decay * steps
    dmix = jnp.zeros((rows, rows), F32)
    db = jnp.zeros((rows, NS), F32)
    dc = jnp.zeros((rows, NS), F32)
    to_state = jnp.zeros((rows, LANES), F32)
    from_state = jnp.zeros((rows, LANES), F32)
    skips = jnp.zeros((1, LANES), F32)
    agree = jnp.zeros((1, LANES), F32)
    head_lane = lax.broadcasted_iota(jnp.int32, (rows, LANES), 1)
    for pair in range(M_SHARE // 2):
        lanes = slice(pair * LANES, (pair + 1) * LANES)
        feats, grad = f_ref[0, :, lanes], d_ref[0, :, lanes]
        wide, wide_grad = feats.astype(F32), grad.astype(F32)
        later = pair_rows(laters, pair)
        state = pair_rows(states, pair)
        agreed = later.astype(F32) * state.astype(F32)
        pushed = mm(inject, later, NT)
        read = mm(readout, state, NT)
        push_part = wide * pushed
        read_part = wide_grad * read
        skip_part = wide * wide_grad
        grads = []
        for half, head in enumerate((2 * pair, 2 * pair + 1)):
            column = slice(head, head + 1)
            lane = lax.broadcasted_iota(jnp.int32, wide.shape, 1)
            mine = (lane < SHD) if half == 0 else (lane >= SHD)
            step_row = steps_t[column, :]
            gap = jnp.minimum(logs[:, column] - logs_t[column, :], 0.0)
            fade = jnp.exp(gap)
            dkernel = mm(jnp.where(mine, wide_grad, 0.0).astype(BF16), feats, NT)
            faded = dkernel * fade
            stepped = faded * step_row
            dmix = dmix + stepped
            kernel = mix * fade * step_row
            columns[column, 0:rows] = jnp.sum(faded * mix, axis=0, keepdims=True)
            here = head_lane == head
            row_sums[...] += jnp.where(here, jnp.sum(stepped * mix, axis=1, keepdims=True), 0.0)
            grads.append(mm(kernel.astype(BF16), grad, TN))
            to_state = to_state + jnp.where(
                here, jnp.sum(jnp.where(mine, push_part, 0.0), axis=1, keepdims=True), 0.0
            )
            from_state = from_state + jnp.where(
                here, jnp.sum(jnp.where(mine, read_part, 0.0), axis=1, keepdims=True), 0.0
            )
            same = agreed[half * SHD : (half + 1) * SHD]
            same = jnp.sum(jnp.sum(same, axis=0, keepdims=True), axis=1, keepdims=True)
            agree = agree + jnp.where(here[:1], same, 0.0)
            skips = skips + jnp.where(
                here[:1],
                jnp.sum(
                    jnp.sum(jnp.where(mine, skip_part, 0.0), axis=1, keepdims=True),
                    axis=0,
                    keepdims=True,
                ),
                0.0,
            )
        first, second = slice(2 * pair, 2 * pair + 1), slice(2 * pair + 1, 2 * pair + 2)
        weight = paired(tail[:, first], tail[:, second], wide.shape)
        df_ref[0, :, lanes] = (
            paired(grads[0], grads[1], wide.shape) + skip_ref[:, lanes] * wide_grad + weight * pushed
        )
        db = db + mm((wide * weight).astype(BF16), later)
        seen = paired(decay[:, first], decay[:, second], wide.shape)
        dc = dc + mm((wide_grad * seen).astype(BF16), state)
    low = dmix * jnp.where(keep, 1.0, 0.0)
    low = low.astype(BF16)
    db_ref[0] = db + mm(low, readout, TN)
    dc_ref[0] = dc + mm(low, inject)
    direct = columns[...].T[:rows]
    push = end_decay * to_state
    dlogs = row_sums[...] - steps * direct + decay * from_state - steps * push
    end = jnp.sum(steps * push, axis=0, keepdims=True) + decay[rows - 1 :] * agree
    last = lax.broadcasted_iota(jnp.int32, (rows, LANES), 0) == rows - 1
    dlogs = dlogs + jnp.where(last, end, 0.0)
    summed = mm(lower(rows, True).astype(F32), dlogs, NN, lax.Precision.HIGHEST)
    dsteps = direct + push + summed * rate_ref[...]
    draw = dsteps * jax.nn.sigmoid(raw_ref[0] + bias_ref[...])
    draw_ref[0] = draw
    line = lax.broadcasted_iota(jnp.int32, (8, LANES), 0)
    dbias = jnp.sum(draw, axis=0, keepdims=True)
    dlog = jnp.sum(summed * steps, axis=0, keepdims=True) * rate_ref[...]
    sums_ref[0] = jnp.where(
        line == 0, dbias, jnp.where(line == 1, dlog, jnp.where(line == 2, skips, 0.0))
    )


def over_pieces(kernel, name, args, whole, outs, micros, at, scratch=()):
    pieces = args[0].shape[0]

    def spec(shape, split):
        if split:
            return pl.BlockSpec((1,) + shape[1:], lambda i: (i,) + (0,) * (len(shape) - 1))
        return pl.BlockSpec(shape, lambda i: (0,) * len(shape))

    shapes = [(arg.shape, index not in whole) for index, arg in enumerate(args)]
    return pl.pallas_call(
        kernel,
        grid=(pieces,),
        in_specs=[spec(shape, split) for shape, split in shapes]
        + [pl.BlockSpec(memory_space=pltpu.SMEM)],
        out_specs=[spec(shape, True) for shape, _ in outs],
        out_shape=[jax.ShapeDtypeStruct(shape, dtype) for shape, dtype in outs],
        scratch_shapes=list(scratch),
        compiler_params=pltpu.CompilerParams(vmem_limit_bytes=VMEM),
        cost_estimate=cost(micros),
        name=name,
    )(*args, at)


def keep_heads(held, state, pair):
    share = M_SHARE // held.shape[0]
    for half in range(2):
        group, spot = divmod(2 * pair + half, share)
        held[group, spot * SHD : (spot + 1) * SHD, :] = state[half * SHD : (half + 1) * SHD]


def pair_rows(held, pair):
    share = M_SHARE // held.shape[0]
    found = []
    for half in range(2):
        group, spot = divmod(2 * pair + half, share)
        found.append(held[group, spot * SHD : (spot + 1) * SHD, :])
    return jnp.concatenate(found, axis=0)


def send_groups(held, refs, at_ref):
    for r, ref in enumerate(refs):
        ref[0] = held[lax.rem(at_ref[2] + r, len(refs))]


def take_groups(held, refs, at_ref):
    for r, ref in enumerate(refs):
        held[lax.rem(at_ref[2] + len(refs) - r, len(refs))] = ref[0]


def scan_kernel(at_ref, *refs, groups, chips, share, reverse, last):
    rows = share * SHD
    states, marks = refs[:groups], refs[groups : 2 * groups]
    refs = refs[2 * groups :]
    chip, z, core = at_ref[4], at_ref[2], at_ref[3]
    lane = lax.broadcasted_iota(jnp.int32, (1, LANES), 1)

    def pick(pair, offset):
        both = pair[0:1].astype(F32) + pair[1:2].astype(F32)
        return [
            jnp.sum(jnp.where(lane == offset + i, both, 0.0), axis=1, keepdims=True)
            for i in range(share)
        ]

    def step(run, factors, new):
        return jnp.concatenate(
            [
                factors[i] * run[i * SHD : (i + 1) * SHD] + new[i * SHD : (i + 1) * SHD]
                for i in range(share)
            ],
            axis=0,
        )

    if last:
        totals, fades = refs[: chips - 1], refs[chips - 1 : 2 * chips - 2]
        outs, held, decay, entered = (
            refs[2 * chips - 2 : 2 * chips - 2 + groups],
            refs[-3],
            refs[-2],
            refs[-1],
        )
    else:
        total_ref, held, decay = refs
    for r in range(groups):
        to = lax.rem(z + groups - r, groups)
        held[to] = states[r][:, 0, :rows]
        decay[to] = marks[r][:, 0]
    run = jnp.zeros((rows, NS), F32)
    if last:
        for k in range(chips - 1, 0, -1):
            part = chips - k if reverse else k
            reached = chip + k < chips if reverse else chip >= k
            new = step(run, pick(fades[part - 1][0], 0), totals[part - 1][0, :rows].astype(F32))
            run = jnp.where(reached, new, run)
    fade = [jnp.ones((1, 1), F32)] * share
    order = [(h, k) for h in range(CORES) for k in range(groups)]
    for h, k in order[::-1] if reverse else order:
        e = lax.rem(h + core, CORES)
        if last:
            entered[k, e] = run.astype(BF16)
        factors = pick(decay[k, e], z * share)
        run = step(run, factors, held[k, e].astype(F32))
        fade = [one * two for one, two in zip(fade, factors)]
    if last:
        for r in range(groups):
            outs[r][:, 0] = entered[lax.rem(z + r, groups)]
        return
    line = lax.broadcasted_iota(jnp.int32, (EXTRA, LANES), 0)
    place = lax.broadcasted_iota(jnp.int32, (EXTRA, LANES), 1)
    extra = jnp.zeros((EXTRA, LANES), F32)
    for i in range(share):
        high = fade[i].astype(BF16).astype(F32)
        extra = extra + jnp.where((line == 0) & (place == i), high, 0.0)
        extra = extra + jnp.where((line == 1) & (place == i), fade[i] - high, 0.0)
    total_ref[0, :rows] = run.astype(BF16)
    total_ref[0, rows:] = extra.astype(BF16)


def carried(
    place,
    at,
    states,
    marks,
    fades,
    reverse,
    before=lambda x: x,
    between=lambda x: x,
    after=lambda x: x,
):
    groups, chips = place.size["z"], place.chips
    share = M_SHARE // groups
    rows = share * SHD
    slots = states[0].shape[1]
    parts = before(
        [part if r == 0 else place.shift(part, "z", r) for r, part in enumerate(states)]
    )
    marks = parts if marks is None else marks
    block = [pl.BlockSpec((CORES, 1, part.shape[2], NS), lambda s, *_: (0, s, 0, 0)) for part in parts]
    mark = pl.BlockSpec((CORES, 1, EXTRA, NS), lambda s, *_: (0, s, rows // EXTRA, 0))
    total = pl.BlockSpec((1, rows + EXTRA, NS), lambda s, *_: (s, 0, 0))
    fade = pl.BlockSpec((1, EXTRA, NS), lambda s, *_: (s, rows // EXTRA, 0))
    result = pl.BlockSpec((CORES, 1, rows, NS), lambda s, *_: (0, s, 0, 0))
    scratch = [
        pltpu.VMEM((groups, CORES, rows, NS), BF16),
        pltpu.VMEM((groups, CORES, EXTRA, NS), BF16),
    ]

    def call(last, args, specs, outs, out_specs, more):
        return pl.pallas_call(
            functools.partial(
                scan_kernel, groups=groups, chips=chips, share=share, reverse=reverse, last=last
            ),
            grid_spec=pltpu.PrefetchScalarGridSpec(
                num_scalar_prefetch=1,
                grid=(slots,),
                in_specs=block + [mark] * groups + specs,
                out_specs=out_specs,
                scratch_shapes=scratch + more,
            ),
            out_shape=outs,
            compiler_params=pltpu.CompilerParams(vmem_limit_bytes=VMEM),
            cost_estimate=cost(3),
            name="scan",
        )(at, *parts, *marks, *args)

    leaving = call(
        False, [], [], jax.ShapeDtypeStruct((slots, rows + EXTRA, NS), BF16), total, []
    )
    totals = [lax.ppermute(leaving, AXES, place.chip_pairs(k)) for k in range(1, chips)]
    totals = between(totals)
    fades = totals if fades is None else fades
    entering = call(
        True,
        [*totals, *fades],
        [total] * (chips - 1) + [fade] * (chips - 1),
        [jax.ShapeDtypeStruct((CORES, slots, rows, NS), BF16)] * groups,
        [result] * groups,
        [pltpu.VMEM((groups, CORES, rows, NS), BF16)],
    )
    entering = after(entering)
    found = [part if r == 0 else place.shift(part, "z", r) for r, part in enumerate(entering)]
    return [part.reshape(CORES * slots, rows, NS) for part in found], marks, fades


def shards(
    hidden_in,
    out_grad,
    lengths,
    input_gain,
    attn_in_weight,
    attn_out_weight,
    zgate_weight,
    mixer_in_weight,
    step_weight,
    conv_weight,
    conv_bias,
    step_bias,
    decay_log,
    skip_scale,
    mixer_gain,
    mixer_out_weight,
    post_gain,
    gate_weight,
    up_weight,
    down_weight,
):
    place = Place()
    core = place.at["c"]
    groups, chips, devices = place.size["z"], place.chips, place.devices
    na, nb = place.size["a"], place.size["b"]
    slots, piece, width = hidden_in.shape
    span = piece * groups
    rows_all = CORES * slots * piece
    rows_halo = CORES * slots * (piece + HALO)
    q_cols, m_cols = Q_SHARE * HD, M_SHARE * SHD
    lin_cols = q_cols + 2 * HD
    c_cols = m_cols + NS
    at = place.scalars
    shard_rows = attn_in_weight.shape[0]
    out_rows, mix_rows, ff_rows = (
        attn_out_weight.shape[0],
        mixer_out_weight.shape[0],
        down_weight.shape[0],
    )
    ff_half = ff_rows * groups * chips

    rim = lax.ppermute(
        hidden_in[:, piece - KC + 1 :], AXES, [(i, i + 1) for i in range(devices - 1)]
    )
    block = jnp.concatenate(
        [jnp.zeros((slots, HALO - KC + 1, width), BF16), rim, hidden_in], axis=1
    )
    other_index = place.flat + jnp.where(core == 0, groups, -groups)
    pieces_at = jnp.stack([place.flat, other_index]) * piece
    positions = pieces_at[:, None] + jnp.arange(piece, dtype=jnp.int32)
    valid = (positions[:, None, :] < lengths[None, :, None]).astype(F32)
    tokens = jnp.stack([block, place.swap(block)]).astype(F32)
    dy_own = out_grad.astype(F32) * valid[0][..., None]
    dy_low = dy_own.astype(BF16)
    dy = jnp.stack([dy_low, place.swap(dy_low)]).reshape(rows_all, width)

    small = jnp.concatenate([input_gain, mixer_gain, post_gain, conv_bias, conv_weight.reshape(-1)])
    vector_size = small.shape[0]
    terms = jnp.stack([step_bias, decay_log, skip_scale])
    term_size = terms.size
    split_terms = []
    for _ in range(3):
        part = lax.reduce_precision(terms, 8, 7)
        split_terms.append(part.reshape(-1).astype(BF16))
        terms = terms - part
    small = jnp.concatenate([small, *split_terms])
    small_cols = -(-small.shape[0] // shard_rows)
    small = jnp.pad(small, (0, small_cols * shard_rows - small.shape[0]))
    small = small.reshape(shard_rows, small_cols)
    small_at = M_SHARE
    ms_cols = -(-(small_at + small_cols) // LANES) * LANES
    a_cols, b_cols = lin_cols + ms_cols, c_cols

    def early_columns(half):
        return jnp.concatenate(
            [
                attn_in_weight[:, half * q_cols : (half + 1) * q_cols],
                attn_in_weight[:, QH * HD + half * HD : QH * HD + (half + 1) * HD],
                attn_in_weight[:, (QH + KVH + half) * HD : (QH + KVH + half + 1) * HD],
                step_weight[:, half * M_SHARE : (half + 1) * M_SHARE],
                small,
                jnp.zeros((shard_rows, ms_cols - small_at - small_cols), BF16),
                mixer_in_weight[:, half * m_cols : (half + 1) * m_cols],
                mixer_in_weight[:, SH * SHD + half * NS : SH * SHD + (half + 1) * NS],
            ],
            axis=1,
        )

    def sorted_halves(columns):
        halves = (columns(0), columns(1))
        kept = place.by_core(*halves)
        got = place.swap(place.by_core(halves[1], halves[0]))
        return jnp.concatenate([place.by_core(kept, got), place.by_core(got, kept)], axis=0)

    early = place.spread_z(sorted_halves(early_columns))

    def side_by_side(weight):
        return weight.reshape(2, shard_rows, width).transpose(1, 0, 2).reshape(shard_rows, 2 * width)

    out_weights = jnp.concatenate([attn_out_weight, mixer_out_weight], axis=0)
    middle = jnp.concatenate([zgate_weight, side_by_side(out_weights)], axis=1)
    middle = lax.all_gather(middle, AXES, axis=0, tiled=True)
    ff_all = jnp.concatenate([gate_weight, up_weight, side_by_side(down_weight)], axis=1)
    early = place.place_z(early, [[(0, a_cols, 2)], [(a_cols, b_cols, 2)]])
    early = place.plane_second(place.plane_first(early))
    w_a, w_b = place.plane_third(early, [(0, 0, a_cols, 0, 0), (1, 0, b_cols, 1, 0)])
    tail_at = lin_cols
    vectors = w_a[:, tail_at + small_at : tail_at + small_at + small_cols]
    vectors = vectors.reshape(devices, -1).astype(F32)
    sizes = [input_gain.shape[0], mixer_gain.shape[0], post_gain.shape[0], conv_bias.shape[0]]
    ends = [sum(sizes[: k + 1]) for k in range(4)]
    gain_in = vectors[:, : ends[0]].reshape(-1)
    gain_mixer = vectors[:, ends[0] : ends[1]].reshape(-1)
    gain_mixer = place.by_core(gain_mixer[:m_cols], gain_mixer[m_cols:])
    gain_post = vectors[:, ends[1] : ends[2]].reshape(-1)
    shift_all = vectors[:, ends[2] : ends[3]].reshape(-1)
    taps_all = vectors[:, ends[3] : vector_size].reshape(devices, KC, sizes[3])
    taps_all = jnp.transpose(taps_all, (1, 0, 2)).reshape(KC, -1)

    def conv_half(value):
        first = jnp.concatenate(
            [value[..., :m_cols], value[..., 2 * m_cols : 2 * m_cols + NS]], axis=-1
        )
        second = jnp.concatenate(
            [value[..., m_cols : 2 * m_cols], value[..., 2 * m_cols + NS :]], axis=-1
        )
        return place.by_core(first, second)

    taps, shift = conv_half(taps_all), conv_half(shift_all)
    terms = vectors[:groups, vector_size : vector_size + 3 * term_size]
    terms = terms.reshape(groups, 3, 3, SH // groups)
    terms = terms[:, 0] + terms[:, 1] + terms[:, 2]
    terms = jnp.transpose(terms, (1, 0, 2)).reshape(3, SH)
    terms = place.by_core(terms[:, :M_SHARE], terms[:, M_SHARE:])
    bias, log_rates, skip = terms[0], terms[1], terms[2]
    rates = -jnp.exp(log_rates)

    scale_in = inverse_rms(tokens)
    normed = (tokens * scale_in * gain_in).astype(BF16).reshape(rows_halo, width)

    def body_rows(value):
        return value.reshape(CORES, slots, piece + HALO, -1)[:, :, HALO:]

    linear = body_rows(mm(normed, w_a[:, :lin_cols]))
    mixed = mm(normed, w_b).astype(BF16).reshape(CORES, slots, piece + HALO, c_cols)
    step_raw = mm(normed, w_a[:, tail_at:]).astype(BF16)
    step_raw = body_rows(step_raw[:, :M_SHARE]).astype(F32)

    def rows_plan(source, start, pieces_of):
        found = []
        for device in range(devices // 2):
            for first, count, output, to, pitch in pieces_of:
                side, row = divmod(first, shard_rows)

                def where(at, device=device, side=side, row=row, count=count):
                    first = (at[3] * (devices // 2) + device) * shard_rows + row
                    return pl.ds(first, count), pl.ds(start + side * width, width)

                def goal(at, device=device, to=to, pitch=pitch, count=count):
                    return pl.ds(device * pitch + to, count), pl.ds(0, width)

                found.append((source, where, output, goal))
        return found

    def columns_plan(source, start, size, output):
        def where(at):
            return pl.ds(0, width), pl.ds(pl.multiple_of(start + at[3] * size, LANES), size)

        return [(source, where, output, lambda at: (pl.ds(0, width), pl.ds(0, size)))]

    low = jax.ShapeDtypeStruct
    w_z, w_attn_out, w_mixer_out = moved(
        place,
        [middle],
        [low((width, m_cols), BF16), low((q_cols, width), BF16), low((m_cols, width), BF16)],
        columns_plan(0, 0, m_cols, 0)
        + rows_plan(
            0,
            2 * m_cols,
            [
                (0, out_rows, 1, 0, out_rows),
                (out_rows, shard_rows - out_rows, 2, 0, mix_rows),
                (shard_rows, shard_rows, 2, shard_rows - out_rows, mix_rows),
            ],
        ),
    )
    cos_part, sin_part = rotary_tables(positions, HD)
    cos_part, sin_part = cos_part[:, None, :, None], sin_part[:, None, :, None]
    queries = rotate(
        linear[..., :q_cols].reshape(CORES, slots, piece, Q_SHARE, HD), cos_part, sin_part
    ).astype(BF16)
    keys = rotate(
        linear[..., q_cols : q_cols + HD][..., None, :], cos_part, sin_part
    ).astype(BF16)[..., 0, :]
    kv_own = jnp.concatenate([keys, linear[..., q_cols + HD :].astype(BF16)], axis=-1)
    kv_parts = [part.reshape(-1, 2 * HD) for part in place.spread_z(kv_own)]
    plan = []
    for r in range(groups):
        for e in range(CORES):
            for s in range(slots):

                def source(at, e=e, s=s):
                    return pl.ds((e * slots + s) * piece, piece), pl.ds(0, 2 * HD)

                def goal(at, r=r, e=e):
                    z = lax.rem(at[2] + groups - r, groups)
                    h = lax.rem(at[3] + e, CORES)
                    return pl.ds((h * groups + z) * piece, piece), pl.ds(0, 2 * HD)

                plan.append((r, source, s, goal))
    kv_size = jax.ShapeDtypeStruct((CORES * groups * piece, 2 * HD), BF16)
    kv = moved(place, kv_parts, [kv_size] * slots, plan)
    kv = place.plane_first(kv)
    def by_heads(value, before, after):
        value = jnp.transpose(value, (1, 0, 3, 2, 4)).reshape(slots, CORES, Q_SHARE * piece, HD)
        return jnp.pad(value, ((0, 0), (0, 0), (0, 0), (before, after)))

    def from_heads(value):
        value = value.reshape(slots, CORES, Q_SHARE, piece, HD)
        return jnp.transpose(value, (1, 0, 3, 2, 4))

    scale = HD ** (-0.5)
    queries = by_heads(queries * jnp.asarray(scale, BF16), 0, HD)
    pre = shift
    for tap in range(KC):
        first = HALO - KC + 1 + tap
        pre = pre + taps[tap] * mixed[:, :, first : first + piece].astype(F32)
    conv_out, conv_slope = silu_and_slope(pre)
    conv_out = conv_out.astype(BF16)
    features = conv_out[..., :m_cols].reshape(CORES * slots, piece, m_cols)
    shared = conv_out[..., m_cols:]
    shared_other = place.swap(shared)[::-1]
    inject = place.by_core(shared, shared_other).reshape(CORES * slots, piece, NS)
    readout = place.by_core(shared_other, shared).reshape(CORES * slots, piece, NS)
    raw = jnp.pad(step_raw.reshape(CORES * slots, piece, M_SHARE), ((0, 0), (0, 0), (0, LANES - M_SHARE)))
    raw_t = jnp.transpose(raw[..., :16], (0, 2, 1))
    bias_row = jnp.pad(bias, (0, LANES - M_SHARE))[None]
    rate_row = jnp.pad(rates, (0, LANES - M_SHARE))[None]
    bias_col, rate_col = bias_row[0, :16, None], rate_row[0, :16, None]
    skip_row = jnp.repeat(skip, SHD)[None]
    pieces = CORES * slots
    chunk_args = [
        features, inject, readout, raw, raw_t, bias_row, bias_col, rate_row, rate_col, skip_row,
    ]
    share_rows = m_cols // groups
    held = pltpu.VMEM((groups, share_rows, NS), BF16)
    held_more = pltpu.VMEM((groups, share_rows + EXTRA, NS), BF16)
    within, logs, *local = over_pieces(
        chunk_kernel,
        "chunk",
        chunk_args,
        range(5, 10),
        [
            ((pieces, piece, m_cols), F32),
            ((pieces, piece, LANES), F32),
            *[((pieces, share_rows + EXTRA, NS), BF16)] * groups,
        ],
        9,
        at,
        [held_more],
    )
    local = [part.reshape(CORES, slots, share_rows + EXTRA, NS) for part in local]
    held_back = {"kv": kv}

    def before_states(parts):
        parts, held_back["kv"], columns = tie(parts, held_back["kv"], ff_all)
        held_back["ff"] = lax.all_gather(columns, AXES, axis=0, tiled=True)
        held_back["kv"] = place.plane_second(held_back["kv"])
        return parts

    def between_states(totals):
        totals, held_back["kv"] = tie(totals, held_back["kv"])
        return totals

    def after_states(entering):
        entering, held_back["queries"] = tie(entering, queries)
        return entering

    state_in, marks, fades = carried(
        place, at, local, None, None, False, before_states, between_states, after_states
    )
    queries = held_back["queries"]
    kv = place.plane_third(held_back["kv"], [(s, 0, 2 * HD, s, 0) for s in range(slots)])
    ff_whole = held_back["ff"]
    w_gate, w_up, w_down = moved(
        place,
        [ff_whole],
        [low((width, ff_half), BF16), low((width, ff_half), BF16), low((ff_half, width), BF16)],
        columns_plan(0, 0, ff_half, 0)
        + columns_plan(0, 2 * ff_half, ff_half, 1)
        + rows_plan(
            0,
            4 * ff_half,
            [
                (0, shard_rows, 2, 0, ff_rows),
                (shard_rows, shard_rows, 2, shard_rows, ff_rows),
            ],
        ),
    )

    heads_out, lse = zip(
        *[
            attend(pieces_at, lengths[s : s + 1], queries[s : s + 1], kv[s][None], piece)
            for s in range(slots)
        ]
    )
    attended = from_heads(jnp.concatenate(heads_out)[..., HD:]).reshape(rows_all, q_cols)

    attended, state_in = tie(attended, state_in)
    (ssd,) = over_pieces(
        carry_kernel,
        "carry",
        [within, readout, logs, *state_in],
        (),
        [((pieces, piece, m_cols), BF16)],
        5,
        at,
        [held],
    )
    ssd = ssd.reshape(CORES, slots, piece, m_cols).astype(F32)
    zgate = body_rows(mm(normed, w_z).astype(BF16))
    gate_value, gate_slope = silu_and_slope(zgate.astype(F32))
    gated_raw = ssd * gate_value
    squares = jnp.sum(gated_raw * gated_raw, axis=-1)
    squares = squares + place.swap(squares)[::-1]
    scale_mixer = lax.rsqrt(squares / (SH * SHD) + 1e-05)[..., None]
    gated = (gated_raw * scale_mixer * gain_mixer).astype(BF16).reshape(rows_all, m_cols)

    def own_sum(partial):
        partial = partial.reshape(CORES, -1, partial.shape[-1])
        return partial[0] + place.swap(partial[1].astype(BF16)).astype(F32)

    def with_other(value):
        return jnp.stack([value, place.swap(value)]).reshape(-1, value.shape[-1])

    mixers = own_sum(mm(attended, w_attn_out) + mm(gated, w_mixer_out))
    residual = tokens[0][:, HALO:].reshape(-1, width) + mixers
    scale_post = inverse_rms(residual)
    post = with_other((residual * scale_post * gain_post).astype(BF16))
    gate_lin = mm(post, w_gate)
    up_lin = mm(post, w_up)
    gate_act, gate_act_slope = silu_and_slope(gate_lin)
    hidden = (gate_act * up_lin).astype(BF16)
    valid_own = valid[0].reshape(-1, 1)
    layer_out = (valid_own * (residual + own_sum(mm(hidden, w_down)))).astype(BF16)

    dhidden = mm(dy, w_down, NT)
    dgate = (dhidden * up_lin * gate_act_slope).astype(BF16)
    dup = (dhidden * gate_act).astype(BF16)

    def own_parity(grad):
        grad = grad.astype(BF16).reshape(chips // 2, CORES, -1, width)
        kept = lax.dynamic_index_in_dim(grad, core, 1, False)
        got = place.swap(lax.dynamic_index_in_dim(grad, 1 - core, 1, False))
        grad = jnp.concatenate([place.by_core(kept, got), place.by_core(got, kept)], axis=0)
        return grad.reshape(-1, width)

    dpost = own_sum(mm(dgate, w_gate, NT) + mm(dup, w_up, NT))
    dresidual = dy_own.reshape(-1, width) + rms_back(residual, scale_post, gain_post, dpost)
    grad_post_gain = jnp.sum(dpost * residual * scale_post, axis=0)
    dmix = with_other(dresidual.astype(BF16))

    dattended = mm(dmix, w_attn_out, NT).astype(BF16)
    dgated = mm(dmix, w_mixer_out, NT).reshape(CORES, slots, piece, m_cols)
    scaled = dgated * gain_mixer
    inner = jnp.sum(scaled * gated_raw, axis=-1)
    inner = (inner + place.swap(inner)[::-1])[..., None] / (SH * SHD)
    dgated_raw = scale_mixer * scaled - gated_raw * (scale_mixer**3 * inner)
    grad_mixer_gain = jnp.sum(dgated * gated_raw * scale_mixer, axis=(0, 1, 2))
    dssd = (dgated_raw * gate_value).astype(BF16).reshape(pieces, piece, m_cols)
    dzgate = (dgated_raw * ssd * gate_slope).astype(BF16)

    def halo_rows(value):
        value = value.reshape(CORES, slots, piece, -1)
        return jnp.pad(value, ((0, 0), (0, 0), (HALO, 0), (0, 0)))

    dzgate = halo_rows(dzgate).reshape(rows_halo, m_cols)

    direct = over_pieces(
        direct_kernel,
        "direct",
        [dssd, readout, logs],
        (),
        [((pieces, share_rows, NS), BF16)] * groups,
        5,
        at,
        [held],
    )
    direct = [part.reshape(CORES, slots, share_rows, NS) for part in direct]
    dgate, dup, hidden, direct = tie(dgate, dup, hidden, direct)
    ff_grads, ff_start, ff_finish = place.reduce_far(
        [
            (mm(post, dgate, TN).astype(BF16), 2),
            (mm(post, dup, TN).astype(BF16), 2),
            (own_parity(mm(hidden, dy, TN)), 1),
        ]
    )
    out_side = {}

    def before_scan(parts):
        parts, flat = tie(parts, ff_grads)
        out_side["ff"] = ff_start(flat)
        return parts

    def between_scans(totals):
        totals, out_side["dz"], dmix_late = tie(totals, dzgate, dmix)
        grad_outs = jnp.concatenate(
            [
                mm(attended, dmix_late, TN).astype(BF16).reshape(devices // 2, out_rows, width),
                mm(gated, dmix_late, TN).astype(BF16).reshape(devices // 2, mix_rows, width),
            ],
            axis=1,
        )
        mid_grads, mid_start, out_side["finish"] = place.reduce_far(
            [
                (own_parity(grad_outs), 1),
                (mm(normed, out_side["dz"], TN).astype(BF16), 2),
            ]
        )
        totals, mid_grads = tie(totals, mid_grads)
        out_side["mid"] = mid_start(mid_grads)
        return totals

    def after_scans(entering):
        entering, out_side["dattended"] = tie(entering, dattended)
        return entering

    later, _, _ = carried(
        place, at, direct, marks, fades, True, before_scan, between_scans, after_scans
    )
    ff_grads, mid_grads, mid_finish = out_side["ff"], out_side["mid"], out_side["finish"]
    dattended = out_side["dattended"]
    dnormed = mm(out_side["dz"], w_z, NT)

    dout = by_heads(
        dattended.reshape(CORES, slots, piece, Q_SHARE, HD), HD, 0
    )
    dqueries, dkv = zip(
        *[
            attend_back(
                pieces_at,
                lengths[s : s + 1],
                queries[s : s + 1],
                kv[s][None],
                heads_out[s],
                dout[s : s + 1],
                lse[s],
                piece,
            )
            for s in range(slots)
        ]
    )
    dqueries = jnp.concatenate(dqueries)
    dkv, later = tie(dkv, later)
    dkv = [
        place.reduce_first(dkv[s].reshape(na, nb, CORES, groups, piece, 2 * HD), s % 2 == 0)
        for s in range(slots)
    ]

    dfeatures, dinject, dreadout, draw, sums = over_pieces(
        chunk_back_kernel,
        "chunk_back",
        chunk_args + [dssd, *state_in, *later],
        range(5, 10),
        [
            ((pieces, piece, m_cols), F32),
            ((pieces, piece, NS), F32),
            ((pieces, piece, NS), F32),
            ((pieces, piece, LANES), F32),
            ((pieces, 8, LANES), F32),
        ],
        28,
        at,
        [pltpu.VMEM((LANES, 2 * LANES), F32), pltpu.VMEM((piece, LANES), F32), held, held],
    )
    ff_grads, dkv, dfeatures = tie(ff_grads, dkv, dfeatures)
    dkv = [place.reduce_second(dkv[s], s % 2 == 0) for s in range(slots)]
    dinject = dinject.reshape(CORES, slots, piece, NS)
    dreadout = dreadout.reshape(CORES, slots, piece, NS)
    dshared = place.by_core(dinject, dreadout) + place.swap(
        place.by_core(dreadout, dinject).astype(BF16)
    )[::-1].astype(F32)
    dconv = jnp.concatenate([dfeatures.reshape(CORES, slots, piece, m_cols), dshared], axis=-1)
    dpre = dconv * conv_slope
    grad_taps = []
    dmixed = jnp.zeros((CORES, slots, piece + HALO, c_cols), F32)
    for tap in range(KC):
        first = HALO - KC + 1 + tap
        seen = mixed[:, :, first : first + piece].astype(F32)
        grad_taps.append(jnp.sum(dpre * seen, axis=(0, 1, 2)))
        dmixed = dmixed + jnp.pad(
            dpre * taps[tap], ((0, 0), (0, 0), (first, KC - 1 - tap), (0, 0))
        )
    grad_shift = jnp.sum(dpre, axis=(0, 1, 2))
    dmixed = dmixed.astype(BF16)

    def by_columns(grad):
        return grad.reshape(na, nb, CORES, groups, shard_rows, grad.shape[-1])


    dstep = draw[..., :M_SHARE].astype(BF16)
    db_low = dmixed.reshape(rows_halo, b_cols)
    dkv, db_low = tie(dkv, db_low)
    grad_b = place.reduce_first(by_columns(mm(normed, db_low, TN)), False)
    dkv_own = place.reduce_z(dkv)
    ff_grads, db_late = tie(ff_grads, db_low)
    ff_grads = ff_finish(ff_grads)
    dnormed = dnormed + mm(db_late, w_b, NT)
    head_sums = place.sum_along(jnp.sum(sums, axis=0)[:3, :M_SHARE], "z")
    dkv_own, grad_b, dnormed, head_sums = tie(dkv_own, grad_b, dnormed, head_sums)
    dkv_own = jnp.stack([part.reshape(CORES, piece, 2 * HD) for part in dkv_own], axis=1)
    dkv_own = place.by_core(dkv_own, dkv_own[::-1])
    grad_b = place.reduce_second(grad_b, False)
    dq_rows = from_heads(dqueries[..., :HD] * scale)
    dq_rows = rotate(dq_rows, cos_part, -sin_part).reshape(CORES, slots, piece, q_cols)
    dk_rows = rotate(dkv_own[..., None, :HD], cos_part, -sin_part)[..., 0, :]
    tail_zeros = jnp.zeros((CORES, slots, piece, ms_cols - M_SHARE), BF16)
    dlin = jnp.concatenate([dq_rows, dk_rows, dkv_own[..., HD:]], axis=-1).astype(BF16)
    da_low = halo_rows(
        jnp.concatenate(
            [dlin, dstep.reshape(CORES, slots, piece, -1), tail_zeros], axis=-1
        )
    ).reshape(rows_halo, a_cols)
    dnormed = dnormed + mm(da_low, w_a, NT)
    grad_input_gain = jnp.sum(
        dnormed.reshape(CORES, slots, piece + HALO, width) * (tokens * scale_in), axis=(0, 1, 2)
    )
    dnormed = own_sum(dnormed).reshape(slots, piece + HALO, width)
    rim_back = lax.ppermute(
        dnormed[:, HALO - KC + 1 : HALO].astype(BF16),
        AXES,
        [(i + 1, i) for i in range(devices - 1)],
    ).astype(F32)
    dnormed = dnormed[:, HALO:] + jnp.pad(rim_back, ((0, 0), (piece - KC + 1, 0), (0, 0)))
    own, own_scale = tokens[0][:, HALO:], scale_in[0][:, HALO:]
    input_grad = dresidual.reshape(slots, piece, width) + rms_back(
        own, own_scale, gain_in, dnormed
    )

    zero_half = jnp.zeros((m_cols,), F32)

    def conv_whole(value):
        none = jnp.zeros_like(value)
        first, second = place.by_core(value, none), place.by_core(none, value)
        return jnp.concatenate(
            [first[..., :m_cols], second[..., :m_cols], first[..., m_cols:], second[..., m_cols:]],
            axis=-1,
        )

    grad_mixer_gain = jnp.concatenate(
        [place.by_core(grad_mixer_gain, zero_half), place.by_core(zero_half, grad_mixer_gain)]
    )
    grad_taps = conv_whole(jnp.stack(grad_taps)).reshape(KC, devices, -1)
    vector_grads = jnp.concatenate(
        [
            grad_input_gain.reshape(devices, -1),
            grad_mixer_gain.reshape(devices, -1),
            grad_post_gain.reshape(devices, -1),
            conv_whole(grad_shift).reshape(devices, -1),
            jnp.transpose(grad_taps, (1, 0, 2)).reshape(devices, -1),
        ],
        axis=1,
    )
    vector_grads = jnp.pad(
        vector_grads, ((0, 0), (0, small_cols * shard_rows - vector_size))
    ).reshape(width, small_cols)
    grad_a = mm(normed, da_low, TN)
    grad_a = grad_a + jnp.pad(
        vector_grads,
        ((0, 0), (tail_at + small_at, a_cols - tail_at - small_at - small_cols)),
    )
    mid_grads, grad_a, grad_b = tie(mid_grads, grad_a, grad_b)
    mid_grads = mid_finish(mid_grads)
    grad_b = place.reduce_z([grad_b])[0]
    grad_a = place.reduce_first(by_columns(grad_a), True)
    head_sums = place.sum_along(head_sums, "b")
    grad_a, grad_b, head_sums = tie(grad_a, grad_b, head_sums)
    grad_a = place.reduce_second(grad_a, True)
    head_sums = place.sum_along(head_sums, "a")
    grad_a, head_sums = tie(grad_a, head_sums)
    (grad_a,) = place.reduce_z([grad_a])
    other_sums = place.swap(head_sums)
    head_sums = jnp.concatenate(
        [place.by_core(head_sums, other_sums), place.by_core(other_sums, head_sums)], axis=1
    )
    head_sums = lax.dynamic_slice_in_dim(head_sums, place.at["z"] * (SH // groups), SH // groups, 1)

    def between_cores(columns):
        columns = columns.reshape(CORES, shard_rows, -1)
        kept = lax.dynamic_index_in_dim(columns, core, 0, False)
        got = place.swap(lax.dynamic_index_in_dim(columns, 1 - core, 0, False))
        return place.by_core(kept, got), place.by_core(got, kept)

    ff_rows_each = ff_grads.shape[0] // 3
    both = between_cores(
        jnp.concatenate([ff_grads[:ff_rows_each], ff_grads[ff_rows_each : 2 * ff_rows_each]], axis=1)
    )
    grad_gate = jnp.concatenate([half[:, :ff_half] for half in both], axis=1).astype(F32)
    grad_up = jnp.concatenate([half[:, ff_half:] for half in both], axis=1).astype(F32)
    grad_down = ff_grads[2 * ff_rows_each :].astype(F32)
    grad_outs = mid_grads[:, :width].astype(F32)
    grad_zgate = jnp.concatenate(between_cores(mid_grads[:, width:]), axis=1).astype(F32)
    conv_first, conv_second = between_cores(grad_b)
    first, second = between_cores(grad_a)

    def both_halves(start, size):
        return jnp.concatenate([first[:, start : start + size], second[:, start : start + size]], 1)

    grad_attn_in = jnp.concatenate(
        [both_halves(0, q_cols), both_halves(q_cols, HD), both_halves(q_cols + HD, HD)], axis=1
    )
    grad_mixer_in = jnp.concatenate(
        [conv_first[:, :m_cols], conv_second[:, :m_cols], conv_first[:, m_cols:], conv_second[:, m_cols:]],
        axis=1,
    )
    grad_step = both_halves(lin_cols, M_SHARE)
    small_at = lin_cols + small_at
    small_sum = (first + second)[:, small_at : small_at + small_cols].reshape(-1)

    return (
        layer_out.reshape(slots, piece, width),
        input_grad,
        small_sum[: ends[0]],
        grad_attn_in,
        grad_outs[:out_rows],
        grad_zgate,
        grad_mixer_in,
        grad_step,
        small_sum[ends[3] : vector_size].reshape(KC, -1),
        small_sum[ends[2] : ends[3]],
        head_sums[0],
        head_sums[1],
        head_sums[2],
        small_sum[ends[0] : ends[1]],
        grad_outs[out_rows:],
        small_sum[ends[1] : ends[2]],
        grad_gate,
        grad_up,
        grad_down,
    )


def solution(mesh):
    rows, columns, vector = P(AXES, None), P(None, AXES), P(AXES)
    tokens, heads = P(None, AXES, None), P("sp")
    in_specs = (
        tokens,
        tokens,
        P(),
        vector,
        rows,
        rows,
        rows,
        rows,
        rows,
        columns,
        vector,
        heads,
        heads,
        heads,
        vector,
        rows,
        vector,
        rows,
        rows,
        rows,
    )
    out_specs = (
        tokens,
        tokens,
        vector,
        rows,
        rows,
        rows,
        rows,
        rows,
        columns,
        vector,
        heads,
        heads,
        heads,
        vector,
        rows,
        vector,
        rows,
        rows,
        rows,
    )
    return jax.shard_map(shards, mesh=mesh, in_specs=in_specs, out_specs=out_specs, check_vma=False)
```

```python
import functools
import math

import jax
import jax.numpy as jnp
from jax import lax
from jax.experimental import pallas as pl
from jax.experimental.pallas import tpu as pltpu
from jax.sharding import PartitionSpec as P

QH = 8
KVH = 2
HD = 64
SH = 24
SHD = 64
NS = 128
KC = 4
CORES = 2
MASKED = -1e30
AXES = ("ctx", "sp")
F32 = jnp.float32
BF16 = jnp.bfloat16
LANES = 128
HALO = 8
EXTRA = 16
Q_SHARE = QH // CORES
M_SHARE = SH // CORES
VMEM = 56 * 2**20

NT = (((1,), (1,)), ((), ()))
TN = (((0,), (0,)), ((), ()))
NN = (((1,), (0,)), ((), ()))


def mm(left, right, dims=NN, precision=None):
    return lax.dot_general(
        left, right, dims, precision=precision, preferred_element_type=F32
    )


def tie(*values):
    return lax.optimization_barrier(values)


def cost(micros):
    return pl.CostEstimate(flops=int(micros * 1.15e9), bytes_accessed=0, transcendentals=0)


class Place:
    def __init__(self):
        ctx = lax.axis_size("ctx")
        groups = lax.axis_size("sp")
        chips = ctx // CORES
        nb = math.isqrt(chips)
        self.size = {"a": chips // nb, "b": nb, "z": groups, "c": CORES}
        self.devices = ctx * groups
        index = lax.axis_index("ctx")
        self.at = {
            "a": index // CORES // nb,
            "b": (index // CORES) % nb,
            "z": lax.axis_index("sp"),
            "c": index % CORES,
        }
        self.chip = index // CORES
        self.chips = chips
        self.scalars = jnp.stack(
            [self.at["a"], self.at["b"], self.at["z"], self.at["c"], self.chip]
        ).astype(jnp.int32)
        self.flat = index * groups + self.at["z"]

    def flat_of(self, a, b, z, c):
        return ((a * self.size["b"] + b) * CORES + c) * self.size["z"] + z

    def pairs(self, dim, by):
        found = []
        for a in range(self.size["a"]):
            for b in range(self.size["b"]):
                for z in range(self.size["z"]):
                    for c in range(CORES):
                        spot = {"a": a, "b": b, "z": z, "c": c}
                        goal = dict(spot)
                        goal[dim] = (spot[dim] + by) % self.size[dim]
                        found.append((self.flat_of(**spot), self.flat_of(**goal)))
        return found

    def shift(self, x, dim, by):
        return lax.ppermute(x, AXES, self.pairs(dim, by))

    def swap(self, x):
        return self.shift(x, "c", 1)

    def by_core(self, zero, one):
        return jnp.where(self.at["c"] == 0, zero, one)

    def chip_pairs(self, by):
        groups = self.size["z"]
        return [
            ((chip * CORES + c) * groups + z, (((chip + by) % self.chips) * CORES + c) * groups + z)
            for chip in range(self.chips)
            for c in range(CORES)
            for z in range(groups)
        ]

    def spread_z(self, x):
        return [x] + [self.shift(x, "z", k) for k in range(1, self.size["z"])]

    def plane_first(self, halves):
        found = []
        for index, half in enumerate(halves):
            dim = "ab"[index % 2 == 0]
            found.append([half] + [self.shift(half, dim, k) for k in range(1, self.size[dim])])
        return found

    def plane_second(self, halves):
        found = []
        for index, parts in enumerate(halves):
            dim = "ba"[index % 2 == 0]
            moves = range(1, self.size[dim])
            found.append([parts] + [[self.shift(part, dim, k) for part in parts] for k in moves])
        return found

    def place_z(self, parts, halves):
        groups = self.size["z"]
        rows = parts[0].shape[0]
        outs = [
            jax.ShapeDtypeStruct((groups * rows, sum(size for _, size, _ in half)), parts[0].dtype)
            for half in halves
        ]
        plan = []
        for index, half in enumerate(halves):
            to = 0
            for start, size, count in half:
                block = rows // count
                for r in range(groups):
                    for m in range(count):

                        def source(at, m=m, start=start, size=size, block=block):
                            return pl.ds(m * block, block), pl.ds(start, size)

                        def goal(at, m=m, r=r, to=to, size=size, block=block):
                            z = lax.rem(at[2] + groups - r, groups)
                            return pl.ds((m * groups + z) * block, block), pl.ds(to, size)

                        plan.append((r, source, index, goal))
                to += size
        return moved(self, parts, outs, plan)

    def plane_third(self, halves, wanted):
        rows, dtype = halves[0][0][0].shape[0], halves[0][0][0].dtype
        na, nb = self.size["a"], self.size["b"]
        keys = [(da, db) for da in range(na) for db in range(nb)]
        widths = {}
        heights = {}
        for _, _, size, array, column, *base in wanted:
            widths[array] = max(widths.get(array, 0), column + size)
            heights[array] = max(heights.get(array, 0), sum(base) + self.chips * rows)
        outs = [jax.ShapeDtypeStruct((heights[k], widths[k]), dtype) for k in range(len(widths))]
        sources = []
        for index, half in enumerate(halves):
            sources += [half[da][db] if index % 2 == 0 else half[db][da] for da, db in keys]
        plan = []
        for half, start, size, array, column, *base in wanted:
            for index, (da, db) in enumerate(keys):

                def source(at, start=start, size=size):
                    return pl.ds(0, rows), pl.ds(start, size)

                def goal(at, da=da, db=db, column=column, size=size, base=sum(base)):
                    chip = lax.rem(at[0] + na - da, na) * nb + lax.rem(at[1] + nb - db, nb)
                    return pl.ds(base + chip * rows, rows), pl.ds(column, size)

                plan.append((half * len(keys) + index, source, array, goal))
        return moved(self, sources, outs, plan)

    def stack_far(self, grads):
        cores = [[chip * CORES + c for chip in range(self.chips)] for c in range(CORES)]
        chips = self.chips
        rows, wide = grads[0].shape[0] // chips, grads[0].shape[1]
        high = len(grads) * rows
        plan = []
        for k in range(len(grads)):
            for chip in range(chips):

                def source(at, chip=chip):
                    return pl.ds(chip * rows, rows), pl.ds(0, wide)

                def goal(at, chip=chip, row=k * rows):
                    return pl.ds(chip * high + row, rows), pl.ds(0, wide)

                plan.append((k, source, 0, goal))
        (flat,) = moved(self, grads, [jax.ShapeDtypeStruct((chips * high, wide), BF16)], plan)

        def start(flat):
            return lax.psum_scatter(
                flat, "ctx", scatter_dimension=0, tiled=True, axis_index_groups=cores
            )

        return flat, start

    def finish_far(self, flats, counts):
        groups, wide = self.size["z"], flats[0].shape[1]
        height = sum(flat.shape[0] for flat in flats)
        deep = height // groups
        plan, to = [], 0
        for index, (flat, ms) in enumerate(zip(flats, counts)):
            share = flat.shape[0] // len(ms)
            for k, count in enumerate(ms):
                block = share // groups // count
                for z in range(groups):
                    for m in range(count):

                        def source(at, row=k * share + (m * groups + z) * block, block=block):
                            return pl.ds(row, block), pl.ds(0, wide)

                        def goal(at, row=z * deep + to + m * block, block=block):
                            return pl.ds(row, block), pl.ds(0, wide)

                        plan.append((index, source, 0, goal))
                to += share // groups
        (flat,) = moved(self, flats, [jax.ShapeDtypeStruct((height, wide), BF16)], plan)
        return lax.psum_scatter(flat, "sp", scatter_dimension=0, tiled=True)

    def reduce(self, x, dim, axis):
        n, v = self.size[dim], self.at[dim]
        total = lax.dynamic_index_in_dim(x, v, axis, False).astype(F32)
        for k in range(1, n):
            piece = lax.dynamic_index_in_dim(x, (v + k) % n, axis, False).astype(BF16)
            total = total + self.shift(piece, dim, k).astype(F32)
        return total

    def reduce_first(self, grad, b_first):
        return self.reduce(grad, "a", 0) if b_first else self.reduce(grad, "b", 1)

    def reduce_second(self, grad, b_first):
        return self.reduce(grad, "b" if b_first else "a", 0)

    def reduce_z(self, left):
        n, v = self.size["z"], self.at["z"]

        def cut(x, index):
            piece = lax.dynamic_index_in_dim(x, index, 1, False)
            return piece.reshape(-1, piece.shape[-1])

        totals = [cut(x, v) for x in left]
        for k in range(1, n):
            sent = jnp.concatenate([cut(x, (v + k) % n).astype(BF16) for x in left], axis=-1)
            got = self.shift(sent, "z", k).astype(F32)
            start = 0
            for index, total in enumerate(totals):
                stop = start + total.shape[-1]
                totals[index] = total + got[:, start:stop]
                start = stop
        return totals

    def sum_step(self, x, dim, step):
        found = []
        for a in range(self.size["a"]):
            for b in range(self.size["b"]):
                for z in range(self.size["z"]):
                    for c in range(CORES):
                        spot = {"a": a, "b": b, "z": z, "c": c}
                        goal = dict(spot)
                        goal[dim] = spot[dim] ^ step
                        found.append((self.flat_of(**spot), self.flat_of(**goal)))
        return x + lax.ppermute(x, AXES, found)

    def sum_along(self, x, dims):
        for dim in dims:
            step = 1
            while step < self.size[dim]:
                x = self.sum_step(x, dim, step)
                step *= 2
        return x


def moved_kernel(at_ref, *refs, plan, count):
    sems = refs[-1]
    copies = [
        pltpu.make_async_copy(
            refs[source].at[where(at_ref)], refs[count + goal].at[to(at_ref)], sems.at[index]
        )
        for index, (source, where, goal, to) in enumerate(plan)
    ]
    for copy in copies:
        copy.start()
    for copy in copies:
        copy.wait()


def moved(place, sources, outs, plan):
    size = sum(math.prod(out.shape) * out.dtype.itemsize for out in outs)
    return pl.pallas_call(
        functools.partial(moved_kernel, plan=plan, count=len(sources)),
        in_specs=[pl.BlockSpec(memory_space=pltpu.SMEM)]
        + [pl.BlockSpec(memory_space=pl.ANY)] * len(sources),
        out_specs=[pl.BlockSpec(memory_space=pltpu.VMEM)] * len(outs),
        out_shape=outs,
        scratch_shapes=[pltpu.SemaphoreType.DMA((len(plan),))],
        compiler_params=pltpu.CompilerParams(vmem_limit_bytes=VMEM),
        cost_estimate=pl.CostEstimate(flops=0, bytes_accessed=2 * size, transcendentals=0),
        name="moved",
    )(place.scalars, *sources)


def rotary_tables(positions, width):
    half_width = width // 2
    inverse = 100000000000.0 ** (-jnp.arange(half_width, dtype=F32) * 2.0 / width)
    angles = positions.astype(F32)[..., None] * inverse
    return (jnp.cos(angles), jnp.sin(angles))


def rotate(value, cos_part, sin_part):
    half_width = value.shape[-1] // 2
    first = value[..., :half_width]
    second = value[..., half_width:]
    return jnp.concatenate(
        [first * cos_part - second * sin_part, second * cos_part + first * sin_part], axis=-1
    )


def inverse_rms(value):
    return lax.rsqrt(jnp.mean(value * value, axis=-1, keepdims=True) + 1e-05)


def rms_back(value, scale, gain, grad):
    scaled = grad * gain
    inner = jnp.mean(scaled * value, axis=-1, keepdims=True)
    return scale * scaled - value * (scale * scale * scale * inner)


def silu_and_slope(value):
    gate = jax.nn.sigmoid(value)
    out = value * gate
    return out, gate + out * (1.0 - gate)


def causal_keep(first_key, first_query, keys, piece, columns):
    key = first_key + lax.broadcasted_iota(jnp.int32, (keys, columns), 0)
    column = lax.broadcasted_iota(jnp.int32, (keys, columns), 1)
    head = sum((column >= piece * k).astype(jnp.int32) for k in range(1, columns // piece))
    return key <= first_query + column - head * piece


def stack_heads(block, high):
    found = []
    for head in range(Q_SHARE):
        pair = block[:, head // 2 * LANES : (head // 2 + 1) * LANES].astype(F32)
        if (head % 2 == 1) != high:
            pair = pltpu.roll(pair, HD, 1)
        lane = lax.broadcasted_iota(jnp.int32, pair.shape, 1)
        found.append(jnp.where((lane >= HD) if high else (lane < HD), pair, 0.0))
    return jnp.concatenate(found, axis=0).astype(BF16)


def unstack_heads(stacked, piece, high):
    found = []
    for pair in range(Q_SHARE // 2):
        first = stacked[2 * pair * piece : (2 * pair + 1) * piece]
        second = stacked[(2 * pair + 1) * piece : (2 * pair + 2) * piece]
        if high:
            first = pltpu.roll(first, HD, 1)
        else:
            second = pltpu.roll(second, HD, 1)
        lane = lax.broadcasted_iota(jnp.int32, first.shape, 1)
        found.append(jnp.where(lane < HD, first, second))
    return jnp.concatenate(found, axis=1)


def attend_kernel(places, lengths, q_ref, kv_ref, out_ref, lse_ref, acc, top, total, held, *, piece):
    slot, which = pl.program_id(0), pl.program_id(1)
    first_query = places[which]
    columns = held.shape[0]
    block = columns
    out_ref[...] = jnp.zeros_like(out_ref)
    lse_ref[...] = jnp.zeros_like(lse_ref)

    @pl.when(first_query < lengths[slot])
    def _():
        held[...] = stack_heads(q_ref[0, 0], False)
        acc[...] = jnp.zeros_like(acc)
        top[...] = jnp.full_like(top, MASKED)
        total[...] = jnp.zeros_like(total)
        whole = first_query // block

        def visit(index, masked):
            start = pl.multiple_of(index * block, block)
            kv = kv_ref[0, pl.ds(start, block), :]
            scores = mm(kv, held[...], NT)
            if masked:
                keep = causal_keep(start, first_query, block, piece, columns)
                scores = jnp.where(keep, scores, MASKED)
            before = top[...]
            now = jnp.maximum(before, jnp.max(scores, axis=0, keepdims=True))
            weights = jnp.exp(scores - now)
            ratio = jnp.exp(before - now)
            total[...] = total[...] * ratio + jnp.sum(weights, axis=0, keepdims=True)
            acc[...] = acc[...] * ratio + mm(kv, weights.astype(BF16), TN)
            top[...] = now

        @pl.loop(0, whole)
        def _(index):
            visit(index, False)

        visit(whole, True)
        out_ref[0, 0] = unstack_heads((acc[...] / total[...]).T, piece, True).astype(BF16)
        lse_ref[0, 0] = top[...] + jnp.log(total[...])


def attend(places, lengths, queries, kv, piece):
    _, slots, _, wide = queries.shape
    length, width = kv.shape[1:]
    columns = Q_SHARE * piece
    rows = pl.BlockSpec((1, 1, piece, wide), lambda s, e, *_: (e, s, 0, 0))
    return pl.pallas_call(
        functools.partial(attend_kernel, piece=piece),
        grid_spec=pltpu.PrefetchScalarGridSpec(
            num_scalar_prefetch=2,
            grid=(slots, CORES),
            in_specs=[
                rows,
                pl.BlockSpec((1, length, width), lambda s, e, *_: (s, 0, 0)),
            ],
            out_specs=[
                rows,
                pl.BlockSpec((1, 1, 1, columns), lambda s, e, *_: (s, e, 0, 0)),
            ],
            scratch_shapes=[
                pltpu.VMEM((width, columns), F32),
                pltpu.VMEM((1, columns), F32),
                pltpu.VMEM((1, columns), F32),
                pltpu.VMEM((columns, width), BF16),
            ],
        ),
        out_shape=[
            jax.ShapeDtypeStruct(queries.shape, BF16),
            jax.ShapeDtypeStruct((slots, CORES, 1, columns), F32),
        ],
        compiler_params=pltpu.CompilerParams(vmem_limit_bytes=VMEM),
        cost_estimate=cost(20),
        name="attend",
    )(places, lengths, queries, kv)


def attend_back_kernel(
    places, lengths, q_ref, kv_ref, out_ref, dout_ref, lse_ref, dq_ref, dkv_ref, dkv, dq, *, piece
):
    slot, which = pl.program_id(0), pl.program_id(1)
    first_query = places[which]
    columns = dq.shape[1]
    block = columns
    dq_ref[...] = jnp.zeros_like(dq_ref)

    @pl.when(which == 0)
    def _():
        dkv[...] = jnp.zeros_like(dkv)

    @pl.when(first_query < lengths[slot])
    def _():
        dq[...] = jnp.zeros_like(dq)
        queries = stack_heads(q_ref[0, 0], False)
        dout = stack_heads(dout_ref[0, 0], True)
        both = dout.astype(F32) * stack_heads(out_ref[0, 0], True).astype(F32)
        delta = mm(jnp.ones((8, both.shape[1]), F32), both, NT, lax.Precision.HIGHEST)[:1]
        lse = lse_ref[0, 0]
        whole = first_query // block

        def visit(index, masked):
            start = pl.multiple_of(index * block, block)
            kv = kv_ref[0, pl.ds(start, block), :]
            scores = mm(kv, queries, NT)
            if masked:
                keep = causal_keep(start, first_query, block, piece, columns)
                scores = jnp.where(keep, scores, MASKED)
            probs = jnp.exp(scores - lse)
            dprobs = mm(kv, dout, NT)
            dscores = (probs * (dprobs - delta)).astype(BF16)
            probs = probs.astype(BF16)
            dkv[pl.ds(start, block), :] += mm(dscores, queries) + mm(probs, dout)
            dq[...] += mm(kv, dscores, TN)

        @pl.loop(0, whole)
        def _(index):
            visit(index, False)

        visit(whole, True)
        dq_ref[0, 0] = unstack_heads(dq[...].T, piece, False)

    @pl.when(which == CORES - 1)
    def _():
        dkv_ref[0] = dkv[...].astype(dkv_ref.dtype)


def attend_back(places, lengths, queries, kv, out, dout, lse, piece):
    _, slots, _, wide = queries.shape
    length, width = kv.shape[1:]
    columns = Q_SHARE * piece
    rows = pl.BlockSpec((1, 1, piece, wide), lambda s, e, *_: (e, s, 0, 0))
    keys = pl.BlockSpec((1, length, width), lambda s, e, *_: (s, 0, 0))
    return pl.pallas_call(
        functools.partial(attend_back_kernel, piece=piece),
        grid_spec=pltpu.PrefetchScalarGridSpec(
            num_scalar_prefetch=2,
            grid=(slots, CORES),
            in_specs=[
                rows,
                keys,
                rows,
                rows,
                pl.BlockSpec((1, 1, 1, columns), lambda s, e, *_: (s, e, 0, 0)),
            ],
            out_specs=[rows, keys],
            scratch_shapes=[pltpu.VMEM((length, width), F32), pltpu.VMEM((width, columns), F32)],
        ),
        out_shape=[
            jax.ShapeDtypeStruct(queries.shape, F32),
            jax.ShapeDtypeStruct(kv.shape, BF16),
        ],
        compiler_params=pltpu.CompilerParams(vmem_limit_bytes=VMEM),
        cost_estimate=cost(25),
        name="attend_back",
    )(places, lengths, queries, kv, out, dout, lse)


def lower(rows, transposed=False):
    row = lax.broadcasted_iota(jnp.int32, (rows, rows), 0)
    column = lax.broadcasted_iota(jnp.int32, (rows, rows), 1)
    return row <= column if transposed else row >= column


def paired(first, second, shape):
    lane = lax.broadcasted_iota(jnp.int32, shape, 1)
    return jnp.where(lane < SHD, first, second)


def chunk_terms(raw_ref, bias_ref, rate_ref):
    raw = raw_ref[0].astype(F32)[HALO:] + bias_ref[...]
    rows = raw.shape[0]
    steps = jax.nn.softplus(raw)
    logs = mm(lower(rows).astype(F32), steps * rate_ref[...], NN, lax.Precision.HIGHEST)

    def turned(value):
        more = jnp.zeros((2 * LANES - rows, LANES), F32)
        return jnp.concatenate([value, more], axis=0).T[:, :rows]

    return raw, steps, turned(steps), logs, turned(logs)


def chunk_kernel(
    f_ref, b_ref, c_ref, raw_ref, bias_ref, rate_ref, skip_ref,
    at_ref, out_ref, logs_ref, *rest,
):
    state_refs, held = rest[:-1], rest[-1]
    raw, steps, steps_t, logs, logs_t = chunk_terms(raw_ref, bias_ref, rate_ref)
    logs_ref[0] = logs
    rows = logs.shape[0]
    inject = b_ref[0]
    mix = jnp.where(lower(rows), mm(c_ref[0], inject, NT), 0.0)
    tail = jnp.exp(logs[rows - 1 :] - logs) * steps
    for pair in range(M_SHARE // 2):
        lanes = slice(pair * LANES, (pair + 1) * LANES)
        feats = f_ref[0, :, lanes]
        outs = []
        for head in (2 * pair, 2 * pair + 1):
            gap = jnp.minimum(logs[:, head : head + 1] - logs_t[head : head + 1, :], 0.0)
            kernel = mix * jnp.exp(gap) * steps_t[head : head + 1, :]
            outs.append(mm(kernel.astype(BF16), feats))
        wide = feats.astype(F32)
        out_ref[0, :, lanes] = paired(outs[0], outs[1], wide.shape) + skip_ref[:, lanes] * wide
        weight = paired(
            tail[:, 2 * pair : 2 * pair + 1], tail[:, 2 * pair + 1 : 2 * pair + 2], wide.shape
        )
        state = mm((wide * weight).astype(BF16), inject, TN).astype(BF16)
        keep_heads(held, state, pair)
    decay = jnp.exp(logs[rows - 1 :])
    line = lax.broadcasted_iota(jnp.int32, (EXTRA, LANES), 0)
    high = decay.astype(BF16).astype(F32)
    extra = jnp.where(line == 0, high, jnp.where(line == 1, decay - high, 0.0)).astype(BF16)
    for group in range(len(state_refs)):
        held[group, held.shape[1] - EXTRA :, :] = extra
    send_groups(held, state_refs, at_ref)


def carry_kernel(out_ref, c_ref, logs_ref, *rest):
    groups = len(rest) - 3
    at_ref, ssd_ref, held = rest[groups], rest[groups + 1], rest[groups + 2]
    take_groups(held, rest[:groups], at_ref)
    decay = jnp.exp(logs_ref[0])
    for pair in range(M_SHARE // 2):
        lanes = slice(pair * LANES, (pair + 1) * LANES)
        read = mm(c_ref[0], pair_rows(held, pair), NT)
        weight = paired(
            decay[:, 2 * pair : 2 * pair + 1], decay[:, 2 * pair + 1 : 2 * pair + 2], read.shape
        )
        ssd_ref[0, :, lanes] = (out_ref[0, :, lanes] + read * weight).astype(BF16)


def direct_kernel(d_ref, c_ref, logs_ref, at_ref, *rest):
    held = rest[-1]
    decay = jnp.exp(logs_ref[0])
    for pair in range(M_SHARE // 2):
        lanes = slice(pair * LANES, (pair + 1) * LANES)
        grad = d_ref[0, :, lanes].astype(F32)
        weight = paired(
            decay[:, 2 * pair : 2 * pair + 1], decay[:, 2 * pair + 1 : 2 * pair + 2], grad.shape
        )
        state = mm((grad * weight).astype(BF16), c_ref[0], TN).astype(BF16)
        keep_heads(held, state, pair)
    send_groups(held, rest[:-1], at_ref)


def chunk_back_kernel(
    f_ref, b_ref, c_ref, raw_ref, bias_ref, rate_ref, skip_ref,
    d_ref, *rest,
):
    groups = (len(rest) - 10) // 2
    at_ref = rest[2 * groups]
    df_ref, db_ref, dc_ref, draw_ref, sums_ref = rest[2 * groups + 1 : 2 * groups + 6]
    columns, row_sums, states, laters = rest[2 * groups + 6 :]
    take_groups(states, rest[:groups], at_ref)
    take_groups(laters, rest[groups : 2 * groups], at_ref)
    raw, steps, steps_t, logs, logs_t = chunk_terms(raw_ref, bias_ref, rate_ref)
    rows = logs.shape[0]
    inject, readout = b_ref[0], c_ref[0]
    keep = lower(rows)
    mix = jnp.where(keep, mm(readout, inject, NT), 0.0)
    columns[...] = jnp.zeros_like(columns)
    row_sums[...] = jnp.zeros_like(row_sums)
    decay = jnp.exp(logs)
    end_decay = jnp.exp(logs[rows - 1 :] - logs)
    tail = end_decay * steps
    dmix = jnp.zeros((rows, rows), F32)
    db = jnp.zeros((rows, NS), F32)
    dc = jnp.zeros((rows, NS), F32)
    to_state = jnp.zeros((rows, LANES), F32)
    from_state = jnp.zeros((rows, LANES), F32)
    skips = jnp.zeros((1, LANES), F32)
    agree = jnp.zeros((1, LANES), F32)
    head_lane = lax.broadcasted_iota(jnp.int32, (rows, LANES), 1)
    for pair in range(M_SHARE // 2):
        lanes = slice(pair * LANES, (pair + 1) * LANES)
        feats, grad = f_ref[0, :, lanes], d_ref[0, :, lanes]
        wide, wide_grad = feats.astype(F32), grad.astype(F32)
        later = pair_rows(laters, pair)
        state = pair_rows(states, pair)
        agreed = later.astype(F32) * state.astype(F32)
        pushed = mm(inject, later, NT)
        read = mm(readout, state, NT)
        push_part = wide * pushed
        read_part = wide_grad * read
        skip_part = wide * wide_grad
        grads = []
        for half, head in enumerate((2 * pair, 2 * pair + 1)):
            column = slice(head, head + 1)
            lane = lax.broadcasted_iota(jnp.int32, wide.shape, 1)
            mine = (lane < SHD) if half == 0 else (lane >= SHD)
            step_row = steps_t[column, :]
            gap = jnp.minimum(logs[:, column] - logs_t[column, :], 0.0)
            fade = jnp.exp(gap)
            dkernel = mm(jnp.where(mine, wide_grad, 0.0).astype(BF16), feats, NT)
            faded = dkernel * fade
            stepped = faded * step_row
            dmix = dmix + stepped
            kernel = mix * fade * step_row
            columns[column, 0:rows] = jnp.sum(faded * mix, axis=0, keepdims=True)
            here = head_lane == head
            row_sums[...] += jnp.where(here, jnp.sum(stepped * mix, axis=1, keepdims=True), 0.0)
            grads.append(mm(kernel.astype(BF16), grad, TN))
            to_state = to_state + jnp.where(
                here, jnp.sum(jnp.where(mine, push_part, 0.0), axis=1, keepdims=True), 0.0
            )
            from_state = from_state + jnp.where(
                here, jnp.sum(jnp.where(mine, read_part, 0.0), axis=1, keepdims=True), 0.0
            )
            same = agreed[half * SHD : (half + 1) * SHD]
            same = jnp.sum(jnp.sum(same, axis=0, keepdims=True), axis=1, keepdims=True)
            agree = agree + jnp.where(here[:1], same, 0.0)
            skips = skips + jnp.where(
                here[:1],
                jnp.sum(
                    jnp.sum(jnp.where(mine, skip_part, 0.0), axis=1, keepdims=True),
                    axis=0,
                    keepdims=True,
                ),
                0.0,
            )
        first, second = slice(2 * pair, 2 * pair + 1), slice(2 * pair + 1, 2 * pair + 2)
        weight = paired(tail[:, first], tail[:, second], wide.shape)
        df_ref[0, :, lanes] = (
            paired(grads[0], grads[1], wide.shape) + skip_ref[:, lanes] * wide_grad + weight * pushed
        )
        db = db + mm((wide * weight).astype(BF16), later)
        seen = paired(decay[:, first], decay[:, second], wide.shape)
        dc = dc + mm((wide_grad * seen).astype(BF16), state)
    low = dmix * jnp.where(keep, 1.0, 0.0)
    low = low.astype(BF16)
    db_ref[0] = db + mm(low, readout, TN)
    dc_ref[0] = dc + mm(low, inject)
    direct = columns[...].T[:rows]
    push = end_decay * to_state
    dlogs = row_sums[...] - steps * direct + decay * from_state - steps * push
    end = jnp.sum(steps * push, axis=0, keepdims=True) + decay[rows - 1 :] * agree
    last = lax.broadcasted_iota(jnp.int32, (rows, LANES), 0) == rows - 1
    dlogs = dlogs + jnp.where(last, end, 0.0)
    summed = mm(lower(rows, True).astype(F32), dlogs, NN, lax.Precision.HIGHEST)
    dsteps = direct + push + summed * rate_ref[...]
    draw = dsteps * jax.nn.sigmoid(raw)
    draw_ref[0] = draw
    line = lax.broadcasted_iota(jnp.int32, (8, LANES), 0)
    dbias = jnp.sum(draw, axis=0, keepdims=True)
    dlog = jnp.sum(summed * steps, axis=0, keepdims=True) * rate_ref[...]
    sums_ref[0] = jnp.where(
        line == 0, dbias, jnp.where(line == 1, dlog, jnp.where(line == 2, skips, 0.0))
    )


def conv_back_kernel(mixed_ref, df_ref, dshared_ref, taps_ref, shift_ref, _, dmixed_ref, sums_ref):
    mixed = mixed_ref[0].astype(F32)
    rows = df_ref.shape[1]
    first = HALO - KC + 1
    pre = shift_ref[...]
    for tap in range(KC):
        pre = pre + taps_ref[tap : tap + 1, :] * mixed[first + tap : first + tap + rows]
    gate = jax.nn.sigmoid(pre)
    slope = gate + pre * gate * (1.0 - gate)
    dpre = jnp.concatenate([df_ref[0], dshared_ref[0]], axis=1) * slope
    line = lax.broadcasted_iota(jnp.int32, (8, dpre.shape[1]), 0)
    sums = jnp.where(line == KC, jnp.sum(dpre, axis=0, keepdims=True), 0.0)
    none = jnp.zeros((HALO, dpre.shape[1]), F32)
    padded = jnp.concatenate([none, dpre, none], axis=0)
    total = jnp.zeros(mixed.shape, F32)
    for tap in range(KC):
        seen = mixed[first + tap : first + tap + rows]
        sums = sums + jnp.where(line == tap, jnp.sum(dpre * seen, axis=0, keepdims=True), 0.0)
        start = HALO - first - tap
        total = total + taps_ref[tap : tap + 1, :] * padded[start : start + rows + HALO]
    dmixed_ref[0] = total.astype(BF16)
    sums_ref[0] = sums


def over_pieces(kernel, name, args, whole, outs, micros, at, scratch=()):
    pieces = args[0].shape[0]

    def spec(shape, split):
        if split:
            return pl.BlockSpec((1,) + shape[1:], lambda i: (i,) + (0,) * (len(shape) - 1))
        return pl.BlockSpec(shape, lambda i: (0,) * len(shape))

    shapes = [(arg.shape, index not in whole) for index, arg in enumerate(args)]
    return pl.pallas_call(
        kernel,
        grid=(pieces,),
        in_specs=[spec(shape, split) for shape, split in shapes]
        + [pl.BlockSpec(memory_space=pltpu.SMEM)],
        out_specs=[spec(shape, True) for shape, _ in outs],
        out_shape=[jax.ShapeDtypeStruct(shape, dtype) for shape, dtype in outs],
        scratch_shapes=list(scratch),
        compiler_params=pltpu.CompilerParams(vmem_limit_bytes=VMEM),
        cost_estimate=cost(micros),
        name=name,
    )(*args, at)


def keep_heads(held, state, pair):
    share = M_SHARE // held.shape[0]
    for half in range(2):
        group, spot = divmod(2 * pair + half, share)
        held[group, spot * SHD : (spot + 1) * SHD, :] = state[half * SHD : (half + 1) * SHD]


def pair_rows(held, pair):
    share = M_SHARE // held.shape[0]
    found = []
    for half in range(2):
        group, spot = divmod(2 * pair + half, share)
        found.append(held[group, spot * SHD : (spot + 1) * SHD, :])
    return jnp.concatenate(found, axis=0)


def send_groups(held, refs, at_ref):
    for r, ref in enumerate(refs):
        ref[0] = held[lax.rem(at_ref[2] + r, len(refs))]


def take_groups(held, refs, at_ref):
    for r, ref in enumerate(refs):
        held[lax.rem(at_ref[2] + len(refs) - r, len(refs))] = ref[0]


def scan_kernel(at_ref, *refs, groups, chips, share, reverse, last):
    rows = share * SHD
    states, marks = refs[:groups], refs[groups : 2 * groups]
    refs = refs[2 * groups :]
    chip, z, core = at_ref[4], at_ref[2], at_ref[3]
    lane = lax.broadcasted_iota(jnp.int32, (1, LANES), 1)

    def pick(pair, offset):
        both = pair[0:1].astype(F32) + pair[1:2].astype(F32)
        return [
            jnp.sum(jnp.where(lane == offset + i, both, 0.0), axis=1, keepdims=True)
            for i in range(share)
        ]

    def step(run, factors, new):
        return jnp.concatenate(
            [
                factors[i] * run[i * SHD : (i + 1) * SHD] + new[i * SHD : (i + 1) * SHD]
                for i in range(share)
            ],
            axis=0,
        )

    if last:
        totals, fades = refs[: chips - 1], refs[chips - 1 : 2 * chips - 2]
        outs, held, decay, entered = (
            refs[2 * chips - 2 : 2 * chips - 2 + groups],
            refs[-3],
            refs[-2],
            refs[-1],
        )
    else:
        total_ref, held, decay = refs
    for r in range(groups):
        to = lax.rem(z + groups - r, groups)
        held[to] = states[r][:, 0, :rows]
        decay[to] = marks[r][:, 0]
    run = jnp.zeros((rows, NS), F32)
    if last:
        for k in range(chips - 1, 0, -1):
            part = chips - k if reverse else k
            reached = chip + k < chips if reverse else chip >= k
            new = step(run, pick(fades[part - 1][0], 0), totals[part - 1][0, :rows].astype(F32))
            run = jnp.where(reached, new, run)
    fade = [jnp.ones((1, 1), F32)] * share
    order = [(h, k) for h in range(CORES) for k in range(groups)]
    for h, k in order[::-1] if reverse else order:
        e = lax.rem(h + core, CORES)
        if last:
            entered[k, e] = run.astype(BF16)
        factors = pick(decay[k, e], z * share)
        run = step(run, factors, held[k, e].astype(F32))
        fade = [one * two for one, two in zip(fade, factors)]
    if last:
        for r in range(groups):
            outs[r][:, 0] = entered[lax.rem(z + r, groups)]
        return
    line = lax.broadcasted_iota(jnp.int32, (EXTRA, LANES), 0)
    place = lax.broadcasted_iota(jnp.int32, (EXTRA, LANES), 1)
    extra = jnp.zeros((EXTRA, LANES), F32)
    for i in range(share):
        high = fade[i].astype(BF16).astype(F32)
        extra = extra + jnp.where((line == 0) & (place == i), high, 0.0)
        extra = extra + jnp.where((line == 1) & (place == i), fade[i] - high, 0.0)
    total_ref[0, :rows] = run.astype(BF16)
    total_ref[0, rows:] = extra.astype(BF16)


def carried(
    place,
    at,
    states,
    marks,
    fades,
    reverse,
    before=lambda x: x,
    between=lambda x: x,
    after=lambda x: x,
):
    groups, chips = place.size["z"], place.chips
    share = M_SHARE // groups
    rows = share * SHD
    slots = states[0].shape[1]
    parts = before(
        [part if r == 0 else place.shift(part, "z", r) for r, part in enumerate(states)]
    )
    marks = parts if marks is None else marks
    block = [pl.BlockSpec((CORES, 1, part.shape[2], NS), lambda s, *_: (0, s, 0, 0)) for part in parts]
    mark = pl.BlockSpec((CORES, 1, EXTRA, NS), lambda s, *_: (0, s, rows // EXTRA, 0))
    total = pl.BlockSpec((1, rows + EXTRA, NS), lambda s, *_: (s, 0, 0))
    fade = pl.BlockSpec((1, EXTRA, NS), lambda s, *_: (s, rows // EXTRA, 0))
    result = pl.BlockSpec((CORES, 1, rows, NS), lambda s, *_: (0, s, 0, 0))
    scratch = [
        pltpu.VMEM((groups, CORES, rows, NS), BF16),
        pltpu.VMEM((groups, CORES, EXTRA, NS), BF16),
    ]

    def call(last, args, specs, outs, out_specs, more):
        return pl.pallas_call(
            functools.partial(
                scan_kernel, groups=groups, chips=chips, share=share, reverse=reverse, last=last
            ),
            grid_spec=pltpu.PrefetchScalarGridSpec(
                num_scalar_prefetch=1,
                grid=(slots,),
                in_specs=block + [mark] * groups + specs,
                out_specs=out_specs,
                scratch_shapes=scratch + more,
            ),
            out_shape=outs,
            compiler_params=pltpu.CompilerParams(vmem_limit_bytes=VMEM),
            cost_estimate=cost(3),
            name="scan",
        )(at, *parts, *marks, *args)

    leaving = call(
        False, [], [], jax.ShapeDtypeStruct((slots, rows + EXTRA, NS), BF16), total, []
    )
    totals = [lax.ppermute(leaving, AXES, place.chip_pairs(k)) for k in range(1, chips)]
    totals = between(totals)
    fades = totals if fades is None else fades
    entering = call(
        True,
        [*totals, *fades],
        [total] * (chips - 1) + [fade] * (chips - 1),
        [jax.ShapeDtypeStruct((CORES, slots, rows, NS), BF16)] * groups,
        [result] * groups,
        [pltpu.VMEM((groups, CORES, rows, NS), BF16)],
    )
    entering = after(entering)
    found = [part if r == 0 else place.shift(part, "z", r) for r, part in enumerate(entering)]
    return [part.reshape(CORES * slots, rows, NS) for part in found], marks, fades


def shards(
    hidden_in,
    out_grad,
    lengths,
    input_gain,
    attn_in_weight,
    attn_out_weight,
    zgate_weight,
    mixer_in_weight,
    step_weight,
    conv_weight,
    conv_bias,
    step_bias,
    decay_log,
    skip_scale,
    mixer_gain,
    mixer_out_weight,
    post_gain,
    gate_weight,
    up_weight,
    down_weight,
):
    place = Place()
    core = place.at["c"]
    groups, chips, devices = place.size["z"], place.chips, place.devices
    na, nb = place.size["a"], place.size["b"]
    slots, piece, width = hidden_in.shape
    span = piece * groups
    rows_all = CORES * slots * piece
    rows_halo = CORES * slots * (piece + HALO)
    q_cols, m_cols = Q_SHARE * HD, M_SHARE * SHD
    lin_cols = q_cols + 2 * HD
    c_cols = m_cols + NS
    at = place.scalars
    shard_rows = attn_in_weight.shape[0]
    out_rows, mix_rows, ff_rows = (
        attn_out_weight.shape[0],
        mixer_out_weight.shape[0],
        down_weight.shape[0],
    )
    ff_half = ff_rows * groups * chips

    rim = lax.ppermute(
        hidden_in[:, piece - KC + 1 :], AXES, [(i, i + 1) for i in range(devices - 1)]
    )
    block = jnp.concatenate(
        [jnp.zeros((slots, HALO - KC + 1, width), BF16), rim, hidden_in], axis=1
    )
    other_index = place.flat + jnp.where(core == 0, groups, -groups)
    pieces_at = jnp.stack([place.flat, other_index]) * piece
    positions = pieces_at[:, None] + jnp.arange(piece, dtype=jnp.int32)
    valid = (positions[:, None, :] < lengths[None, :, None]).astype(F32)
    tokens = jnp.stack([block, place.swap(block)]).astype(F32)
    dy_own = out_grad.astype(F32) * valid[0][..., None]
    dy_low = dy_own.astype(BF16)
    dy = jnp.stack([dy_low, place.swap(dy_low)]).reshape(rows_all, width)

    small = jnp.concatenate([input_gain, mixer_gain, post_gain, conv_bias, conv_weight.reshape(-1)])
    vector_size = small.shape[0]
    terms = jnp.stack([step_bias, decay_log, skip_scale])
    term_size = terms.size
    split_terms = []
    for _ in range(3):
        part = lax.reduce_precision(terms, 8, 7)
        split_terms.append(part.reshape(-1).astype(BF16))
        terms = terms - part
    small = jnp.concatenate([small, *split_terms])
    small_cols = -(-small.shape[0] // shard_rows)
    small = jnp.pad(small, (0, small_cols * shard_rows - small.shape[0]))
    small = small.reshape(shard_rows, small_cols)
    small_at = M_SHARE
    ms_cols = -(-(small_at + small_cols) // LANES) * LANES
    a_cols, b_cols = lin_cols + ms_cols, c_cols

    def early_columns(half):
        return jnp.concatenate(
            [
                attn_in_weight[:, half * q_cols : (half + 1) * q_cols],
                attn_in_weight[:, QH * HD + half * HD : QH * HD + (half + 1) * HD],
                attn_in_weight[:, (QH + KVH + half) * HD : (QH + KVH + half + 1) * HD],
                step_weight[:, half * M_SHARE : (half + 1) * M_SHARE],
                small,
                jnp.zeros((shard_rows, ms_cols - small_at - small_cols), BF16),
                mixer_in_weight[:, half * m_cols : (half + 1) * m_cols],
                mixer_in_weight[:, SH * SHD + half * NS : SH * SHD + (half + 1) * NS],
            ],
            axis=1,
        )

    def sorted_halves(columns):
        halves = (columns(0), columns(1))
        kept = place.by_core(*halves)
        got = place.swap(place.by_core(halves[1], halves[0]))
        return jnp.concatenate([place.by_core(kept, got), place.by_core(got, kept)], axis=0)

    early = place.spread_z(sorted_halves(early_columns))

    def side_by_side(weight):
        return weight.reshape(2, shard_rows, width).transpose(1, 0, 2).reshape(shard_rows, 2 * width)

    out_weights = jnp.concatenate([attn_out_weight, mixer_out_weight], axis=0)
    middle = jnp.concatenate([zgate_weight, side_by_side(out_weights)], axis=1)
    middle = lax.all_gather(middle, AXES, axis=0, tiled=True)
    ff_all = jnp.concatenate([gate_weight, up_weight, side_by_side(down_weight)], axis=1)
    early = place.place_z(early, [[(0, a_cols, 2)], [(a_cols, b_cols, 2)]])
    early = place.plane_second(place.plane_first(early))
    w_a, w_b = place.plane_third(early, [(0, 0, a_cols, 0, 0), (1, 0, b_cols, 1, 0)])
    tail_at = lin_cols
    vectors = w_a[:, tail_at + small_at : tail_at + small_at + small_cols]
    vectors = vectors.reshape(devices, -1).astype(F32)
    sizes = [input_gain.shape[0], mixer_gain.shape[0], post_gain.shape[0], conv_bias.shape[0]]
    ends = [sum(sizes[: k + 1]) for k in range(4)]
    gain_in = vectors[:, : ends[0]].reshape(-1)
    gain_mixer = vectors[:, ends[0] : ends[1]].reshape(-1)
    gain_mixer = place.by_core(gain_mixer[:m_cols], gain_mixer[m_cols:])
    gain_post = vectors[:, ends[1] : ends[2]].reshape(-1)
    shift_all = vectors[:, ends[2] : ends[3]].reshape(-1)
    taps_all = vectors[:, ends[3] : vector_size].reshape(devices, KC, sizes[3])
    taps_all = jnp.transpose(taps_all, (1, 0, 2)).reshape(KC, -1)

    def conv_half(value):
        first = jnp.concatenate(
            [value[..., :m_cols], value[..., 2 * m_cols : 2 * m_cols + NS]], axis=-1
        )
        second = jnp.concatenate(
            [value[..., m_cols : 2 * m_cols], value[..., 2 * m_cols + NS :]], axis=-1
        )
        return place.by_core(first, second)

    taps, shift = conv_half(taps_all), conv_half(shift_all)
    terms = vectors[:groups, vector_size : vector_size + 3 * term_size]
    terms = terms.reshape(groups, 3, 3, SH // groups)
    terms = terms[:, 0] + terms[:, 1] + terms[:, 2]
    terms = jnp.transpose(terms, (1, 0, 2)).reshape(3, SH)
    terms = place.by_core(terms[:, :M_SHARE], terms[:, M_SHARE:])
    bias, log_rates, skip = terms[0], terms[1], terms[2]
    rates = -jnp.exp(log_rates)

    scale_in = inverse_rms(tokens)
    normed = (tokens * scale_in * gain_in).astype(BF16).reshape(rows_halo, width)

    def body_rows(value):
        return value.reshape(CORES, slots, piece + HALO, -1)[:, :, HALO:]

    linear = body_rows(mm(normed, w_a[:, :lin_cols]))
    mixed = mm(normed, w_b).astype(BF16).reshape(CORES, slots, piece + HALO, c_cols)
    step_raw = mm(normed, w_a[:, tail_at:]).astype(BF16)

    def rows_plan(source, start, pieces_of):
        found = []
        for device in range(devices // 2):
            for first, count, output, to, pitch in pieces_of:
                side, row = divmod(first, shard_rows)

                def where(at, device=device, side=side, row=row, count=count):
                    first = (at[3] * (devices // 2) + device) * shard_rows + row
                    return pl.ds(first, count), pl.ds(start + side * width, width)

                def goal(at, device=device, to=to, pitch=pitch, count=count):
                    return pl.ds(device * pitch + to, count), pl.ds(0, width)

                found.append((source, where, output, goal))
        return found

    def columns_plan(source, start, size, output):
        def where(at):
            return pl.ds(0, width), pl.ds(pl.multiple_of(start + at[3] * size, LANES), size)

        return [(source, where, output, lambda at: (pl.ds(0, width), pl.ds(0, size)))]

    low = jax.ShapeDtypeStruct
    w_z, w_attn_out, w_mixer_out = moved(
        place,
        [middle],
        [low((width, m_cols), BF16), low((q_cols, width), BF16), low((m_cols, width), BF16)],
        columns_plan(0, 0, m_cols, 0)
        + rows_plan(
            0,
            2 * m_cols,
            [
                (0, out_rows, 1, 0, out_rows),
                (out_rows, shard_rows - out_rows, 2, 0, mix_rows),
                (shard_rows, shard_rows, 2, shard_rows - out_rows, mix_rows),
            ],
        ),
    )
    cos_part, sin_part = rotary_tables(positions, HD)
    cos_part, sin_part = cos_part[:, None, :, None], sin_part[:, None, :, None]
    queries = rotate(
        linear[..., :q_cols].reshape(CORES, slots, piece, Q_SHARE, HD), cos_part, sin_part
    ).astype(BF16)
    keys = rotate(
        linear[..., q_cols : q_cols + HD][..., None, :], cos_part, sin_part
    ).astype(BF16)[..., 0, :]
    kv_own = jnp.concatenate([keys, linear[..., q_cols + HD :].astype(BF16)], axis=-1)
    kv_parts = [part.reshape(-1, 2 * HD) for part in place.spread_z(kv_own)]
    plan = []
    for r in range(groups):
        for e in range(CORES):
            for s in range(slots):

                def source(at, e=e, s=s):
                    return pl.ds((e * slots + s) * piece, piece), pl.ds(0, 2 * HD)

                def goal(at, r=r, e=e):
                    z = lax.rem(at[2] + groups - r, groups)
                    h = lax.rem(at[3] + e, CORES)
                    return pl.ds((h * groups + z) * piece, piece), pl.ds(0, 2 * HD)

                plan.append((r, source, s, goal))
    kv_size = jax.ShapeDtypeStruct((CORES * groups * piece, 2 * HD), BF16)
    kv = moved(place, kv_parts, [kv_size] * slots, plan)
    kv = place.plane_first(kv)
    scale = HD ** (-0.5)
    queries = (queries * jnp.asarray(scale, BF16)).reshape(CORES, slots, piece, q_cols)
    pre = shift
    for tap in range(KC):
        first = HALO - KC + 1 + tap
        pre = pre + taps[tap] * mixed[:, :, first : first + piece].astype(F32)
    conv_out = jax.nn.silu(pre).astype(BF16)
    features = conv_out[..., :m_cols].reshape(CORES * slots, piece, m_cols)
    shared = conv_out[..., m_cols:]
    shared_other = place.swap(shared)[::-1]
    inject = place.by_core(shared, shared_other).reshape(CORES * slots, piece, NS)
    readout = place.by_core(shared_other, shared).reshape(CORES * slots, piece, NS)
    raw = step_raw.reshape(CORES * slots, piece + HALO, ms_cols)
    bias_row = jnp.pad(bias, (0, LANES - M_SHARE))[None]
    rate_row = jnp.pad(rates, (0, LANES - M_SHARE))[None]
    skip_row = jnp.repeat(skip, SHD)[None]
    pieces = CORES * slots
    chunk_args = [
        features, inject, readout, raw, bias_row, rate_row, skip_row,
    ]
    share_rows = m_cols // groups
    held = pltpu.VMEM((groups, share_rows, NS), BF16)
    held_more = pltpu.VMEM((groups, share_rows + EXTRA, NS), BF16)
    within, logs, *local = over_pieces(
        chunk_kernel,
        "chunk",
        chunk_args,
        range(4, 7),
        [
            ((pieces, piece, m_cols), F32),
            ((pieces, piece, LANES), F32),
            *[((pieces, share_rows + EXTRA, NS), BF16)] * groups,
        ],
        9,
        at,
        [held_more],
    )
    local = [part.reshape(CORES, slots, share_rows + EXTRA, NS) for part in local]
    held_back = {"kv": kv}

    def before_states(parts):
        parts, held_back["kv"], columns = tie(parts, held_back["kv"], ff_all)
        held_back["ff"] = lax.all_gather(columns, AXES, axis=0, tiled=True)
        held_back["kv"] = place.plane_second(held_back["kv"])
        return parts

    def between_states(totals):
        totals, held_back["kv"] = tie(totals, held_back["kv"])
        return totals

    def after_states(entering):
        entering, held_back["queries"] = tie(entering, queries)
        return entering

    state_in, marks, fades = carried(
        place, at, local, None, None, False, before_states, between_states, after_states
    )
    queries = held_back["queries"]
    rows = chips * CORES * groups * piece
    (kv,) = place.plane_third(
        held_back["kv"], [(s, 0, 2 * HD, 0, 0, s * rows) for s in range(slots)]
    )
    kv = kv.reshape(slots, rows, 2 * HD)
    ff_whole = held_back["ff"]
    w_gate, w_up, w_down = moved(
        place,
        [ff_whole],
        [low((width, ff_half), BF16), low((width, ff_half), BF16), low((ff_half, width), BF16)],
        columns_plan(0, 0, ff_half, 0)
        + columns_plan(0, 2 * ff_half, ff_half, 1)
        + rows_plan(
            0,
            4 * ff_half,
            [
                (0, shard_rows, 2, 0, ff_rows),
                (shard_rows, shard_rows, 2, shard_rows, ff_rows),
            ],
        ),
    )

    heads_out, lse = attend(pieces_at, lengths, queries, kv, piece)
    attended = heads_out.reshape(rows_all, q_cols)
    attended, state_in = tie(attended, state_in)
    (ssd,) = over_pieces(
        carry_kernel,
        "carry",
        [within, readout, logs, *state_in],
        (),
        [((pieces, piece, m_cols), BF16)],
        5,
        at,
        [held],
    )
    ssd = ssd.reshape(CORES, slots, piece, m_cols).astype(F32)
    zgate = body_rows(mm(normed, w_z).astype(BF16))
    gate_value, gate_slope = silu_and_slope(zgate.astype(F32))
    gated_raw = ssd * gate_value
    squares = jnp.sum(gated_raw * gated_raw, axis=-1)
    squares = squares + place.swap(squares)[::-1]
    scale_mixer = lax.rsqrt(squares / (SH * SHD) + 1e-05)[..., None]
    gated = (gated_raw * scale_mixer * gain_mixer).astype(BF16).reshape(rows_all, m_cols)

    def own_sum(partial):
        partial = partial.reshape(CORES, -1, partial.shape[-1])
        return partial[0] + place.swap(partial[1].astype(BF16)).astype(F32)

    def with_other(value):
        return jnp.stack([value, place.swap(value)]).reshape(-1, value.shape[-1])

    mixers = own_sum(mm(attended, w_attn_out) + mm(gated, w_mixer_out))
    residual = tokens[0][:, HALO:].reshape(-1, width) + mixers
    scale_post = inverse_rms(residual)
    post = with_other((residual * scale_post * gain_post).astype(BF16))
    gate_lin = mm(post, w_gate)
    up_lin = mm(post, w_up)
    gate_act, gate_act_slope = silu_and_slope(gate_lin)
    hidden = (gate_act * up_lin).astype(BF16)
    valid_own = valid[0].reshape(-1, 1)
    layer_out = (valid_own * (residual + own_sum(mm(hidden, w_down)))).astype(BF16)

    dhidden = mm(dy, w_down, NT)
    dgate = (dhidden * up_lin * gate_act_slope).astype(BF16)
    dup = (dhidden * gate_act).astype(BF16)

    def own_parity(grad):
        grad = grad.astype(BF16).reshape(chips // 2, CORES, -1, width)
        kept = lax.dynamic_index_in_dim(grad, core, 1, False)
        got = place.swap(lax.dynamic_index_in_dim(grad, 1 - core, 1, False))
        grad = jnp.concatenate([place.by_core(kept, got), place.by_core(got, kept)], axis=0)
        return grad.reshape(-1, width)

    dpost = own_sum(mm(dgate, w_gate, NT) + mm(dup, w_up, NT))
    dresidual = dy_own.reshape(-1, width) + rms_back(residual, scale_post, gain_post, dpost)
    grad_post_gain = jnp.sum(dpost * residual * scale_post, axis=0)
    dmix = with_other(dresidual.astype(BF16))

    dattended = mm(dmix, w_attn_out, NT).astype(BF16)
    dgated = mm(dmix, w_mixer_out, NT).reshape(CORES, slots, piece, m_cols)
    scaled = dgated * gain_mixer
    inner = jnp.sum(scaled * gated_raw, axis=-1)
    inner = (inner + place.swap(inner)[::-1])[..., None] / (SH * SHD)
    dgated_raw = scale_mixer * scaled - gated_raw * (scale_mixer**3 * inner)
    grad_mixer_gain = jnp.sum(dgated * gated_raw * scale_mixer, axis=(0, 1, 2))
    dssd = (dgated_raw * gate_value).astype(BF16).reshape(pieces, piece, m_cols)
    dzgate = (dgated_raw * ssd * gate_slope).astype(BF16)

    def halo_rows(value):
        value = value.reshape(CORES, slots, piece, -1)
        return jnp.pad(value, ((0, 0), (0, 0), (HALO, 0), (0, 0)))

    dzgate = halo_rows(dzgate).reshape(rows_halo, m_cols)

    direct = over_pieces(
        direct_kernel,
        "direct",
        [dssd, readout, logs],
        (),
        [((pieces, share_rows, NS), BF16)] * groups,
        5,
        at,
        [held],
    )
    direct = [part.reshape(CORES, slots, share_rows, NS) for part in direct]
    dgate, dup, hidden, direct = tie(dgate, dup, hidden, direct)
    ff_grads, ff_start = place.stack_far(
        [
            mm(post, dgate, TN).astype(BF16),
            mm(post, dup, TN).astype(BF16),
            own_parity(mm(hidden, dy, TN)),
        ]
    )
    out_side = {}

    def before_scan(parts):
        parts, flat = tie(parts, ff_grads)
        out_side["ff"] = ff_start(flat)
        return parts

    def between_scans(totals):
        totals, out_side["dz"], dmix_late = tie(totals, dzgate, dmix)
        grad_outs = jnp.concatenate(
            [
                mm(attended, dmix_late, TN).astype(BF16).reshape(devices // 2, out_rows, width),
                mm(gated, dmix_late, TN).astype(BF16).reshape(devices // 2, mix_rows, width),
            ],
            axis=1,
        )
        wide_dz = jnp.pad(out_side["dz"], ((0, 0), (0, width - m_cols)))
        mid_grads, mid_start = place.stack_far(
            [own_parity(grad_outs), mm(normed, wide_dz, TN).astype(BF16)]
        )
        totals, mid_grads = tie(totals, mid_grads)
        out_side["mid"] = mid_start(mid_grads)
        return totals

    def after_scans(entering):
        entering, out_side["dattended"] = tie(entering, dattended)
        return entering

    later, _, _ = carried(
        place, at, direct, marks, fades, True, before_scan, between_scans, after_scans
    )
    ff_grads, mid_grads = out_side["ff"], out_side["mid"]
    dattended = out_side["dattended"]
    dnormed = mm(out_side["dz"], w_z, NT)

    dqueries, dkv = attend_back(
        pieces_at,
        lengths,
        queries,
        kv,
        heads_out,
        dattended.reshape(heads_out.shape),
        lse,
        piece,
    )
    dkv, later = tie(dkv, later)
    dkv = [
        place.reduce_first(dkv[s].reshape(na, nb, CORES, groups, piece, 2 * HD), s % 2 == 0)
        for s in range(slots)
    ]

    dfeatures, dinject, dreadout, draw, sums = over_pieces(
        chunk_back_kernel,
        "chunk_back",
        chunk_args + [dssd, *state_in, *later],
        range(4, 7),
        [
            ((pieces, piece, m_cols), F32),
            ((pieces, piece, NS), F32),
            ((pieces, piece, NS), F32),
            ((pieces, piece, LANES), F32),
            ((pieces, 8, LANES), F32),
        ],
        28,
        at,
        [pltpu.VMEM((LANES, 2 * LANES), F32), pltpu.VMEM((piece, LANES), F32), held, held],
    )
    ff_grads, dkv, dfeatures = tie(ff_grads, dkv, dfeatures)
    dkv = [place.reduce_second(dkv[s], s % 2 == 0) for s in range(slots)]
    dinject = dinject.reshape(CORES, slots, piece, NS)
    dreadout = dreadout.reshape(CORES, slots, piece, NS)
    dshared = place.by_core(dinject, dreadout) + place.swap(
        place.by_core(dreadout, dinject).astype(BF16)
    )[::-1].astype(F32)
    dmixed, conv_sums = over_pieces(
        conv_back_kernel,
        "conv_back",
        [
            mixed.reshape(pieces, piece + HALO, c_cols),
            dfeatures,
            dshared.reshape(pieces, piece, NS),
            taps,
            shift[None],
        ],
        range(3, 5),
        [((pieces, piece + HALO, c_cols), BF16), ((pieces, 8, c_cols), F32)],
        6,
        at,
    )
    conv_sums = jnp.sum(conv_sums, axis=0)
    grad_taps, grad_shift = conv_sums[:KC], conv_sums[KC]

    def by_columns(grad):
        return grad.reshape(na, nb, CORES, groups, shard_rows, grad.shape[-1])


    dstep = draw[..., :M_SHARE].astype(BF16)
    db_low = dmixed.reshape(rows_halo, b_cols)
    dkv, db_low = tie(dkv, db_low)
    grad_b = place.reduce_first(by_columns(mm(normed, db_low, TN)), False)
    dkv_own = place.reduce_z(dkv)
    dnormed = dnormed + mm(db_low, w_b, NT)
    head_sums = place.sum_along(jnp.sum(sums, axis=0)[:3, :M_SHARE], "z")
    dkv_own, grad_b, dnormed, head_sums, ff_grads, mid_grads = tie(
        dkv_own, grad_b, dnormed, head_sums, ff_grads, mid_grads
    )
    far_grads = place.finish_far([ff_grads, mid_grads], [[2, 2, 1], [1, 2]])
    dkv_own = jnp.stack([part.reshape(CORES, piece, 2 * HD) for part in dkv_own], axis=1)
    dkv_own = place.by_core(dkv_own, dkv_own[::-1])
    grad_b = place.reduce_second(grad_b, False)
    dq_rows = (dqueries * scale).reshape(CORES, slots, piece, Q_SHARE, HD)
    dq_rows = rotate(dq_rows, cos_part, -sin_part).reshape(CORES, slots, piece, q_cols)
    dk_rows = rotate(dkv_own[..., None, :HD], cos_part, -sin_part)[..., 0, :]
    tail_zeros = jnp.zeros((CORES, slots, piece, ms_cols - M_SHARE), BF16)
    dlin = jnp.concatenate([dq_rows, dk_rows, dkv_own[..., HD:]], axis=-1).astype(BF16)
    da_low = halo_rows(
        jnp.concatenate(
            [dlin, dstep.reshape(CORES, slots, piece, -1), tail_zeros], axis=-1
        )
    ).reshape(rows_halo, a_cols)
    dnormed = dnormed + mm(da_low, w_a, NT)
    grad_input_gain = jnp.sum(
        dnormed.reshape(CORES, slots, piece + HALO, width) * (tokens * scale_in), axis=(0, 1, 2)
    )
    dnormed = own_sum(dnormed).reshape(slots, piece + HALO, width)
    rim_back = lax.ppermute(
        dnormed[:, HALO - KC + 1 : HALO].astype(BF16),
        AXES,
        [(i + 1, i) for i in range(devices - 1)],
    ).astype(F32)
    dnormed = dnormed[:, HALO:] + jnp.pad(rim_back, ((0, 0), (piece - KC + 1, 0), (0, 0)))
    own, own_scale = tokens[0][:, HALO:], scale_in[0][:, HALO:]
    input_grad = dresidual.reshape(slots, piece, width) + rms_back(
        own, own_scale, gain_in, dnormed
    )

    zero_half = jnp.zeros((m_cols,), F32)

    def conv_whole(value):
        none = jnp.zeros_like(value)
        first, second = place.by_core(value, none), place.by_core(none, value)
        return jnp.concatenate(
            [first[..., :m_cols], second[..., :m_cols], first[..., m_cols:], second[..., m_cols:]],
            axis=-1,
        )

    grad_mixer_gain = jnp.concatenate(
        [place.by_core(grad_mixer_gain, zero_half), place.by_core(zero_half, grad_mixer_gain)]
    )
    grad_taps = conv_whole(grad_taps).reshape(KC, devices, -1)
    vector_grads = jnp.concatenate(
        [
            grad_input_gain.reshape(devices, -1),
            grad_mixer_gain.reshape(devices, -1),
            grad_post_gain.reshape(devices, -1),
            conv_whole(grad_shift).reshape(devices, -1),
            jnp.transpose(grad_taps, (1, 0, 2)).reshape(devices, -1),
        ],
        axis=1,
    )
    vector_grads = jnp.pad(
        vector_grads, ((0, 0), (0, small_cols * shard_rows - vector_size))
    ).reshape(width, small_cols)
    grad_a = mm(normed, da_low, TN)
    grad_a = grad_a + jnp.pad(
        vector_grads,
        ((0, 0), (tail_at + small_at, a_cols - tail_at - small_at - small_cols)),
    )
    grad_a, grad_b = tie(grad_a, grad_b)
    grad_b = place.reduce_z([grad_b])[0]
    grad_a = place.reduce_first(by_columns(grad_a), True)
    head_sums = place.sum_along(head_sums, "b")
    grad_a, grad_b, head_sums = tie(grad_a, grad_b, head_sums)
    grad_a = place.reduce_second(grad_a, True)
    head_sums = place.sum_along(head_sums, "a")
    grad_a, head_sums = tie(grad_a, head_sums)
    (grad_a,) = place.reduce_z([grad_a])
    other_sums = place.swap(head_sums)
    head_sums = jnp.concatenate(
        [place.by_core(head_sums, other_sums), place.by_core(other_sums, head_sums)], axis=1
    )
    head_sums = lax.dynamic_slice_in_dim(head_sums, place.at["z"] * (SH // groups), SH // groups, 1)

    def between_cores(columns):
        columns = columns.reshape(CORES, shard_rows, -1)
        kept = lax.dynamic_index_in_dim(columns, core, 0, False)
        got = place.swap(lax.dynamic_index_in_dim(columns, 1 - core, 0, False))
        return place.by_core(kept, got), place.by_core(got, kept)

    part = far_grads.shape[0] // 5
    far_grads = [far_grads[k * part : (k + 1) * part] for k in range(5)]
    both = between_cores(jnp.concatenate([far_grads[0], far_grads[1], far_grads[4]], axis=1))
    grad_gate = jnp.concatenate([half[:, :ff_half] for half in both], axis=1).astype(F32)
    grad_up = jnp.concatenate([half[:, ff_half : 2 * ff_half] for half in both], axis=1)
    grad_up = grad_up.astype(F32)
    grad_down = far_grads[2].astype(F32)
    grad_outs = far_grads[3].astype(F32)
    grad_zgate = jnp.concatenate(
        [half[:, 2 * ff_half : 2 * ff_half + m_cols] for half in both], axis=1
    ).astype(F32)
    conv_first, conv_second = between_cores(grad_b)
    first, second = between_cores(grad_a)

    def both_halves(start, size):
        return jnp.concatenate([first[:, start : start + size], second[:, start : start + size]], 1)

    grad_attn_in = jnp.concatenate(
        [both_halves(0, q_cols), both_halves(q_cols, HD), both_halves(q_cols + HD, HD)], axis=1
    )
    grad_mixer_in = jnp.concatenate(
        [conv_first[:, :m_cols], conv_second[:, :m_cols], conv_first[:, m_cols:], conv_second[:, m_cols:]],
        axis=1,
    )
    grad_step = both_halves(lin_cols, M_SHARE)
    small_at = lin_cols + small_at
    small_sum = (first + second)[:, small_at : small_at + small_cols].reshape(-1)

    return (
        layer_out.reshape(slots, piece, width),
        input_grad,
        small_sum[: ends[0]],
        grad_attn_in,
        grad_outs[:out_rows],
        grad_zgate,
        grad_mixer_in,
        grad_step,
        small_sum[ends[3] : vector_size].reshape(KC, -1),
        small_sum[ends[2] : ends[3]],
        head_sums[0],
        head_sums[1],
        head_sums[2],
        small_sum[ends[0] : ends[1]],
        grad_outs[out_rows:],
        small_sum[ends[1] : ends[2]],
        grad_gate,
        grad_up,
        grad_down,
    )


def solution(mesh):
    rows, columns, vector = P(AXES, None), P(None, AXES), P(AXES)
    tokens, heads = P(None, AXES, None), P("sp")
    in_specs = (
        tokens,
        tokens,
        P(),
        vector,
        rows,
        rows,
        rows,
        rows,
        rows,
        columns,
        vector,
        heads,
        heads,
        heads,
        vector,
        rows,
        vector,
        rows,
        rows,
        rows,
    )
    out_specs = (
        tokens,
        tokens,
        vector,
        rows,
        rows,
        rows,
        rows,
        rows,
        columns,
        vector,
        heads,
        heads,
        heads,
        vector,
        rows,
        vector,
        rows,
        rows,
        rows,
    )
    return jax.shard_map(shards, mesh=mesh, in_specs=in_specs, out_specs=out_specs, check_vma=False)
```

```python
import functools
import math

import jax
import jax.numpy as jnp
from jax import lax
from jax.experimental import pallas as pl
from jax.experimental.pallas import tpu as pltpu
from jax.sharding import PartitionSpec as P

QH = 8
KVH = 2
HD = 64
SH = 24
SHD = 64
NS = 128
KC = 4
CORES = 2
MASKED = -1e30
AXES = ("ctx", "sp")
F32 = jnp.float32
BF16 = jnp.bfloat16
LANES = 128
HALO = 8
EXTRA = 16
Q_SHARE = QH // CORES
M_SHARE = SH // CORES
VMEM = 56 * 2**20

NT = (((1,), (1,)), ((), ()))
TN = (((0,), (0,)), ((), ()))
NN = (((1,), (0,)), ((), ()))


def mm(left, right, dims=NN, precision=None):
    return lax.dot_general(
        left, right, dims, precision=precision, preferred_element_type=F32
    )


def tie(*values):
    return lax.optimization_barrier(values)


def cost(micros):
    return pl.CostEstimate(flops=int(micros * 1.15e9), bytes_accessed=0, transcendentals=0)


class Place:
    def __init__(self):
        ctx = lax.axis_size("ctx")
        groups = lax.axis_size("sp")
        chips = ctx // CORES
        nb = math.isqrt(chips)
        self.size = {"a": chips // nb, "b": nb, "z": groups, "c": CORES}
        self.devices = ctx * groups
        index = lax.axis_index("ctx")
        self.at = {
            "a": index // CORES // nb,
            "b": (index // CORES) % nb,
            "z": lax.axis_index("sp"),
            "c": index % CORES,
        }
        self.chip = index // CORES
        self.chips = chips
        self.scalars = jnp.stack(
            [self.at["a"], self.at["b"], self.at["z"], self.at["c"], self.chip]
        ).astype(jnp.int32)
        self.flat = index * groups + self.at["z"]

    def flat_of(self, a, b, z, c):
        return ((a * self.size["b"] + b) * CORES + c) * self.size["z"] + z

    def pairs(self, dim, by):
        found = []
        for a in range(self.size["a"]):
            for b in range(self.size["b"]):
                for z in range(self.size["z"]):
                    for c in range(CORES):
                        spot = {"a": a, "b": b, "z": z, "c": c}
                        goal = dict(spot)
                        goal[dim] = (spot[dim] + by) % self.size[dim]
                        found.append((self.flat_of(**spot), self.flat_of(**goal)))
        return found

    def shift(self, x, dim, by):
        return lax.ppermute(x, AXES, self.pairs(dim, by))

    def swap(self, x):
        return self.shift(x, "c", 1)

    def by_core(self, zero, one):
        return jnp.where(self.at["c"] == 0, zero, one)

    def chip_pairs(self, by):
        groups = self.size["z"]
        return [
            ((chip * CORES + c) * groups + z, (((chip + by) % self.chips) * CORES + c) * groups + z)
            for chip in range(self.chips)
            for c in range(CORES)
            for z in range(groups)
        ]

    def spread_z(self, x):
        return [x] + [self.shift(x, "z", k) for k in range(1, self.size["z"])]

    def plane_first(self, halves):
        found = []
        for index, half in enumerate(halves):
            dim = "ab"[index % 2 == 0]
            found.append([half] + [self.shift(half, dim, k) for k in range(1, self.size[dim])])
        return found

    def plane_second(self, halves):
        found = []
        for index, parts in enumerate(halves):
            dim = "ba"[index % 2 == 0]
            moves = range(1, self.size[dim])
            found.append([parts] + [[self.shift(part, dim, k) for part in parts] for k in moves])
        return found

    def place_z(self, parts, halves):
        groups = self.size["z"]
        rows = parts[0].shape[0]
        outs = [
            jax.ShapeDtypeStruct((groups * rows, sum(size for _, size, _ in half)), parts[0].dtype)
            for half in halves
        ]
        plan = []
        for index, half in enumerate(halves):
            to = 0
            for start, size, count in half:
                block = rows // count
                for r in range(groups):
                    for m in range(count):

                        def source(at, m=m, start=start, size=size, block=block):
                            return pl.ds(m * block, block), pl.ds(start, size)

                        def goal(at, m=m, r=r, to=to, size=size, block=block):
                            z = lax.rem(at[2] + groups - r, groups)
                            return pl.ds((m * groups + z) * block, block), pl.ds(to, size)

                        plan.append((r, source, index, goal))
                to += size
        return moved(self, parts, outs, plan)

    def plane_third(self, halves, wanted):
        rows, dtype = halves[0][0][0].shape[0], halves[0][0][0].dtype
        na, nb = self.size["a"], self.size["b"]
        keys = [(da, db) for da in range(na) for db in range(nb)]
        widths = {}
        heights = {}
        for _, _, size, array, column, *base in wanted:
            widths[array] = max(widths.get(array, 0), column + size)
            heights[array] = max(heights.get(array, 0), sum(base) + self.chips * rows)
        outs = [jax.ShapeDtypeStruct((heights[k], widths[k]), dtype) for k in range(len(widths))]
        sources = []
        for index, half in enumerate(halves):
            sources += [half[da][db] if index % 2 == 0 else half[db][da] for da, db in keys]
        plan = []
        for half, start, size, array, column, *base in wanted:
            for index, (da, db) in enumerate(keys):

                def source(at, start=start, size=size):
                    return pl.ds(0, rows), pl.ds(start, size)

                def goal(at, da=da, db=db, column=column, size=size, base=sum(base)):
                    chip = lax.rem(at[0] + na - da, na) * nb + lax.rem(at[1] + nb - db, nb)
                    return pl.ds(base + chip * rows, rows), pl.ds(column, size)

                plan.append((half * len(keys) + index, source, array, goal))
        return moved(self, sources, outs, plan)

    def stack_far(self, grads):
        cores = [[chip * CORES + c for chip in range(self.chips)] for c in range(CORES)]
        chips = self.chips
        rows, wide = grads[0].shape[0] // chips, grads[0].shape[1]
        high = len(grads) * rows
        plan = []
        for k in range(len(grads)):
            for chip in range(chips):

                def source(at, chip=chip):
                    return pl.ds(chip * rows, rows), pl.ds(0, wide)

                def goal(at, chip=chip, row=k * rows):
                    return pl.ds(chip * high + row, rows), pl.ds(0, wide)

                plan.append((k, source, 0, goal))
        (flat,) = moved(self, grads, [jax.ShapeDtypeStruct((chips * high, wide), BF16)], plan)

        def start(flat):
            return lax.psum_scatter(
                flat, "ctx", scatter_dimension=0, tiled=True, axis_index_groups=cores
            )

        return flat, start

    def finish_far(self, flats, counts):
        groups, wide = self.size["z"], flats[0].shape[1]
        height = sum(flat.shape[0] for flat in flats)
        deep = height // groups
        plan, to = [], 0
        for index, (flat, ms) in enumerate(zip(flats, counts)):
            share = flat.shape[0] // len(ms)
            for k, count in enumerate(ms):
                block = share // groups // count
                for z in range(groups):
                    for m in range(count):

                        def source(at, row=k * share + (m * groups + z) * block, block=block):
                            return pl.ds(row, block), pl.ds(0, wide)

                        def goal(at, row=z * deep + to + m * block, block=block):
                            return pl.ds(row, block), pl.ds(0, wide)

                        plan.append((index, source, 0, goal))
                to += share // groups
        (flat,) = moved(self, flats, [jax.ShapeDtypeStruct((height, wide), BF16)], plan)
        return lax.psum_scatter(flat, "sp", scatter_dimension=0, tiled=True)

    def reduce(self, x, dim, axis):
        n, v = self.size[dim], self.at[dim]
        total = lax.dynamic_index_in_dim(x, v, axis, False).astype(F32)
        for k in range(1, n):
            piece = lax.dynamic_index_in_dim(x, (v + k) % n, axis, False).astype(BF16)
            total = total + self.shift(piece, dim, k).astype(F32)
        return total

    def reduce_first(self, grad, b_first):
        return self.reduce(grad, "a", 0) if b_first else self.reduce(grad, "b", 1)

    def reduce_second(self, grad, b_first):
        return self.reduce(grad, "b" if b_first else "a", 0)

    def reduce_z(self, left):
        n, v = self.size["z"], self.at["z"]

        def cut(x, index):
            piece = lax.dynamic_index_in_dim(x, index, 1, False)
            return piece.reshape(-1, piece.shape[-1])

        totals = [cut(x, v) for x in left]
        for k in range(1, n):
            sent = jnp.concatenate([cut(x, (v + k) % n).astype(BF16) for x in left], axis=-1)
            got = self.shift(sent, "z", k).astype(F32)
            start = 0
            for index, total in enumerate(totals):
                stop = start + total.shape[-1]
                totals[index] = total + got[:, start:stop]
                start = stop
        return totals

    def sum_step(self, x, dim, step):
        found = []
        for a in range(self.size["a"]):
            for b in range(self.size["b"]):
                for z in range(self.size["z"]):
                    for c in range(CORES):
                        spot = {"a": a, "b": b, "z": z, "c": c}
                        goal = dict(spot)
                        goal[dim] = spot[dim] ^ step
                        found.append((self.flat_of(**spot), self.flat_of(**goal)))
        return x + lax.ppermute(x, AXES, found)

    def sum_along(self, x, dims):
        for dim in dims:
            step = 1
            while step < self.size[dim]:
                x = self.sum_step(x, dim, step)
                step *= 2
        return x


def moved_kernel(at_ref, *refs, plan, count):
    sems = refs[-1]
    copies = [
        pltpu.make_async_copy(
            refs[source].at[where(at_ref)], refs[count + goal].at[to(at_ref)], sems.at[index]
        )
        for index, (source, where, goal, to) in enumerate(plan)
    ]
    for copy in copies:
        copy.start()
    for copy in copies:
        copy.wait()


def moved(place, sources, outs, plan):
    size = sum(math.prod(out.shape) * out.dtype.itemsize for out in outs)
    return pl.pallas_call(
        functools.partial(moved_kernel, plan=plan, count=len(sources)),
        in_specs=[pl.BlockSpec(memory_space=pltpu.SMEM)]
        + [pl.BlockSpec(memory_space=pl.ANY)] * len(sources),
        out_specs=[pl.BlockSpec(memory_space=pltpu.VMEM)] * len(outs),
        out_shape=outs,
        scratch_shapes=[pltpu.SemaphoreType.DMA((len(plan),))],
        compiler_params=pltpu.CompilerParams(vmem_limit_bytes=VMEM),
        cost_estimate=pl.CostEstimate(flops=0, bytes_accessed=2 * size, transcendentals=0),
        name="moved",
    )(place.scalars, *sources)


def rotary_tables(positions, width):
    half_width = width // 2
    inverse = 100000000000.0 ** (-jnp.arange(half_width, dtype=F32) * 2.0 / width)
    angles = positions.astype(F32)[..., None] * inverse
    return (jnp.cos(angles), jnp.sin(angles))


def rotate(value, cos_part, sin_part):
    half_width = value.shape[-1] // 2
    first = value[..., :half_width]
    second = value[..., half_width:]
    return jnp.concatenate(
        [first * cos_part - second * sin_part, second * cos_part + first * sin_part], axis=-1
    )


def inverse_rms(value):
    return lax.rsqrt(jnp.mean(value * value, axis=-1, keepdims=True) + 1e-05)


def rms_back(value, scale, gain, grad):
    scaled = grad * gain
    inner = jnp.mean(scaled * value, axis=-1, keepdims=True)
    return scale * scaled - value * (scale * scale * scale * inner)


def silu_and_slope(value):
    gate = jax.nn.sigmoid(value)
    out = value * gate
    return out, gate + out * (1.0 - gate)


def causal_keep(first_key, first_query, keys, piece, columns):
    key = first_key + lax.broadcasted_iota(jnp.int32, (keys, columns), 0)
    column = lax.broadcasted_iota(jnp.int32, (keys, columns), 1)
    head = sum((column >= piece * k).astype(jnp.int32) for k in range(1, columns // piece))
    return key <= first_query + column - head * piece


def stack_heads(block, high):
    found = []
    for head in range(Q_SHARE):
        pair = block[:, head // 2 * LANES : (head // 2 + 1) * LANES].astype(F32)
        if (head % 2 == 1) != high:
            pair = pltpu.roll(pair, HD, 1)
        lane = lax.broadcasted_iota(jnp.int32, pair.shape, 1)
        found.append(jnp.where((lane >= HD) if high else (lane < HD), pair, 0.0))
    return jnp.concatenate(found, axis=0).astype(BF16)


def unstack_heads(stacked, piece, high):
    found = []
    for pair in range(Q_SHARE // 2):
        first = stacked[2 * pair * piece : (2 * pair + 1) * piece]
        second = stacked[(2 * pair + 1) * piece : (2 * pair + 2) * piece]
        if high:
            first = pltpu.roll(first, HD, 1)
        else:
            second = pltpu.roll(second, HD, 1)
        lane = lax.broadcasted_iota(jnp.int32, first.shape, 1)
        found.append(jnp.where(lane < HD, first, second))
    return jnp.concatenate(found, axis=1)


def attend_kernel(places, lengths, q_ref, kv_ref, out_ref, lse_ref, acc, top, total, held, *, piece):
    slot, which = pl.program_id(0), pl.program_id(1)
    first_query = places[which]
    columns = held.shape[0]
    block = columns
    out_ref[...] = jnp.zeros_like(out_ref)
    lse_ref[...] = jnp.zeros_like(lse_ref)

    @pl.when(first_query < lengths[slot])
    def _():
        held[...] = stack_heads(q_ref[0, 0], False)
        acc[...] = jnp.zeros_like(acc)
        top[...] = jnp.full_like(top, MASKED)
        total[...] = jnp.zeros_like(total)
        whole = first_query // block

        def visit(index, masked):
            start = pl.multiple_of(index * block, block)
            kv = kv_ref[0, pl.ds(start, block), :]
            scores = mm(kv, held[...], NT)
            if masked:
                keep = causal_keep(start, first_query, block, piece, columns)
                scores = jnp.where(keep, scores, MASKED)
            before = top[...]
            now = jnp.maximum(before, jnp.max(scores, axis=0, keepdims=True))
            weights = jnp.exp(scores - now)
            ratio = jnp.exp(before - now)
            total[...] = total[...] * ratio + jnp.sum(weights, axis=0, keepdims=True)
            acc[...] = acc[...] * ratio + mm(kv, weights.astype(BF16), TN)
            top[...] = now

        @pl.loop(0, whole)
        def _(index):
            visit(index, False)

        visit(whole, True)
        out_ref[0, 0] = unstack_heads((acc[...] / total[...]).T, piece, True).astype(BF16)
        lse_ref[0, 0] = top[...] + jnp.log(total[...])


def attend(places, lengths, queries, kv, piece):
    _, slots, _, wide = queries.shape
    length, width = kv.shape[1:]
    columns = Q_SHARE * piece
    rows = pl.BlockSpec((1, 1, piece, wide), lambda s, e, *_: (e, s, 0, 0))
    return pl.pallas_call(
        functools.partial(attend_kernel, piece=piece),
        grid_spec=pltpu.PrefetchScalarGridSpec(
            num_scalar_prefetch=2,
            grid=(slots, CORES),
            in_specs=[
                rows,
                pl.BlockSpec((1, length, width), lambda s, e, *_: (s, 0, 0)),
            ],
            out_specs=[
                rows,
                pl.BlockSpec((1, 1, 1, columns), lambda s, e, *_: (s, e, 0, 0)),
            ],
            scratch_shapes=[
                pltpu.VMEM((width, columns), F32),
                pltpu.VMEM((1, columns), F32),
                pltpu.VMEM((1, columns), F32),
                pltpu.VMEM((columns, width), BF16),
            ],
        ),
        out_shape=[
            jax.ShapeDtypeStruct(queries.shape, BF16),
            jax.ShapeDtypeStruct((slots, CORES, 1, columns), F32),
        ],
        compiler_params=pltpu.CompilerParams(vmem_limit_bytes=VMEM),
        cost_estimate=cost(20),
        name="attend",
    )(places, lengths, queries, kv)


def attend_back_kernel(
    places, lengths, q_ref, kv_ref, out_ref, dout_ref, lse_ref, dq_ref, dkv_ref, dkv, dq, *, piece
):
    slot, which = pl.program_id(0), pl.program_id(1)
    first_query = places[which]
    columns = dq.shape[1]
    block = columns
    dq_ref[...] = jnp.zeros_like(dq_ref)

    @pl.when(which == 0)
    def _():
        dkv[...] = jnp.zeros_like(dkv)

    @pl.when(first_query < lengths[slot])
    def _():
        dq[...] = jnp.zeros_like(dq)
        queries = stack_heads(q_ref[0, 0], False)
        dout = stack_heads(dout_ref[0, 0], True)
        both = dout.astype(F32) * stack_heads(out_ref[0, 0], True).astype(F32)
        delta = mm(jnp.ones((8, both.shape[1]), F32), both, NT, lax.Precision.HIGHEST)[:1]
        lse = lse_ref[0, 0]
        whole = first_query // block

        def visit(index, masked):
            start = pl.multiple_of(index * block, block)
            kv = kv_ref[0, pl.ds(start, block), :]
            scores = mm(kv, queries, NT)
            if masked:
                keep = causal_keep(start, first_query, block, piece, columns)
                scores = jnp.where(keep, scores, MASKED)
            probs = jnp.exp(scores - lse)
            dprobs = mm(kv, dout, NT)
            dscores = (probs * (dprobs - delta)).astype(BF16)
            probs = probs.astype(BF16)
            dkv[pl.ds(start, block), :] += mm(dscores, queries) + mm(probs, dout)
            dq[...] += mm(kv, dscores, TN)

        @pl.loop(0, whole)
        def _(index):
            visit(index, False)

        visit(whole, True)
        dq_ref[0, 0] = unstack_heads(dq[...].T, piece, False)

    @pl.when(which == CORES - 1)
    def _():
        dkv_ref[0] = dkv[...].astype(dkv_ref.dtype)


def attend_back(places, lengths, queries, kv, out, dout, lse, piece):
    _, slots, _, wide = queries.shape
    length, width = kv.shape[1:]
    columns = Q_SHARE * piece
    rows = pl.BlockSpec((1, 1, piece, wide), lambda s, e, *_: (e, s, 0, 0))
    keys = pl.BlockSpec((1, length, width), lambda s, e, *_: (s, 0, 0))
    return pl.pallas_call(
        functools.partial(attend_back_kernel, piece=piece),
        grid_spec=pltpu.PrefetchScalarGridSpec(
            num_scalar_prefetch=2,
            grid=(slots, CORES),
            in_specs=[
                rows,
                keys,
                rows,
                rows,
                pl.BlockSpec((1, 1, 1, columns), lambda s, e, *_: (s, e, 0, 0)),
            ],
            out_specs=[rows, keys],
            scratch_shapes=[pltpu.VMEM((length, width), F32), pltpu.VMEM((width, columns), F32)],
        ),
        out_shape=[
            jax.ShapeDtypeStruct(queries.shape, F32),
            jax.ShapeDtypeStruct(kv.shape, BF16),
        ],
        compiler_params=pltpu.CompilerParams(vmem_limit_bytes=VMEM),
        cost_estimate=cost(25),
        name="attend_back",
    )(places, lengths, queries, kv, out, dout, lse)


def lower(rows, transposed=False):
    row = lax.broadcasted_iota(jnp.int32, (rows, rows), 0)
    column = lax.broadcasted_iota(jnp.int32, (rows, rows), 1)
    return row <= column if transposed else row >= column


def paired(first, second, shape):
    lane = lax.broadcasted_iota(jnp.int32, shape, 1)
    return jnp.where(lane < SHD, first, second)


def chunk_terms(raw_ref, bias_ref, rate_ref):
    raw = raw_ref[0].astype(F32)[HALO:] + bias_ref[...]
    rows = raw.shape[0]
    steps = jax.nn.softplus(raw)
    logs = mm(lower(rows).astype(F32), steps * rate_ref[...], NN, lax.Precision.HIGHEST)

    def turned(value):
        more = jnp.zeros((2 * LANES - rows, LANES), F32)
        return jnp.concatenate([value, more], axis=0).T[:, :rows]

    return raw, steps, turned(steps), logs, turned(logs)


def chunk_kernel(
    f_ref, b_ref, c_ref, raw_ref, bias_ref, rate_ref, skip_ref,
    at_ref, out_ref, logs_ref, *rest,
):
    state_refs, held = rest[:-1], rest[-1]
    raw, steps, steps_t, logs, logs_t = chunk_terms(raw_ref, bias_ref, rate_ref)
    logs_ref[0] = logs
    rows = logs.shape[0]
    inject = b_ref[0]
    mix = jnp.where(lower(rows), mm(c_ref[0], inject, NT), 0.0)
    tail = jnp.exp(logs[rows - 1 :] - logs) * steps
    for pair in range(M_SHARE // 2):
        lanes = slice(pair * LANES, (pair + 1) * LANES)
        feats = f_ref[0, :, lanes]
        outs = []
        for head in (2 * pair, 2 * pair + 1):
            gap = jnp.minimum(logs[:, head : head + 1] - logs_t[head : head + 1, :], 0.0)
            kernel = mix * jnp.exp(gap) * steps_t[head : head + 1, :]
            outs.append(mm(kernel.astype(BF16), feats))
        wide = feats.astype(F32)
        out_ref[0, :, lanes] = paired(outs[0], outs[1], wide.shape) + skip_ref[:, lanes] * wide
        weight = paired(
            tail[:, 2 * pair : 2 * pair + 1], tail[:, 2 * pair + 1 : 2 * pair + 2], wide.shape
        )
        state = mm((wide * weight).astype(BF16), inject, TN).astype(BF16)
        keep_heads(held, state, pair)
    decay = jnp.exp(logs[rows - 1 :])
    line = lax.broadcasted_iota(jnp.int32, (EXTRA, LANES), 0)
    high = decay.astype(BF16).astype(F32)
    extra = jnp.where(line == 0, high, jnp.where(line == 1, decay - high, 0.0)).astype(BF16)
    for group in range(len(state_refs)):
        held[group, held.shape[1] - EXTRA :, :] = extra
    send_groups(held, state_refs, at_ref)


def carry_kernel(out_ref, c_ref, logs_ref, *rest):
    groups = len(rest) - 3
    at_ref, ssd_ref, held = rest[groups], rest[groups + 1], rest[groups + 2]
    take_groups(held, rest[:groups], at_ref)
    decay = jnp.exp(logs_ref[0])
    for pair in range(M_SHARE // 2):
        lanes = slice(pair * LANES, (pair + 1) * LANES)
        read = mm(c_ref[0], pair_rows(held, pair), NT)
        weight = paired(
            decay[:, 2 * pair : 2 * pair + 1], decay[:, 2 * pair + 1 : 2 * pair + 2], read.shape
        )
        ssd_ref[0, :, lanes] = (out_ref[0, :, lanes] + read * weight).astype(BF16)


def direct_kernel(d_ref, c_ref, logs_ref, at_ref, *rest):
    held = rest[-1]
    decay = jnp.exp(logs_ref[0])
    for pair in range(M_SHARE // 2):
        lanes = slice(pair * LANES, (pair + 1) * LANES)
        grad = d_ref[0, :, lanes].astype(F32)
        weight = paired(
            decay[:, 2 * pair : 2 * pair + 1], decay[:, 2 * pair + 1 : 2 * pair + 2], grad.shape
        )
        state = mm((grad * weight).astype(BF16), c_ref[0], TN).astype(BF16)
        keep_heads(held, state, pair)
    send_groups(held, rest[:-1], at_ref)


def chunk_back_kernel(
    f_ref, b_ref, c_ref, raw_ref, bias_ref, rate_ref, skip_ref,
    d_ref, *rest,
):
    groups = (len(rest) - 10) // 2
    at_ref = rest[2 * groups]
    df_ref, db_ref, dc_ref, draw_ref, sums_ref = rest[2 * groups + 1 : 2 * groups + 6]
    columns, row_sums, states, laters = rest[2 * groups + 6 :]
    take_groups(states, rest[:groups], at_ref)
    take_groups(laters, rest[groups : 2 * groups], at_ref)
    raw, steps, steps_t, logs, logs_t = chunk_terms(raw_ref, bias_ref, rate_ref)
    rows = logs.shape[0]
    inject, readout = b_ref[0], c_ref[0]
    keep = lower(rows)
    mix = jnp.where(keep, mm(readout, inject, NT), 0.0)
    columns[...] = jnp.zeros_like(columns)
    row_sums[...] = jnp.zeros_like(row_sums)
    decay = jnp.exp(logs)
    end_decay = jnp.exp(logs[rows - 1 :] - logs)
    tail = end_decay * steps
    dmix = jnp.zeros((rows, rows), F32)
    db = jnp.zeros((rows, NS), F32)
    dc = jnp.zeros((rows, NS), F32)
    to_state = jnp.zeros((rows, LANES), F32)
    from_state = jnp.zeros((rows, LANES), F32)
    skips = jnp.zeros((1, LANES), F32)
    agree = jnp.zeros((1, LANES), F32)
    head_lane = lax.broadcasted_iota(jnp.int32, (rows, LANES), 1)
    for pair in range(M_SHARE // 2):
        lanes = slice(pair * LANES, (pair + 1) * LANES)
        feats, grad = f_ref[0, :, lanes], d_ref[0, :, lanes]
        wide, wide_grad = feats.astype(F32), grad.astype(F32)
        later = pair_rows(laters, pair)
        state = pair_rows(states, pair)
        agreed = later.astype(F32) * state.astype(F32)
        pushed = mm(inject, later, NT)
        read = mm(readout, state, NT)
        push_part = wide * pushed
        read_part = wide_grad * read
        skip_part = wide * wide_grad
        grads = []
        for half, head in enumerate((2 * pair, 2 * pair + 1)):
            column = slice(head, head + 1)
            lane = lax.broadcasted_iota(jnp.int32, wide.shape, 1)
            mine = (lane < SHD) if half == 0 else (lane >= SHD)
            step_row = steps_t[column, :]
            gap = jnp.minimum(logs[:, column] - logs_t[column, :], 0.0)
            fade = jnp.exp(gap)
            dkernel = mm(jnp.where(mine, wide_grad, 0.0).astype(BF16), feats, NT)
            faded = dkernel * fade
            stepped = faded * step_row
            dmix = dmix + stepped
            kernel = mix * fade * step_row
            columns[column, 0:rows] = jnp.sum(faded * mix, axis=0, keepdims=True)
            here = head_lane == head
            row_sums[...] += jnp.where(here, jnp.sum(stepped * mix, axis=1, keepdims=True), 0.0)
            grads.append(mm(kernel.astype(BF16), grad, TN))
            to_state = to_state + jnp.where(
                here, jnp.sum(jnp.where(mine, push_part, 0.0), axis=1, keepdims=True), 0.0
            )
            from_state = from_state + jnp.where(
                here, jnp.sum(jnp.where(mine, read_part, 0.0), axis=1, keepdims=True), 0.0
            )
            same = agreed[half * SHD : (half + 1) * SHD]
            same = jnp.sum(jnp.sum(same, axis=0, keepdims=True), axis=1, keepdims=True)
            agree = agree + jnp.where(here[:1], same, 0.0)
            skips = skips + jnp.where(
                here[:1],
                jnp.sum(
                    jnp.sum(jnp.where(mine, skip_part, 0.0), axis=1, keepdims=True),
                    axis=0,
                    keepdims=True,
                ),
                0.0,
            )
        first, second = slice(2 * pair, 2 * pair + 1), slice(2 * pair + 1, 2 * pair + 2)
        weight = paired(tail[:, first], tail[:, second], wide.shape)
        df_ref[0, :, lanes] = (
            paired(grads[0], grads[1], wide.shape) + skip_ref[:, lanes] * wide_grad + weight * pushed
        )
        db = db + mm((wide * weight).astype(BF16), later)
        seen = paired(decay[:, first], decay[:, second], wide.shape)
        dc = dc + mm((wide_grad * seen).astype(BF16), state)
    low = dmix * jnp.where(keep, 1.0, 0.0)
    low = low.astype(BF16)
    db_ref[0] = db + mm(low, readout, TN)
    dc_ref[0] = dc + mm(low, inject)
    direct = columns[...].T[:rows]
    push = end_decay * to_state
    dlogs = row_sums[...] - steps * direct + decay * from_state - steps * push
    end = jnp.sum(steps * push, axis=0, keepdims=True) + decay[rows - 1 :] * agree
    last = lax.broadcasted_iota(jnp.int32, (rows, LANES), 0) == rows - 1
    dlogs = dlogs + jnp.where(last, end, 0.0)
    summed = mm(lower(rows, True).astype(F32), dlogs, NN, lax.Precision.HIGHEST)
    dsteps = direct + push + summed * rate_ref[...]
    draw = dsteps * jax.nn.sigmoid(raw)
    draw_ref[0] = draw
    line = lax.broadcasted_iota(jnp.int32, (8, LANES), 0)
    dbias = jnp.sum(draw, axis=0, keepdims=True)
    dlog = jnp.sum(summed * steps, axis=0, keepdims=True) * rate_ref[...]
    sums_ref[0] = jnp.where(
        line == 0, dbias, jnp.where(line == 1, dlog, jnp.where(line == 2, skips, 0.0))
    )


def conv_back_kernel(mixed_ref, df_ref, dshared_ref, taps_ref, shift_ref, _, dmixed_ref, sums_ref):
    mixed = mixed_ref[0].astype(F32)
    rows = df_ref.shape[1]
    first = HALO - KC + 1
    pre = shift_ref[...]
    for tap in range(KC):
        pre = pre + taps_ref[tap : tap + 1, :] * mixed[first + tap : first + tap + rows]
    gate = jax.nn.sigmoid(pre)
    slope = gate + pre * gate * (1.0 - gate)
    dpre = jnp.concatenate([df_ref[0], dshared_ref[0]], axis=1) * slope
    line = lax.broadcasted_iota(jnp.int32, (8, dpre.shape[1]), 0)
    sums = jnp.where(line == KC, jnp.sum(dpre, axis=0, keepdims=True), 0.0)
    none = jnp.zeros((HALO, dpre.shape[1]), F32)
    padded = jnp.concatenate([none, dpre, none], axis=0)
    total = jnp.zeros(mixed.shape, F32)
    for tap in range(KC):
        seen = mixed[first + tap : first + tap + rows]
        sums = sums + jnp.where(line == tap, jnp.sum(dpre * seen, axis=0, keepdims=True), 0.0)
        start = HALO - first - tap
        total = total + taps_ref[tap : tap + 1, :] * padded[start : start + rows + HALO]
    dmixed_ref[0] = total.astype(BF16)
    sums_ref[0] = sums


def over_pieces(kernel, name, args, whole, outs, micros, at, scratch=()):
    pieces = args[0].shape[0]

    def spec(shape, split):
        if split:
            return pl.BlockSpec((1,) + shape[1:], lambda i: (i,) + (0,) * (len(shape) - 1))
        return pl.BlockSpec(shape, lambda i: (0,) * len(shape))

    shapes = [(arg.shape, index not in whole) for index, arg in enumerate(args)]
    return pl.pallas_call(
        kernel,
        grid=(pieces,),
        in_specs=[spec(shape, split) for shape, split in shapes]
        + [pl.BlockSpec(memory_space=pltpu.SMEM)],
        out_specs=[spec(shape, True) for shape, _ in outs],
        out_shape=[jax.ShapeDtypeStruct(shape, dtype) for shape, dtype in outs],
        scratch_shapes=list(scratch),
        compiler_params=pltpu.CompilerParams(vmem_limit_bytes=VMEM),
        cost_estimate=cost(micros),
        name=name,
    )(*args, at)


def keep_heads(held, state, pair):
    share = M_SHARE // held.shape[0]
    for half in range(2):
        group, spot = divmod(2 * pair + half, share)
        held[group, spot * SHD : (spot + 1) * SHD, :] = state[half * SHD : (half + 1) * SHD]


def pair_rows(held, pair):
    share = M_SHARE // held.shape[0]
    found = []
    for half in range(2):
        group, spot = divmod(2 * pair + half, share)
        found.append(held[group, spot * SHD : (spot + 1) * SHD, :])
    return jnp.concatenate(found, axis=0)


def send_groups(held, refs, at_ref):
    for r, ref in enumerate(refs):
        ref[0] = held[lax.rem(at_ref[2] + r, len(refs))]


def take_groups(held, refs, at_ref):
    for r, ref in enumerate(refs):
        held[lax.rem(at_ref[2] + len(refs) - r, len(refs))] = ref[0]


def scan_kernel(at_ref, *refs, groups, chips, share, reverse, last):
    rows = share * SHD
    states, marks = refs[:groups], refs[groups : 2 * groups]
    refs = refs[2 * groups :]
    chip, z, core = at_ref[4], at_ref[2], at_ref[3]
    lane = lax.broadcasted_iota(jnp.int32, (1, LANES), 1)

    def pick(pair, offset):
        both = pair[0:1].astype(F32) + pair[1:2].astype(F32)
        return [
            jnp.sum(jnp.where(lane == offset + i, both, 0.0), axis=1, keepdims=True)
            for i in range(share)
        ]

    def step(run, factors, new):
        return jnp.concatenate(
            [
                factors[i] * run[i * SHD : (i + 1) * SHD] + new[i * SHD : (i + 1) * SHD]
                for i in range(share)
            ],
            axis=0,
        )

    if last:
        totals, fades = refs[: chips - 1], refs[chips - 1 : 2 * chips - 2]
        outs, held, decay, entered = (
            refs[2 * chips - 2 : 2 * chips - 2 + groups],
            refs[-3],
            refs[-2],
            refs[-1],
        )
    else:
        total_ref, held, decay = refs
    for r in range(groups):
        to = lax.rem(z + groups - r, groups)
        held[to] = states[r][:, 0, :rows]
        decay[to] = marks[r][:, 0]
    run = jnp.zeros((rows, NS), F32)
    if last:
        for k in range(chips - 1, 0, -1):
            part = chips - k if reverse else k
            reached = chip + k < chips if reverse else chip >= k
            new = step(run, pick(fades[part - 1][0], 0), totals[part - 1][0, :rows].astype(F32))
            run = jnp.where(reached, new, run)
    fade = [jnp.ones((1, 1), F32)] * share
    order = [(h, k) for h in range(CORES) for k in range(groups)]
    for h, k in order[::-1] if reverse else order:
        e = lax.rem(h + core, CORES)
        if last:
            entered[k, e] = run.astype(BF16)
        factors = pick(decay[k, e], z * share)
        run = step(run, factors, held[k, e].astype(F32))
        fade = [one * two for one, two in zip(fade, factors)]
    if last:
        for r in range(groups):
            outs[r][:, 0] = entered[lax.rem(z + r, groups)]
        return
    line = lax.broadcasted_iota(jnp.int32, (EXTRA, LANES), 0)
    place = lax.broadcasted_iota(jnp.int32, (EXTRA, LANES), 1)
    extra = jnp.zeros((EXTRA, LANES), F32)
    for i in range(share):
        high = fade[i].astype(BF16).astype(F32)
        extra = extra + jnp.where((line == 0) & (place == i), high, 0.0)
        extra = extra + jnp.where((line == 1) & (place == i), fade[i] - high, 0.0)
    total_ref[0, :rows] = run.astype(BF16)
    total_ref[0, rows:] = extra.astype(BF16)


def carried(
    place,
    at,
    states,
    marks,
    fades,
    reverse,
    before=lambda x: x,
    between=lambda x: x,
    after=lambda x: x,
):
    groups, chips = place.size["z"], place.chips
    share = M_SHARE // groups
    rows = share * SHD
    slots = states[0].shape[1]
    parts = before(
        [part if r == 0 else place.shift(part, "z", r) for r, part in enumerate(states)]
    )
    marks = parts if marks is None else marks
    block = [pl.BlockSpec((CORES, 1, part.shape[2], NS), lambda s, *_: (0, s, 0, 0)) for part in parts]
    mark = pl.BlockSpec((CORES, 1, EXTRA, NS), lambda s, *_: (0, s, rows // EXTRA, 0))
    total = pl.BlockSpec((1, rows + EXTRA, NS), lambda s, *_: (s, 0, 0))
    fade = pl.BlockSpec((1, EXTRA, NS), lambda s, *_: (s, rows // EXTRA, 0))
    result = pl.BlockSpec((CORES, 1, rows, NS), lambda s, *_: (0, s, 0, 0))
    scratch = [
        pltpu.VMEM((groups, CORES, rows, NS), BF16),
        pltpu.VMEM((groups, CORES, EXTRA, NS), BF16),
    ]

    def call(last, args, specs, outs, out_specs, more):
        return pl.pallas_call(
            functools.partial(
                scan_kernel, groups=groups, chips=chips, share=share, reverse=reverse, last=last
            ),
            grid_spec=pltpu.PrefetchScalarGridSpec(
                num_scalar_prefetch=1,
                grid=(slots,),
                in_specs=block + [mark] * groups + specs,
                out_specs=out_specs,
                scratch_shapes=scratch + more,
            ),
            out_shape=outs,
            compiler_params=pltpu.CompilerParams(vmem_limit_bytes=VMEM),
            cost_estimate=cost(3),
            name="scan",
        )(at, *parts, *marks, *args)

    leaving = call(
        False, [], [], jax.ShapeDtypeStruct((slots, rows + EXTRA, NS), BF16), total, []
    )
    totals = [lax.ppermute(leaving, AXES, place.chip_pairs(k)) for k in range(1, chips)]
    totals = between(totals)
    fades = totals if fades is None else fades
    entering = call(
        True,
        [*totals, *fades],
        [total] * (chips - 1) + [fade] * (chips - 1),
        [jax.ShapeDtypeStruct((CORES, slots, rows, NS), BF16)] * groups,
        [result] * groups,
        [pltpu.VMEM((groups, CORES, rows, NS), BF16)],
    )
    entering = after(entering)
    found = [part if r == 0 else place.shift(part, "z", r) for r, part in enumerate(entering)]
    return [part.reshape(CORES * slots, rows, NS) for part in found], marks, fades


def shards(
    hidden_in,
    out_grad,
    lengths,
    input_gain,
    attn_in_weight,
    attn_out_weight,
    zgate_weight,
    mixer_in_weight,
    step_weight,
    conv_weight,
    conv_bias,
    step_bias,
    decay_log,
    skip_scale,
    mixer_gain,
    mixer_out_weight,
    post_gain,
    gate_weight,
    up_weight,
    down_weight,
):
    place = Place()
    core = place.at["c"]
    groups, chips, devices = place.size["z"], place.chips, place.devices
    na, nb = place.size["a"], place.size["b"]
    slots, piece, width = hidden_in.shape
    span = piece * groups
    rows_all = CORES * slots * piece
    rows_halo = CORES * slots * (piece + HALO)
    q_cols, m_cols = Q_SHARE * HD, M_SHARE * SHD
    lin_cols = q_cols + 2 * HD
    c_cols = m_cols + NS
    at = place.scalars
    shard_rows = attn_in_weight.shape[0]
    out_rows, mix_rows, ff_rows = (
        attn_out_weight.shape[0],
        mixer_out_weight.shape[0],
        down_weight.shape[0],
    )
    ff_half = ff_rows * groups * chips

    rim = lax.ppermute(
        hidden_in[:, piece - KC + 1 :], AXES, [(i, i + 1) for i in range(devices - 1)]
    )
    block = jnp.concatenate(
        [jnp.zeros((slots, HALO - KC + 1, width), BF16), rim, hidden_in], axis=1
    )
    other_index = place.flat + jnp.where(core == 0, groups, -groups)
    pieces_at = jnp.stack([place.flat, other_index]) * piece
    positions = pieces_at[:, None] + jnp.arange(piece, dtype=jnp.int32)
    valid = (positions[:, None, :] < lengths[None, :, None]).astype(F32)
    tokens = jnp.stack([block, place.swap(block)]).astype(F32)
    dy_own = out_grad.astype(F32) * valid[0][..., None]
    dy_low = dy_own.astype(BF16)
    dy = jnp.stack([dy_low, place.swap(dy_low)]).reshape(rows_all, width)

    small = jnp.concatenate([input_gain, mixer_gain, post_gain, conv_bias, conv_weight.reshape(-1)])
    vector_size = small.shape[0]
    terms = jnp.stack([step_bias, decay_log, skip_scale])
    term_size = terms.size
    split_terms = []
    for _ in range(3):
        part = lax.reduce_precision(terms, 8, 7)
        split_terms.append(part.reshape(-1).astype(BF16))
        terms = terms - part
    small = jnp.concatenate([small, *split_terms])
    small_cols = -(-small.shape[0] // shard_rows)
    small = jnp.pad(small, (0, small_cols * shard_rows - small.shape[0]))
    small = small.reshape(shard_rows, small_cols)
    small_at = M_SHARE
    ms_cols = -(-(small_at + small_cols) // LANES) * LANES
    a_cols, b_cols = lin_cols + ms_cols, c_cols

    def early_columns(half):
        return jnp.concatenate(
            [
                attn_in_weight[:, half * q_cols : (half + 1) * q_cols],
                attn_in_weight[:, QH * HD + half * HD : QH * HD + (half + 1) * HD],
                attn_in_weight[:, (QH + KVH + half) * HD : (QH + KVH + half + 1) * HD],
                step_weight[:, half * M_SHARE : (half + 1) * M_SHARE],
                small,
                jnp.zeros((shard_rows, ms_cols - small_at - small_cols), BF16),
                mixer_in_weight[:, half * m_cols : (half + 1) * m_cols],
                mixer_in_weight[:, SH * SHD + half * NS : SH * SHD + (half + 1) * NS],
            ],
            axis=1,
        )

    def sorted_halves(columns):
        halves = (columns(0), columns(1))
        kept = place.by_core(*halves)
        got = place.swap(place.by_core(halves[1], halves[0]))
        return jnp.concatenate([place.by_core(kept, got), place.by_core(got, kept)], axis=0)

    early = place.spread_z(sorted_halves(early_columns))

    def side_by_side(weight):
        return weight.reshape(2, shard_rows, width).transpose(1, 0, 2).reshape(shard_rows, 2 * width)

    out_weights = jnp.concatenate([attn_out_weight, mixer_out_weight], axis=0)
    middle = jnp.concatenate([zgate_weight, side_by_side(out_weights)], axis=1)
    middle = lax.all_gather(middle, AXES, axis=0, tiled=True)
    ff_all = jnp.concatenate([gate_weight, up_weight, side_by_side(down_weight)], axis=1)
    early = place.place_z(early, [[(0, a_cols, 2)], [(a_cols, b_cols, 2)]])
    early = place.plane_second(place.plane_first(early))
    w_a, w_b = place.plane_third(early, [(0, 0, a_cols, 0, 0), (1, 0, b_cols, 1, 0)])
    tail_at = lin_cols
    vectors = w_a[:, tail_at + small_at : tail_at + small_at + small_cols]
    vectors = vectors.reshape(devices, -1).astype(F32)
    sizes = [input_gain.shape[0], mixer_gain.shape[0], post_gain.shape[0], conv_bias.shape[0]]
    ends = [sum(sizes[: k + 1]) for k in range(4)]
    gain_in = vectors[:, : ends[0]].reshape(-1)
    gain_mixer = vectors[:, ends[0] : ends[1]].reshape(-1)
    gain_mixer = place.by_core(gain_mixer[:m_cols], gain_mixer[m_cols:])
    gain_post = vectors[:, ends[1] : ends[2]].reshape(-1)
    shift_all = vectors[:, ends[2] : ends[3]].reshape(-1)
    taps_all = vectors[:, ends[3] : vector_size].reshape(devices, KC, sizes[3])
    taps_all = jnp.transpose(taps_all, (1, 0, 2)).reshape(KC, -1)

    def conv_half(value):
        first = jnp.concatenate(
            [value[..., :m_cols], value[..., 2 * m_cols : 2 * m_cols + NS]], axis=-1
        )
        second = jnp.concatenate(
            [value[..., m_cols : 2 * m_cols], value[..., 2 * m_cols + NS :]], axis=-1
        )
        return place.by_core(first, second)

    taps, shift = conv_half(taps_all), conv_half(shift_all)
    terms = vectors[:groups, vector_size : vector_size + 3 * term_size]
    terms = terms.reshape(groups, 3, 3, SH // groups)
    terms = terms[:, 0] + terms[:, 1] + terms[:, 2]
    terms = jnp.transpose(terms, (1, 0, 2)).reshape(3, SH)
    terms = place.by_core(terms[:, :M_SHARE], terms[:, M_SHARE:])
    bias, log_rates, skip = terms[0], terms[1], terms[2]
    rates = -jnp.exp(log_rates)

    scale_in = inverse_rms(tokens)
    normed = (tokens * scale_in * gain_in).astype(BF16).reshape(rows_halo, width)

    def body_rows(value):
        return value.reshape(CORES, slots, piece + HALO, -1)[:, :, HALO:]

    linear = body_rows(mm(normed, w_a[:, :lin_cols]))
    mixed = mm(normed, w_b).astype(BF16).reshape(CORES, slots, piece + HALO, c_cols)
    step_raw = mm(normed, w_a[:, tail_at:]).astype(BF16)

    def rows_plan(source, start, pieces_of):
        found = []
        for device in range(devices // 2):
            for first, count, output, to, pitch in pieces_of:
                side, row = divmod(first, shard_rows)

                def where(at, device=device, side=side, row=row, count=count):
                    first = (at[3] * (devices // 2) + device) * shard_rows + row
                    return pl.ds(first, count), pl.ds(start + side * width, width)

                def goal(at, device=device, to=to, pitch=pitch, count=count):
                    return pl.ds(device * pitch + to, count), pl.ds(0, width)

                found.append((source, where, output, goal))
        return found

    def columns_plan(source, start, size, output):
        def where(at):
            return pl.ds(0, width), pl.ds(pl.multiple_of(start + at[3] * size, LANES), size)

        return [(source, where, output, lambda at: (pl.ds(0, width), pl.ds(0, size)))]

    low = jax.ShapeDtypeStruct
    w_z, w_attn_out, w_mixer_out = moved(
        place,
        [middle],
        [low((width, m_cols), BF16), low((q_cols, width), BF16), low((m_cols, width), BF16)],
        columns_plan(0, 0, m_cols, 0)
        + rows_plan(
            0,
            2 * m_cols,
            [
                (0, out_rows, 1, 0, out_rows),
                (out_rows, shard_rows - out_rows, 2, 0, mix_rows),
                (shard_rows, shard_rows, 2, shard_rows - out_rows, mix_rows),
            ],
        ),
    )
    cos_part, sin_part = rotary_tables(positions, HD)
    cos_part, sin_part = cos_part[:, None, :, None], sin_part[:, None, :, None]
    queries = rotate(
        linear[..., :q_cols].reshape(CORES, slots, piece, Q_SHARE, HD), cos_part, sin_part
    ).astype(BF16)
    keys = rotate(
        linear[..., q_cols : q_cols + HD][..., None, :], cos_part, sin_part
    ).astype(BF16)[..., 0, :]
    kv_own = jnp.concatenate([keys, linear[..., q_cols + HD :].astype(BF16)], axis=-1)
    kv_parts = [part.reshape(-1, 2 * HD) for part in place.spread_z(kv_own)]
    plan = []
    for r in range(groups):
        for e in range(CORES):
            for s in range(slots):

                def source(at, e=e, s=s):
                    return pl.ds((e * slots + s) * piece, piece), pl.ds(0, 2 * HD)

                def goal(at, r=r, e=e):
                    z = lax.rem(at[2] + groups - r, groups)
                    h = lax.rem(at[3] + e, CORES)
                    return pl.ds((h * groups + z) * piece, piece), pl.ds(0, 2 * HD)

                plan.append((r, source, s, goal))
    kv_size = jax.ShapeDtypeStruct((CORES * groups * piece, 2 * HD), BF16)
    kv = moved(place, kv_parts, [kv_size] * slots, plan)
    kv = place.plane_first(kv)
    scale = HD ** (-0.5)
    queries = (queries * jnp.asarray(scale, BF16)).reshape(CORES, slots, piece, q_cols)
    pre = shift
    for tap in range(KC):
        first = HALO - KC + 1 + tap
        pre = pre + taps[tap] * mixed[:, :, first : first + piece].astype(F32)
    conv_out = jax.nn.silu(pre).astype(BF16)
    features = conv_out[..., :m_cols].reshape(CORES * slots, piece, m_cols)
    shared = conv_out[..., m_cols:]
    shared_other = place.swap(shared)[::-1]
    inject = place.by_core(shared, shared_other).reshape(CORES * slots, piece, NS)
    readout = place.by_core(shared_other, shared).reshape(CORES * slots, piece, NS)
    raw = step_raw.reshape(CORES * slots, piece + HALO, ms_cols)
    bias_row = jnp.pad(bias, (0, LANES - M_SHARE))[None]
    rate_row = jnp.pad(rates, (0, LANES - M_SHARE))[None]
    skip_row = jnp.repeat(skip, SHD)[None]
    pieces = CORES * slots
    chunk_args = [
        features, inject, readout, raw, bias_row, rate_row, skip_row,
    ]
    share_rows = m_cols // groups
    held = pltpu.VMEM((groups, share_rows, NS), BF16)
    held_more = pltpu.VMEM((groups, share_rows + EXTRA, NS), BF16)
    within, logs, *local = over_pieces(
        chunk_kernel,
        "chunk",
        chunk_args,
        range(4, 7),
        [
            ((pieces, piece, m_cols), F32),
            ((pieces, piece, LANES), F32),
            *[((pieces, share_rows + EXTRA, NS), BF16)] * groups,
        ],
        9,
        at,
        [held_more],
    )
    local = [part.reshape(CORES, slots, share_rows + EXTRA, NS) for part in local]
    held_back = {"kv": kv}

    def before_states(parts):
        parts, held_back["kv"], columns = tie(parts, held_back["kv"], ff_all)
        held_back["ff"] = lax.all_gather(columns, AXES, axis=0, tiled=True)
        held_back["kv"] = place.plane_second(held_back["kv"])
        return parts

    def between_states(totals):
        gates = mm(normed, w_z).astype(BF16)
        totals, held_back["kv"], held_back["gates"], held_back["weights"] = tie(
            totals, held_back["kv"], gates, (w_z, w_attn_out, w_mixer_out)
        )
        return totals

    def after_states(entering):
        entering, held_back["queries"] = tie(entering, queries)
        return entering

    state_in, marks, fades = carried(
        place, at, local, None, None, False, before_states, between_states, after_states
    )
    queries = held_back["queries"]
    w_z_late, w_attn_out_late, w_mixer_out_late = held_back["weights"]
    rows = chips * CORES * groups * piece
    (kv,) = place.plane_third(
        held_back["kv"], [(s, 0, 2 * HD, 0, 0, s * rows) for s in range(slots)]
    )
    kv = kv.reshape(slots, rows, 2 * HD)
    ff_whole = held_back["ff"]
    w_gate, w_up, w_down = moved(
        place,
        [ff_whole],
        [low((width, ff_half), BF16), low((width, ff_half), BF16), low((ff_half, width), BF16)],
        columns_plan(0, 0, ff_half, 0)
        + columns_plan(0, 2 * ff_half, ff_half, 1)
        + rows_plan(
            0,
            4 * ff_half,
            [
                (0, shard_rows, 2, 0, ff_rows),
                (shard_rows, shard_rows, 2, shard_rows, ff_rows),
            ],
        ),
    )

    heads_out, lse = attend(pieces_at, lengths, queries, kv, piece)
    attended = heads_out.reshape(rows_all, q_cols)
    attended, state_in = tie(attended, state_in)
    (ssd,) = over_pieces(
        carry_kernel,
        "carry",
        [within, readout, logs, *state_in],
        (),
        [((pieces, piece, m_cols), BF16)],
        5,
        at,
        [held],
    )
    ssd = ssd.reshape(CORES, slots, piece, m_cols).astype(F32)
    zgate = body_rows(held_back["gates"])
    gate_value, gate_slope = silu_and_slope(zgate.astype(F32))
    gated_raw = ssd * gate_value
    squares = jnp.sum(gated_raw * gated_raw, axis=-1)
    squares = squares + place.swap(squares)[::-1]
    scale_mixer = lax.rsqrt(squares / (SH * SHD) + 1e-05)[..., None]
    gated = (gated_raw * scale_mixer * gain_mixer).astype(BF16).reshape(rows_all, m_cols)

    def own_sum(partial):
        partial = partial.reshape(CORES, -1, partial.shape[-1])
        return partial[0] + place.swap(partial[1].astype(BF16)).astype(F32)

    def with_other(value):
        return jnp.stack([value, place.swap(value)]).reshape(-1, value.shape[-1])

    mixers = own_sum(mm(attended, w_attn_out_late) + mm(gated, w_mixer_out_late))
    residual = tokens[0][:, HALO:].reshape(-1, width) + mixers
    scale_post = inverse_rms(residual)
    post = with_other((residual * scale_post * gain_post).astype(BF16))
    gate_lin = mm(post, w_gate)
    up_lin = mm(post, w_up)
    gate_act, gate_act_slope = silu_and_slope(gate_lin)
    hidden = (gate_act * up_lin).astype(BF16)
    valid_own = valid[0].reshape(-1, 1)
    layer_out = (valid_own * (residual + own_sum(mm(hidden, w_down)))).astype(BF16)

    dhidden = mm(dy, w_down, NT)
    dgate = (dhidden * up_lin * gate_act_slope).astype(BF16)
    dup = (dhidden * gate_act).astype(BF16)

    def own_parity(grad):
        grad = grad.astype(BF16).reshape(chips // 2, CORES, -1, width)
        kept = lax.dynamic_index_in_dim(grad, core, 1, False)
        got = place.swap(lax.dynamic_index_in_dim(grad, 1 - core, 1, False))
        grad = jnp.concatenate([place.by_core(kept, got), place.by_core(got, kept)], axis=0)
        return grad.reshape(-1, width)

    dpost = own_sum(mm(dgate, w_gate, NT) + mm(dup, w_up, NT))
    dresidual = dy_own.reshape(-1, width) + rms_back(residual, scale_post, gain_post, dpost)
    grad_post_gain = jnp.sum(dpost * residual * scale_post, axis=0)
    dmix = with_other(dresidual.astype(BF16))

    dattended = mm(dmix, w_attn_out_late, NT).astype(BF16)
    dgated = mm(dmix, w_mixer_out_late, NT).reshape(CORES, slots, piece, m_cols)
    scaled = dgated * gain_mixer
    inner = jnp.sum(scaled * gated_raw, axis=-1)
    inner = (inner + place.swap(inner)[::-1])[..., None] / (SH * SHD)
    dgated_raw = scale_mixer * scaled - gated_raw * (scale_mixer**3 * inner)
    grad_mixer_gain = jnp.sum(dgated * gated_raw * scale_mixer, axis=(0, 1, 2))
    dssd = (dgated_raw * gate_value).astype(BF16).reshape(pieces, piece, m_cols)
    dzgate = (dgated_raw * ssd * gate_slope).astype(BF16)

    def halo_rows(value):
        value = value.reshape(CORES, slots, piece, -1)
        return jnp.pad(value, ((0, 0), (0, 0), (HALO, 0), (0, 0)))

    dzgate = halo_rows(dzgate).reshape(rows_halo, m_cols)

    direct = over_pieces(
        direct_kernel,
        "direct",
        [dssd, readout, logs],
        (),
        [((pieces, share_rows, NS), BF16)] * groups,
        5,
        at,
        [held],
    )
    direct = [part.reshape(CORES, slots, share_rows, NS) for part in direct]
    dgate, dup, hidden, direct = tie(dgate, dup, hidden, direct)
    ff_grads, ff_start = place.stack_far(
        [
            mm(post, dgate, TN).astype(BF16),
            mm(post, dup, TN).astype(BF16),
            own_parity(mm(hidden, dy, TN)),
        ]
    )
    out_side = {}

    def before_scan(parts):
        parts, flat = tie(parts, ff_grads)
        out_side["ff"] = ff_start(flat)
        return parts

    def between_scans(totals):
        totals, out_side["dz"], dmix_late = tie(totals, dzgate, dmix)
        grad_outs = jnp.concatenate(
            [
                mm(attended, dmix_late, TN).astype(BF16).reshape(devices // 2, out_rows, width),
                mm(gated, dmix_late, TN).astype(BF16).reshape(devices // 2, mix_rows, width),
            ],
            axis=1,
        )
        wide_dz = jnp.pad(out_side["dz"], ((0, 0), (0, width - m_cols)))
        mid_grads, mid_start = place.stack_far(
            [own_parity(grad_outs), mm(normed, wide_dz, TN).astype(BF16)]
        )
        totals, mid_grads = tie(totals, mid_grads)
        out_side["mid"] = mid_start(mid_grads)
        return totals

    def after_scans(entering):
        entering, out_side["dattended"] = tie(entering, dattended)
        return entering

    later, _, _ = carried(
        place, at, direct, marks, fades, True, before_scan, between_scans, after_scans
    )
    ff_grads, mid_grads = out_side["ff"], out_side["mid"]
    dattended = out_side["dattended"]
    dnormed = mm(out_side["dz"], w_z_late, NT)

    dqueries, dkv = attend_back(
        pieces_at,
        lengths,
        queries,
        kv,
        heads_out,
        dattended.reshape(heads_out.shape),
        lse,
        piece,
    )
    dkv, later = tie(dkv, later)
    dkv = [
        place.reduce_first(dkv[s].reshape(na, nb, CORES, groups, piece, 2 * HD), s % 2 == 0)
        for s in range(slots)
    ]

    dfeatures, dinject, dreadout, draw, sums = over_pieces(
        chunk_back_kernel,
        "chunk_back",
        chunk_args + [dssd, *state_in, *later],
        range(4, 7),
        [
            ((pieces, piece, m_cols), F32),
            ((pieces, piece, NS), F32),
            ((pieces, piece, NS), F32),
            ((pieces, piece, LANES), F32),
            ((pieces, 8, LANES), F32),
        ],
        28,
        at,
        [pltpu.VMEM((LANES, 2 * LANES), F32), pltpu.VMEM((piece, LANES), F32), held, held],
    )
    ff_grads, dkv, dfeatures = tie(ff_grads, dkv, dfeatures)
    dkv = [place.reduce_second(dkv[s], s % 2 == 0) for s in range(slots)]
    dinject = dinject.reshape(CORES, slots, piece, NS)
    dreadout = dreadout.reshape(CORES, slots, piece, NS)
    dshared = place.by_core(dinject, dreadout) + place.swap(
        place.by_core(dreadout, dinject).astype(BF16)
    )[::-1].astype(F32)
    dmixed, conv_sums = over_pieces(
        conv_back_kernel,
        "conv_back",
        [
            mixed.reshape(pieces, piece + HALO, c_cols),
            dfeatures,
            dshared.reshape(pieces, piece, NS),
            taps,
            shift[None],
        ],
        range(3, 5),
        [((pieces, piece + HALO, c_cols), BF16), ((pieces, 8, c_cols), F32)],
        6,
        at,
    )
    conv_sums = jnp.sum(conv_sums, axis=0)
    grad_taps, grad_shift = conv_sums[:KC], conv_sums[KC]

    def by_columns(grad):
        return grad.reshape(na, nb, CORES, groups, shard_rows, grad.shape[-1])


    dstep = draw[..., :M_SHARE].astype(BF16)
    db_low = dmixed.reshape(rows_halo, b_cols)
    dkv, db_low = tie(dkv, db_low)
    grad_b = place.reduce_first(by_columns(mm(normed, db_low, TN)), False)
    dkv_own = place.reduce_z(dkv)
    dnormed = dnormed + mm(db_low, w_b, NT)
    head_sums = place.sum_along(jnp.sum(sums, axis=0)[:3, :M_SHARE], "z")
    dkv_own, grad_b, dnormed, head_sums, ff_grads, mid_grads = tie(
        dkv_own, grad_b, dnormed, head_sums, ff_grads, mid_grads
    )
    far_grads = place.finish_far([ff_grads, mid_grads], [[2, 2, 1], [1, 2]])
    dkv_own = jnp.stack([part.reshape(CORES, piece, 2 * HD) for part in dkv_own], axis=1)
    dkv_own = place.by_core(dkv_own, dkv_own[::-1])
    grad_b = place.reduce_second(grad_b, False)
    dq_rows = (dqueries * scale).reshape(CORES, slots, piece, Q_SHARE, HD)
    dq_rows = rotate(dq_rows, cos_part, -sin_part).reshape(CORES, slots, piece, q_cols)
    dk_rows = rotate(dkv_own[..., None, :HD], cos_part, -sin_part)[..., 0, :]
    tail_zeros = jnp.zeros((CORES, slots, piece, ms_cols - M_SHARE), BF16)
    dlin = jnp.concatenate([dq_rows, dk_rows, dkv_own[..., HD:]], axis=-1).astype(BF16)
    da_low = halo_rows(
        jnp.concatenate(
            [dlin, dstep.reshape(CORES, slots, piece, -1), tail_zeros], axis=-1
        )
    ).reshape(rows_halo, a_cols)
    dnormed = dnormed + mm(da_low, w_a, NT)
    grad_input_gain = jnp.sum(
        dnormed.reshape(CORES, slots, piece + HALO, width) * (tokens * scale_in), axis=(0, 1, 2)
    )
    dnormed = own_sum(dnormed).reshape(slots, piece + HALO, width)
    rim_back = lax.ppermute(
        dnormed[:, HALO - KC + 1 : HALO].astype(BF16),
        AXES,
        [(i + 1, i) for i in range(devices - 1)],
    ).astype(F32)
    dnormed = dnormed[:, HALO:] + jnp.pad(rim_back, ((0, 0), (piece - KC + 1, 0), (0, 0)))
    own, own_scale = tokens[0][:, HALO:], scale_in[0][:, HALO:]
    input_grad = dresidual.reshape(slots, piece, width) + rms_back(
        own, own_scale, gain_in, dnormed
    )

    zero_half = jnp.zeros((m_cols,), F32)

    def conv_whole(value):
        none = jnp.zeros_like(value)
        first, second = place.by_core(value, none), place.by_core(none, value)
        return jnp.concatenate(
            [first[..., :m_cols], second[..., :m_cols], first[..., m_cols:], second[..., m_cols:]],
            axis=-1,
        )

    grad_mixer_gain = jnp.concatenate(
        [place.by_core(grad_mixer_gain, zero_half), place.by_core(zero_half, grad_mixer_gain)]
    )
    grad_taps = conv_whole(grad_taps).reshape(KC, devices, -1)
    vector_grads = jnp.concatenate(
        [
            grad_input_gain.reshape(devices, -1),
            grad_mixer_gain.reshape(devices, -1),
            grad_post_gain.reshape(devices, -1),
            conv_whole(grad_shift).reshape(devices, -1),
            jnp.transpose(grad_taps, (1, 0, 2)).reshape(devices, -1),
        ],
        axis=1,
    )
    vector_grads = jnp.pad(
        vector_grads, ((0, 0), (0, small_cols * shard_rows - vector_size))
    ).reshape(width, small_cols)
    grad_a = mm(normed, da_low, TN)
    grad_a = grad_a + jnp.pad(
        vector_grads,
        ((0, 0), (tail_at + small_at, a_cols - tail_at - small_at - small_cols)),
    )
    grad_a, grad_b = tie(grad_a, grad_b)
    grad_b = place.reduce_z([grad_b])[0]
    grad_a = place.reduce_first(by_columns(grad_a), True)
    head_sums = place.sum_along(head_sums, "b")
    grad_a, grad_b, head_sums = tie(grad_a, grad_b, head_sums)
    grad_a = place.reduce_second(grad_a, True)
    head_sums = place.sum_along(head_sums, "a")
    grad_a, head_sums = tie(grad_a, head_sums)
    (grad_a,) = place.reduce_z([grad_a])
    other_sums = place.swap(head_sums)
    head_sums = jnp.concatenate(
        [place.by_core(head_sums, other_sums), place.by_core(other_sums, head_sums)], axis=1
    )
    head_sums = lax.dynamic_slice_in_dim(head_sums, place.at["z"] * (SH // groups), SH // groups, 1)

    def between_cores(columns):
        columns = columns.reshape(CORES, shard_rows, -1)
        kept = lax.dynamic_index_in_dim(columns, core, 0, False)
        got = place.swap(lax.dynamic_index_in_dim(columns, 1 - core, 0, False))
        return place.by_core(kept, got), place.by_core(got, kept)

    part = far_grads.shape[0] // 5
    far_grads = [far_grads[k * part : (k + 1) * part] for k in range(5)]
    both = between_cores(jnp.concatenate([far_grads[0], far_grads[1], far_grads[4]], axis=1))
    grad_gate = jnp.concatenate([half[:, :ff_half] for half in both], axis=1).astype(F32)
    grad_up = jnp.concatenate([half[:, ff_half : 2 * ff_half] for half in both], axis=1)
    grad_up = grad_up.astype(F32)
    grad_down = far_grads[2].astype(F32)
    grad_outs = far_grads[3].astype(F32)
    grad_zgate = jnp.concatenate(
        [half[:, 2 * ff_half : 2 * ff_half + m_cols] for half in both], axis=1
    ).astype(F32)
    conv_first, conv_second = between_cores(grad_b)
    first, second = between_cores(grad_a)

    def both_halves(start, size):
        return jnp.concatenate([first[:, start : start + size], second[:, start : start + size]], 1)

    grad_attn_in = jnp.concatenate(
        [both_halves(0, q_cols), both_halves(q_cols, HD), both_halves(q_cols + HD, HD)], axis=1
    )
    grad_mixer_in = jnp.concatenate(
        [conv_first[:, :m_cols], conv_second[:, :m_cols], conv_first[:, m_cols:], conv_second[:, m_cols:]],
        axis=1,
    )
    grad_step = both_halves(lin_cols, M_SHARE)
    small_at = lin_cols + small_at
    small_sum = (first + second)[:, small_at : small_at + small_cols].reshape(-1)

    return (
        layer_out.reshape(slots, piece, width),
        input_grad,
        small_sum[: ends[0]],
        grad_attn_in,
        grad_outs[:out_rows],
        grad_zgate,
        grad_mixer_in,
        grad_step,
        small_sum[ends[3] : vector_size].reshape(KC, -1),
        small_sum[ends[2] : ends[3]],
        head_sums[0],
        head_sums[1],
        head_sums[2],
        small_sum[ends[0] : ends[1]],
        grad_outs[out_rows:],
        small_sum[ends[1] : ends[2]],
        grad_gate,
        grad_up,
        grad_down,
    )


def solution(mesh):
    rows, columns, vector = P(AXES, None), P(None, AXES), P(AXES)
    tokens, heads = P(None, AXES, None), P("sp")
    in_specs = (
        tokens,
        tokens,
        P(),
        vector,
        rows,
        rows,
        rows,
        rows,
        rows,
        columns,
        vector,
        heads,
        heads,
        heads,
        vector,
        rows,
        vector,
        rows,
        rows,
        rows,
    )
    out_specs = (
        tokens,
        tokens,
        vector,
        rows,
        rows,
        rows,
        rows,
        rows,
        columns,
        vector,
        heads,
        heads,
        heads,
        vector,
        rows,
        vector,
        rows,
        rows,
        rows,
    )
    return jax.shard_map(shards, mesh=mesh, in_specs=in_specs, out_specs=out_specs, check_vma=False)
```
